32 devices in a mesh: rep: 8 (over z, y), shard: 4 (over x, core).
Axes of the slice: x: 2, y: 2, z: 4, core: 2. Of those that a mesh axis runs over, the one named last changes fastest.
Arguments:
- frames: bfloat16 [16, 1024, 768], P('rep', 'shard'), may hold values from -6 to 6
- cotangent: bfloat16 [16, 1024, 768], P('rep', 'shard'), may hold values from -6 to 6
- first_gain: bfloat16 [2, 768], P(None, 'shard'), may hold values from 0.5 to 1.5
- first_shift: bfloat16 [2, 768], P(None, 'shard'), may hold values from -1.75 to 1.75
- query_weight: bfloat16 [2, 768, 768], P(None, 'shard'), may hold values from -0.21875 to 0.21875
- query_bias: bfloat16 [2, 768], P(None, 'shard'), may hold values from -3 to 3
- key_weight: bfloat16 [2, 768, 768], P(None, 'shard'), may hold values from -0.21875 to 0.21875
- value_weight: bfloat16 [2, 768, 768], P(None, 'shard'), may hold values from -0.21875 to 0.21875
- value_bias: bfloat16 [2, 768], P(None, 'shard'), may hold values from -3 to 3
- out_weight: bfloat16 [2, 768, 768], P(None, 'shard'), may hold values from -0.875 to 0.875
- out_bias: bfloat16 [2, 768], P(None, 'shard'), may hold values from -3 to 3
- second_gain: bfloat16 [2, 768], P(None, 'shard'), may hold values from 0.5 to 1.5
- second_shift: bfloat16 [2, 768], P(None, 'shard'), may hold values from -1.75 to 1.75
- up_weight: bfloat16 [2, 768, 3072], P(None, 'shard'), may hold values from -0.21875 to 0.21875
- up_bias: bfloat16 [2, 3072], P(None, 'shard'), may hold values from -3 to 3
- down_weight: bfloat16 [2, 3072, 768], P(None, 'shard'), may hold values from -0.109375 to 0.109375
- down_bias: bfloat16 [2, 768], P(None, 'shard'), may hold values from -1.75 to 1.75
Outputs:
- output: bfloat16 [16, 1024, 768], P('rep', 'shard')
- input_grad: float32 [16, 1024, 768], P('rep', 'shard')
- first_gain_grad: float32 [2, 768], P(None, 'shard')
- first_shift_grad: float32 [2, 768], P(None, 'shard')
- query_weight_grad: float32 [2, 768, 768], P(None, 'shard')
- query_bias_grad: float32 [2, 768], P(None, 'shard')
- key_weight_grad: float32 [2, 768, 768], P(None, 'shard')
- value_weight_grad: float32 [2, 768, 768], P(None, 'shard')
- value_bias_grad: float32 [2, 768], P(None, 'shard')
- out_weight_grad: float32 [2, 768, 768], P(None, 'shard')
- out_bias_grad: float32 [2, 768], P(None, 'shard')
- second_gain_grad: float32 [2, 768], P(None, 'shard')
- second_shift_grad: float32 [2, 768], P(None, 'shard')
- up_weight_grad: float32 [2, 768, 3072], P(None, 'shard')
- up_bias_grad: float32 [2, 3072], P(None, 'shard')
- down_weight_grad: float32 [2, 3072, 768], P(None, 'shard')
- down_bias_grad: float32 [2, 768], P(None, 'shard')
The draws below stay inside these ranges and needn't reach their ends.
All inputs are finite; a program needn't handle non-finite values.
Results may differ from the reference program's by a relative error of at most 0.02.
Values may be sent and summed in bfloat16 or wider, within the bound.
No kernel may reach another device: no remote copies, remote signals or barrier semaphores. Data moves between devices by JAX's collectives and lax.ppermute only.
A program may use at most 320 MiB of HBM per device.

```python
import jax
import jax.numpy as jnp
from jax import lax

D = 768
HEADS = 12
HEAD = 64
FF = 3072
FRAMES = 1024
LAYERS = 2
CLIPS = 2
CLIPS_ALL = 16
N_REP = 8


def shard_levels(rng, shape, cuts, least, high):
    factor_of, own = 1.0, jax.random.fold_in(rng, 6)
    for position, shards_of in cuts:
        steps = jnp.exp(jax.random.uniform(jax.random.fold_in(own, position), (shards_of,), jnp.float32, least / len(cuts), high / len(cuts)))
        factor_of = factor_of * jnp.repeat(steps, shape[position] // shards_of).reshape([-1 if axis == position else 1 for axis in range(len(shape))])
    return factor_of


def noise(rng, dims, scale, reach, split=(), dtype=jnp.bfloat16):
    loudness = shard_levels(rng, dims, split, -0.22, 0.18) if split else 1.0
    entries = jax.random.normal(rng, dims, jnp.float32) * scale * loudness
    return jnp.minimum(jnp.maximum(entries, -reach), reach).astype(dtype)


def setup_inputs(seed: int = 0) -> dict:
    arg_keys = jax.random.split(jax.random.key(seed), 18)
    frames = noise(arg_keys[0], (CLIPS_ALL, FRAMES, D), 1.0, 6.0, ((0, 8), (1, 4)))
    cotangent = noise(arg_keys[1], (CLIPS_ALL, FRAMES, D), 1.0, 6.0, ((0, 8), (1, 4)))
    first_gain = jnp.clip(1.0 + 0.1 * jax.random.normal(arg_keys[2], (LAYERS, D), jnp.float32), 0.5, 1.5).astype(jnp.bfloat16)
    first_shift = noise(arg_keys[3], (LAYERS, D), 0.3, 1.75, ((1, 4),))
    query_weight = noise(arg_keys[4], (LAYERS, D, D), D ** -0.5, 0.21875, ((1, 4),))
    query_bias = noise(arg_keys[5], (LAYERS, D), 0.5, 3.0, ((1, 4),))
    key_weight = noise(arg_keys[6], (LAYERS, D, D), D ** -0.5, 0.21875, ((1, 4),))
    value_weight = noise(arg_keys[7], (LAYERS, D, D), D ** -0.5, 0.21875, ((1, 4),))
    value_bias = noise(arg_keys[8], (LAYERS, D), 0.5, 3.0, ((1, 4),))
    out_weight = noise(arg_keys[9], (LAYERS, D, D), (D // 16) ** -0.5, 0.875, ((1, 4),))
    out_bias = noise(arg_keys[10], (LAYERS, D), 0.5, 3.0, ((1, 4),))
    second_gain = jnp.clip(1.0 + 0.1 * jax.random.normal(arg_keys[11], (LAYERS, D), jnp.float32), 0.5, 1.5).astype(jnp.bfloat16)
    second_shift = noise(arg_keys[12], (LAYERS, D), 0.3, 1.75, ((1, 4),))
    up_weight = noise(arg_keys[13], (LAYERS, D, FF), D ** -0.5, 0.21875, ((1, 4),))
    up_bias = noise(arg_keys[14], (LAYERS, FF), 0.5, 3.0, ((1, 4),))
    down_weight = noise(arg_keys[15], (LAYERS, FF, D), FF ** -0.5, 0.109375, ((1, 4),))
    down_bias = noise(arg_keys[16], (LAYERS, D), 0.3, 1.75, ((1, 4),))
    return {"frames": frames, "cotangent": cotangent, "first_gain": first_gain, "first_shift": first_shift, "query_weight": query_weight, "query_bias": query_bias, "key_weight": key_weight, "value_weight": value_weight, "value_bias": value_bias, "out_weight": out_weight, "out_bias": out_bias, "second_gain": second_gain, "second_shift": second_shift, "up_weight": up_weight, "up_bias": up_bias, "down_weight": down_weight, "down_bias": down_bias}


@jax.custom_vjp
def low(v):
    return lax.optimization_barrier(v.astype(jnp.bfloat16)).astype(jnp.float32)

@jax.custom_vjp
def low_back(v):
    return v

def low_keep(v):
    return (low(v), None)

def low_pass(kept, grad):
    return (grad,)

def back_keep(v):
    return (v, None)

def back_low(kept, grad):
    return (low(grad),)
low.defvjp(low_keep, low_pass)
low_back.defvjp(back_keep, back_low)
EPSILON = 1e-05

def matmul(left, right):
    return jnp.einsum('cfd,de->cfe', left, right, precision=lax.Precision.HIGHEST)

def layer_norm(values, norm_gain, norm_shift):
    average = lax.optimization_barrier(jnp.mean(values, axis=-1, keepdims=True))
    centered = values - average
    variance = lax.optimization_barrier(jnp.mean(centered * centered, axis=-1, keepdims=True))
    return centered * lax.rsqrt(variance + EPSILON) * norm_gain + norm_shift

def one_layer(stream, weights):
    first_gain, first_shift, query_weight, query_bias, key_weight, value_weight, value_bias, out_weight, out_bias, second_gain, second_shift, up_weight, up_bias, down_weight, down_bias = weights
    clip_count, frame_count, model_width = stream.shape
    normed = low(layer_norm(stream, first_gain, first_shift))
    queries = low(low_back(matmul(normed, query_weight) + query_bias)).reshape(clip_count, frame_count, HEADS, HEAD)
    keys = low(low_back(matmul(normed, key_weight))).reshape(clip_count, frame_count, HEADS, HEAD)
    values = low(low_back(matmul(normed, value_weight) + value_bias)).reshape(clip_count, frame_count, HEADS, HEAD)
    scores = low_back(HEAD ** (-0.5) * jnp.einsum('cqhe,ckhe->chqk', queries, keys, precision=lax.Precision.HIGHEST))
    probability = low(jax.nn.softmax(scores, axis=-1))
    mixed = jnp.einsum('chqk,ckhe->cqhe', probability, values, precision=lax.Precision.HIGHEST)
    mixed = low(low_back(mixed.reshape(clip_count, frame_count, model_width)))
    attended = stream + low_back(matmul(mixed, out_weight) + out_bias)
    second = low(layer_norm(attended, second_gain, second_shift))
    hidden = low_back(matmul(second, up_weight) + up_bias)
    activated = low(jax.nn.gelu(hidden, approximate=False))
    return attended + low_back(matmul(activated, down_weight) + down_bias)

def forward(stream, params):
    for layer_index in range(LAYERS):
        stream = one_layer(stream, tuple((entry[layer_index] for entry in params)))
    return stream

def reference(frames, cotangent, first_gain, first_shift, query_weight, query_bias, key_weight, value_weight, value_bias, out_weight, out_bias, second_gain, second_shift, up_weight, up_bias, down_weight, down_bias):
    params = tuple((entry.astype(jnp.float32) for entry in (first_gain, first_shift, query_weight, query_bias, key_weight, value_weight, value_bias, out_weight, out_bias, second_gain, second_shift, up_weight, up_bias, down_weight, down_bias)))
    inputs = frames.astype(jnp.float32).reshape(N_REP, CLIPS, FRAMES, D)
    cotangents = cotangent.astype(jnp.float32).reshape(N_REP, CLIPS, FRAMES, D)

    def step(totals, clip_pair):
        clip_in, clip_cot = clip_pair
        clip_out, pullback = jax.vjp(forward, clip_in, params)
        grad_in, grad_params = pullback(clip_cot)
        summed = tuple((left + right for left, right in zip(totals, grad_params)))
        return (summed, (clip_out.astype(jnp.bfloat16), grad_in))
    zero_grads = tuple((jnp.zeros_like(entry) for entry in params))
    totals, (outputs, grads_in) = lax.scan(step, zero_grads, (inputs, cotangents))
    return (outputs.reshape(CLIPS_ALL, FRAMES, D), grads_in.reshape(CLIPS_ALL, FRAMES, D), totals[0], totals[1], totals[2], totals[3], totals[4], totals[5], totals[6], totals[7], totals[8], totals[9], totals[10], totals[11], totals[12], totals[13], totals[14])
```

```python
import functools

import jax
import jax.numpy as jnp
from jax import lax
from jax.experimental import pallas as pl
from jax.experimental.pallas import tpu as pltpu
from jax.sharding import Mesh
from jax.sharding import PartitionSpec as P

HEAD = 64
LAYERS = 2
SHARDS = 4
EPSILON = 1e-05
SWAP = [(0, 1), (1, 0)]
F32 = jnp.float32
BF16 = jnp.bfloat16
NN = (((1,), (0,)), ((), ()))
NT = (((1,), (1,)), ((), ()))
TN = (((0,), (0,)), ((), ()))
VMEM_LIMIT = 56 * 1024 * 1024

ATTENTION, UP, DOWN = slice(0, 4), slice(4, 8), slice(8, 12)


def dot(left, right, dims=NN):
    return lax.dot_general(left, right, dims, preferred_element_type=F32)


def swap(values, axis):
    return lax.ppermute(values, axis, SWAP)


def vmem_spec():
    return pl.BlockSpec(memory_space=pltpu.VMEM)


def any_spec():
    return pl.BlockSpec(memory_space=pl.ANY)


def smem_spec():
    return pl.BlockSpec(memory_space=pltpu.SMEM)


def cost(flops, bytes_accessed, transcendentals=0):
    return pl.CostEstimate(
        flops=int(flops), bytes_accessed=int(bytes_accessed), transcendentals=int(transcendentals)
    )


def shaped(shape, dtype):
    return jax.ShapeDtypeStruct(shape, dtype)


def standardize(values):
    average = jnp.mean(values, axis=-1, keepdims=True)
    centered = values - average
    variance = jnp.mean(centered * centered, axis=-1, keepdims=True)
    inverse_scale = lax.rsqrt(variance + EPSILON)
    return centered * inverse_scale, inverse_scale


def norm_input_grad(grad_out, standard, inverse_scale, gain):
    grad_standard = grad_out * gain
    return inverse_scale * (
        grad_standard
        - jnp.mean(grad_standard, axis=-1, keepdims=True)
        - standard * jnp.mean(grad_standard * standard, axis=-1, keepdims=True)
    )


def column_sum(values):
    return jnp.sum(values.astype(F32), axis=0, keepdims=True)


def gelu_parts(hidden):
    density = jnp.exp(-0.5 * hidden * hidden)
    t = 1.0 / (1.0 + (0.3275911 * 0.7071067811865476) * jnp.abs(hidden))
    series = t * (
        0.127414796
        + t * (-0.142248368 + t * (0.7107068705 + t * (-0.7265760135 + t * 0.5307027145)))
    )
    tail = series * density
    phi = jnp.where(hidden >= 0.0, 1.0 - tail, tail)
    return hidden * phi, phi + (hidden * 0.3989422804014327) * density


def share_places(place_ref):
    s, y = place_ref[0], place_ref[1]
    return ((s, None), (s ^ 1, None), (s ^ 2, y), (s ^ 2, 1 - y), (s ^ 3, y), (s ^ 3, 1 - y))


def load_rows(shares, place_ref, blocks, target, sems, rows):
    copies = []
    for index, (share, (shard, half)) in enumerate(zip(shares, share_places(place_ref))):
        start, size = shard * rows, rows
        if half is not None:
            size = rows // 2
            start = start + half * size
        copies.append(
            pltpu.make_async_copy(
                share.at[blocks], target.at[:, pl.ds(pl.multiple_of(start, size), size), :], sems.at[index]
            )
        )
    return copies


def load_blocks(shares, place_ref, blocks, target, sems, rows):
    count = blocks.stop - blocks.start
    copies = []
    for index, (share, (shard, half)) in enumerate(zip(shares, share_places(place_ref))):
        at = pl.ds(shard * count, count)
        place = target.at[at]
        if half is not None:
            size = rows // 2
            place = target.at[at, pl.ds(pl.multiple_of(half * size, size), size)]
        copies.append(pltpu.make_async_copy(share.at[blocks], place, sems.at[index]))
    return copies


def start_all(copies):
    for copy in copies:
        copy.start()


def wait_all(copies):
    for copy in copies:
        copy.wait()


def qkv_kernel(place_ref, stream_ref, vectors_ref, *refs):
    shares, (queries_ref, keys_ref, values_ref, weights, sems) = refs[:6], refs[6:]
    copies = load_rows(shares, place_ref, slice(0, 3), weights, sems, weights.shape[1] // SHARDS)
    start_all(copies)
    standard, _ = standardize(stream_ref[...])
    normed = (standard * vectors_ref[0:1] + vectors_ref[1:2]).astype(BF16)
    wait_all(copies)
    queries = (dot(normed, weights[0]) + vectors_ref[2:3]).astype(BF16)
    queries_ref[...] = queries * jnp.asarray(HEAD ** (-0.5), BF16)
    keys_ref[...] = dot(normed, weights[1]).astype(BF16)
    values_ref[...] = (dot(normed, weights[2]) + vectors_ref[3:4]).astype(BF16)


def project_qkv(place, stream, vectors, shares):
    rows, width = stream.shape
    out = shaped((rows, width), BF16)
    return pl.pallas_call(
        qkv_kernel,
        out_shape=(out, out, out),
        in_specs=[smem_spec(), vmem_spec(), vmem_spec()] + [any_spec()] * 6,
        out_specs=(vmem_spec(),) * 3,
        scratch_shapes=[pltpu.VMEM((3, width, width), BF16), pltpu.SemaphoreType.DMA((6,))],
        compiler_params=pltpu.CompilerParams(vmem_limit_bytes=VMEM_LIMIT),
        cost_estimate=cost(6 * rows * width * width, 10 * rows * width + 6 * width * width),
        name="project_qkv",
    )(place, stream, vectors, *shares)


def attention_kernel(q_ref, ko_ref, kt_ref, vo_ref, vt_ref, mixed_ref, lse_ref):
    queries_t = q_ref[...].T
    row = lax.broadcasted_iota(jnp.int32, queries_t.shape, 0)
    values_t = (vo_ref[...].T, vt_ref[...].T)
    outs = []
    for head in range(2):
        mine = (row >= head * HEAD) & (row < (head + 1) * HEAD)
        q_t = jnp.where(mine, queries_t, jnp.zeros_like(queries_t))
        scores = (dot(ko_ref[...], q_t), dot(kt_ref[...], q_t))
        peak = jnp.maximum(
            jnp.max(scores[0], axis=0, keepdims=True), jnp.max(scores[1], axis=0, keepdims=True)
        )
        weights = tuple(jnp.exp(part - peak) for part in scores)
        total = jnp.sum(weights[0], axis=0, keepdims=True) + jnp.sum(weights[1], axis=0, keepdims=True)
        lse_ref[0, head : head + 1, :] = peak + jnp.log(total)
        at = slice(head * HEAD, (head + 1) * HEAD)
        out = dot(values_t[0][at], weights[0].astype(BF16)) + dot(values_t[1][at], weights[1].astype(BF16))
        outs.append(out / total)
    mixed_ref[...] = jnp.concatenate(outs, axis=0).T.astype(BF16)


def attend(queries, keys, keys_twin, values, values_twin):
    rows, width = queries.shape
    pairs = width // (2 * HEAD)
    block = pl.BlockSpec((rows, 2 * HEAD), lambda pair: (0, pair))
    return pl.pallas_call(
        attention_kernel,
        grid=(pairs,),
        out_shape=(shaped((rows, width), BF16), shaped((pairs, 8, rows), F32)),
        in_specs=[block] * 5,
        out_specs=(block, pl.BlockSpec((1, 8, rows), lambda pair: (pair, 0, 0))),
        compiler_params=pltpu.CompilerParams(vmem_limit_bytes=VMEM_LIMIT),
        cost_estimate=cost(32 * rows * rows * width, 12 * rows * width, 4 * pairs * rows * rows),
        name="attend",
    )(queries, keys, keys_twin, values, values_twin)


def feed_kernel(place_ref, stream_ref, mixed_ref, vectors_ref, up_bias_ref, *refs):
    shares, refs = refs[:6], refs[6:]
    attended_ref, activated_ref, slope_ref, next_ref, out_w, up_w, down_w, sems = refs
    width = stream_ref.shape[1]
    share = width // SHARDS
    out_copies = load_rows(shares, place_ref, slice(3, 4), out_w, sems.at[0], share)
    up_copies = load_rows(shares, place_ref, UP, up_w, sems.at[1], share)
    down_copies = load_blocks(shares, place_ref, DOWN, down_w, sems.at[2], share)
    start_all(out_copies)
    start_all(up_copies)
    start_all(down_copies)
    wait_all(out_copies)
    attended_ref[...] = stream_ref[...] + dot(mixed_ref[...], out_w[0]) + vectors_ref[4:5]
    standard, _ = standardize(attended_ref[...])
    second = (standard * vectors_ref[5:6] + vectors_ref[6:7]).astype(BF16)
    wait_all(up_copies)
    wait_all(down_copies)
    next_ref[...] = attended_ref[...] + vectors_ref[7:8]
    for block in range(SHARDS):
        at = slice(block * width, (block + 1) * width)
        hidden = dot(second, up_w[block]) + up_bias_ref[:, at]
        activated, slope = gelu_parts(hidden)
        activated = activated.astype(BF16)
        activated_ref[:, at] = activated
        slope_ref[:, at] = slope.astype(BF16)
        down = down_w[block * SHARDS : (block + 1) * SHARDS].reshape(width, width)
        next_ref[...] += dot(activated, down)


def feed_forward(place, stream, mixed, vectors, up_bias, shares):
    rows, width = stream.shape
    wide = SHARDS * width
    share = width // SHARDS
    return pl.pallas_call(
        feed_kernel,
        out_shape=(
            shaped((rows, width), F32),
            shaped((rows, wide), BF16),
            shaped((rows, wide), BF16),
            shaped((rows, width), F32),
        ),
        in_specs=[smem_spec()] + [vmem_spec()] * 4 + [any_spec()] * 6,
        out_specs=(vmem_spec(),) * 4,
        scratch_shapes=[
            pltpu.VMEM((1, width, width), BF16),
            pltpu.VMEM((4, width, width), BF16),
            pltpu.VMEM((4 * SHARDS, share, width), BF16),
            pltpu.SemaphoreType.DMA((3, 6)),
        ],
        compiler_params=pltpu.CompilerParams(vmem_limit_bytes=VMEM_LIMIT),
        cost_estimate=cost(18 * rows * width * width, 32 * rows * width + 18 * width * width, rows * wide),
        name="feed_forward",
    )(place, stream, mixed, vectors, up_bias, *shares)


def feed_back_kernel(place_ref, grad_ref, slope_ref, attended_ref, vectors_ref, *refs):
    shares, refs = refs[:6], refs[6:]
    hidden_ref, attended_grad_ref, mixed_grad_ref, sums_ref, up_sums_ref, out_w, up_w, down_w, sems = refs
    width = grad_ref.shape[1]
    share = width // SHARDS
    down_copies = load_blocks(shares, place_ref, DOWN, down_w, sems.at[2], share)
    up_copies = load_rows(shares, place_ref, UP, up_w, sems.at[1], share)
    out_copies = load_rows(shares, place_ref, slice(3, 4), out_w, sems.at[0], share)
    start_all(down_copies)
    start_all(up_copies)
    start_all(out_copies)
    branch = grad_ref[...].astype(BF16)
    sums_ref[...] = jnp.zeros_like(sums_ref)
    sums_ref[7:8] = column_sum(branch)
    wait_all(down_copies)
    wait_all(up_copies)
    second_grad = None
    for block in range(SHARDS):
        at = slice(block * width, (block + 1) * width)
        down = down_w[block * SHARDS : (block + 1) * SHARDS].reshape(width, width)
        hidden_grad = (dot(branch, down, NT) * slope_ref[:, at].astype(F32)).astype(BF16)
        hidden_ref[:, at] = hidden_grad
        up_sums_ref[:, at] = column_sum(hidden_grad)
        part = dot(hidden_grad, up_w[block], NT)
        second_grad = part if second_grad is None else second_grad + part
    standard, inverse = standardize(attended_ref[...])
    sums_ref[5:6] = column_sum(second_grad * standard)
    sums_ref[6:7] = column_sum(second_grad)
    attended_grad = grad_ref[...] + norm_input_grad(second_grad, standard, inverse, vectors_ref[5:6])
    attended_grad_ref[...] = attended_grad
    out_grad = attended_grad.astype(BF16)
    sums_ref[4:5] = column_sum(out_grad)
    wait_all(out_copies)
    mixed_grad_ref[...] = dot(out_grad, out_w[0], NT).astype(BF16)


def feed_back(place, grad, slope, attended, vectors, shares):
    rows, width = grad.shape
    wide = SHARDS * width
    share = width // SHARDS
    return pl.pallas_call(
        feed_back_kernel,
        out_shape=(
            shaped((rows, wide), BF16),
            shaped((rows, width), F32),
            shaped((rows, width), BF16),
            shaped((8, width), F32),
            shaped((1, wide), F32),
        ),
        in_specs=[smem_spec()] + [vmem_spec()] * 4 + [any_spec()] * 6,
        out_specs=(vmem_spec(),) * 5,
        scratch_shapes=[
            pltpu.VMEM((1, width, width), BF16),
            pltpu.VMEM((4, width, width), BF16),
            pltpu.VMEM((4 * SHARDS, share, width), BF16),
            pltpu.SemaphoreType.DMA((3, 6)),
        ],
        compiler_params=pltpu.CompilerParams(vmem_limit_bytes=VMEM_LIMIT),
        cost_estimate=cost(18 * rows * width * width, 30 * rows * width + 18 * width * width),
        name="feed_back",
    )(place, grad, slope, attended, vectors, *shares)


def store_rows(place_ref, work, keep_ref, send_ref, block, sems, rows):
    s = place_ref[0]
    copies = []
    for index, (shard, target) in enumerate(
        ((s, keep_ref.at[0, block]), (s ^ 2, keep_ref.at[1, block]), (s ^ 1, send_ref.at[0, block]), (s ^ 3, send_ref.at[1, block]))
    ):
        source = work.at[pl.ds(pl.multiple_of(shard * rows, rows), rows), :]
        copies.append(pltpu.make_async_copy(source, target, sems.at[index]))
    return copies


def down_grad_kernel(place_ref, activated_ref, grad_ref, out_ref):
    del place_ref
    rows, width = grad_ref.shape
    result = dot(activated_ref[...], grad_ref[...].astype(BF16), TN).astype(BF16)
    out_ref[...] = result.reshape(out_ref.shape)


def down_weight_grad(place, activated, grad):
    rows, width = grad.shape
    share = width // SHARDS

    def shard_of(step, place_ref):
        return place_ref[0] ^ (step // 2 + 2 * (step % 2))

    return pl.pallas_call(
        down_grad_kernel,
        out_shape=shaped((SHARDS, SHARDS, share, width), BF16),
        grid_spec=pltpu.PrefetchScalarGridSpec(
            num_scalar_prefetch=1,
            grid=(SHARDS,),
            in_specs=[
                pl.BlockSpec((rows, width), lambda step, place_ref: (0, shard_of(step, place_ref))),
                pl.BlockSpec((rows, width), lambda step, place_ref: (0, 0)),
            ],
            out_specs=pl.BlockSpec((1, SHARDS, share, width), lambda step, place_ref: (step, 0, 0, 0)),
        ),
        compiler_params=pltpu.CompilerParams(vmem_limit_bytes=VMEM_LIMIT),
        cost_estimate=cost(8 * rows * width * width, 12 * rows * width + 8 * width * width),
        name="down_weight_grad",
    )(place, activated, grad)


def weight_grad_steps(place_ref, keep_ref, send_ref, work, sems, makers):
    pending = [None, None]
    for block, make in enumerate(makers):
        slot = block % 2
        if pending[slot] is not None:
            wait_all(pending[slot])
        work[slot] = make().astype(BF16)
        copies = store_rows(
            place_ref, work.at[slot], keep_ref, send_ref, block, sems.at[slot], work.shape[1] // SHARDS
        )
        start_all(copies)
        pending[slot] = copies
    for copies in pending:
        if copies is not None:
            wait_all(copies)


def feed_weight_grad_kernel(
    place_ref, hidden_ref, attended_ref, attended_grad_ref, mixed_ref, vectors_ref, keep_ref, send_ref, work, sems
):
    width = attended_ref.shape[1]
    standard, _ = standardize(attended_ref[...])
    second = (standard * vectors_ref[5:6] + vectors_ref[6:7]).astype(BF16)
    second_t = second.T

    def up_block(block):
        return lambda: dot(second_t, hidden_ref[:, block * width : (block + 1) * width])

    def out_block():
        return dot(mixed_ref[...], attended_grad_ref[...].astype(BF16), TN)

    makers = [out_block] + [up_block(block) for block in range(SHARDS)]
    weight_grad_steps(place_ref, keep_ref, send_ref, work, sems, makers)


def grad_shapes(count, width):
    share = width // SHARDS
    return (shaped((2, count, share, width), BF16),) * 2


def grad_scratch(width):
    return [pltpu.VMEM((2, width, width), BF16), pltpu.SemaphoreType.DMA((2, 4))]


def feed_weight_grads(place, hidden_grad, attended, attended_grad, mixed, vectors):
    rows, width = attended.shape
    return pl.pallas_call(
        feed_weight_grad_kernel,
        out_shape=grad_shapes(5, width),
        in_specs=[smem_spec()] + [vmem_spec()] * 5,
        out_specs=(any_spec(),) * 2,
        scratch_shapes=grad_scratch(width),
        compiler_params=pltpu.CompilerParams(vmem_limit_bytes=VMEM_LIMIT),
        cost_estimate=cost(10 * rows * width * width, 20 * rows * width + 10 * width * width),
        name="feed_weight_grads",
    )(place, hidden_grad, attended, attended_grad, mixed, vectors)


def qkv_weight_grad_kernel(
    place_ref, stream_ref, vectors_ref, dq_ref, dkv_ref, sums_ref, keep_ref, send_ref, work, sems
):
    standard, _ = standardize(stream_ref[...])
    normed_t = (standard * vectors_ref[0:1] + vectors_ref[1:2]).astype(BF16).T
    sums_ref[...] = jnp.zeros_like(sums_ref)
    sums_ref[2:3] = column_sum(dq_ref[...])
    sums_ref[3:4] = column_sum(dkv_ref[1])
    makers = [
        lambda: dot(normed_t, dq_ref[...]),
        lambda: dot(normed_t, dkv_ref[0]),
        lambda: dot(normed_t, dkv_ref[1]),
    ]
    weight_grad_steps(place_ref, keep_ref, send_ref, work, sems, makers)


def qkv_weight_grads(place, stream, vectors, dq, dkv):
    rows, width = stream.shape
    return pl.pallas_call(
        qkv_weight_grad_kernel,
        out_shape=(shaped((8, width), F32),) + grad_shapes(3, width),
        in_specs=[smem_spec()] + [vmem_spec()] * 4,
        out_specs=(vmem_spec(), any_spec(), any_spec()),
        scratch_shapes=grad_scratch(width),
        compiler_params=pltpu.CompilerParams(vmem_limit_bytes=VMEM_LIMIT),
        cost_estimate=cost(6 * rows * width * width, 10 * rows * width + 6 * width * width),
        name="qkv_weight_grads",
    )(place, stream, vectors, dq, dkv)


def attention_back_kernel(
    q_ref, ko_ref, kt_ref, vo_ref, vt_ref, lse_ref, out_grad_ref, dq_ref, keep_ref, send_ref
):
    queries = q_ref[...]
    out_grad = out_grad_ref[...]
    queries_t, out_grad_t = queries.T, out_grad.T
    row = lax.broadcasted_iota(jnp.int32, queries_t.shape, 0)
    lane = lax.broadcasted_iota(jnp.int32, queries.shape, 1)
    keys, values = (ko_ref, kt_ref), (vo_ref, vt_ref)
    keys_t = tuple(part[...].T for part in keys)
    key_grads, value_grads, query_grads = [None, None], [None, None], []
    for head in range(2):
        low, high = head * HEAD, (head + 1) * HEAD
        mine_t = (row >= low) & (row < high)
        mine = (lane >= low) & (lane < high)
        q_t = jnp.where(mine_t, queries_t, jnp.zeros_like(queries_t))
        o_t = jnp.where(mine_t, out_grad_t, jnp.zeros_like(queries_t))
        q_h = jnp.where(mine, queries, jnp.zeros_like(queries))
        o_h = jnp.where(mine, out_grad, jnp.zeros_like(queries))
        lse = lse_ref[0, head : head + 1, :]
        probability = [jnp.exp(dot(part[...], q_t) - lse) for part in keys]
        probability_grad = [dot(part[...], o_t) for part in values]
        inner = sum(
            jnp.sum(left * right, axis=0, keepdims=True)
            for left, right in zip(probability, probability_grad)
        )
        query_grad = None
        for index in range(2):
            score_grad = (probability[index] * (probability_grad[index] - inner)).astype(BF16)
            value_part = dot(probability[index].astype(BF16), o_h)
            key_part = dot(score_grad, q_h)
            query_part = dot(keys_t[index][low:high], score_grad)
            if head == 0:
                key_grads[index], value_grads[index] = key_part, value_part
            else:
                key_grads[index] += key_part
                value_grads[index] += value_part
            query_grad = query_part if index == 0 else query_grad + query_part
        query_grads.append(query_grad)
    dq_ref[...] = (jnp.concatenate(query_grads, axis=0).T * HEAD ** (-0.5)).astype(BF16)
    keep_ref[0] = key_grads[0].astype(BF16)
    keep_ref[1] = value_grads[0].astype(BF16)
    send_ref[0] = key_grads[1].astype(BF16)
    send_ref[1] = value_grads[1].astype(BF16)


def attend_back(queries, keys, keys_twin, values, values_twin, lse, out_grad):
    rows, width = queries.shape
    pairs = width // (2 * HEAD)
    block = pl.BlockSpec((rows, 2 * HEAD), lambda pair: (0, pair))
    pair_block = pl.BlockSpec((2, rows, 2 * HEAD), lambda pair: (0, 0, pair))
    return pl.pallas_call(
        attention_back_kernel,
        grid=(pairs,),
        out_shape=(
            shaped((rows, width), BF16),
            shaped((2, rows, width), BF16),
            shaped((2, rows, width), BF16),
        ),
        in_specs=[block] * 5 + [pl.BlockSpec((1, 8, rows), lambda pair: (pair, 0, 0)), block],
        out_specs=(block, pair_block, pair_block),
        compiler_params=pltpu.CompilerParams(vmem_limit_bytes=VMEM_LIMIT),
        cost_estimate=cost(80 * rows * rows * width, 24 * rows * width, 4 * pairs * rows * rows),
        name="attend_back",
    )(queries, keys, keys_twin, values, values_twin, lse, out_grad)


def norm_back_kernel(place_ref, stream_ref, vectors_ref, attended_grad_ref, dq_ref, dkv_ref, *refs):
    shares, (grad_ref, sums_ref, weights, sems) = refs[:6], refs[6:]
    copies = load_rows(shares, place_ref, slice(0, 3), weights, sems, weights.shape[1] // SHARDS)
    start_all(copies)
    standard, inverse = standardize(stream_ref[...])
    wait_all(copies)
    normed_grad = (
        dot(dq_ref[...], weights[0], NT) + dot(dkv_ref[0], weights[1], NT) + dot(dkv_ref[1], weights[2], NT)
    )
    sums_ref[...] = jnp.zeros_like(sums_ref)
    sums_ref[0:1] = column_sum(normed_grad * standard)
    sums_ref[1:2] = column_sum(normed_grad)
    grad_ref[...] = attended_grad_ref[...] + norm_input_grad(
        normed_grad, standard, inverse, vectors_ref[0:1]
    )


def norm_back(place, stream, vectors, attended_grad, dq, dkv, shares):
    rows, width = stream.shape
    return pl.pallas_call(
        norm_back_kernel,
        out_shape=(shaped((rows, width), F32), shaped((8, width), F32)),
        in_specs=[smem_spec()] + [vmem_spec()] * 5 + [any_spec()] * 6,
        out_specs=(vmem_spec(),) * 2,
        scratch_shapes=[pltpu.VMEM((3, width, width), BF16), pltpu.SemaphoreType.DMA((6,))],
        compiler_params=pltpu.CompilerParams(vmem_limit_bytes=VMEM_LIMIT),
        cost_estimate=cost(6 * rows * width * width, 18 * rows * width + 6 * width * width),
        name="norm_back",
    )(place, stream, vectors, attended_grad, dq, dkv, *shares)


def half_of(values, half):
    size = values.shape[-2] // 2
    return lax.dynamic_slice_in_dim(values, half * size, size, axis=values.ndim - 2)


def gather_shares(own, y):
    twin = swap(own, "core")
    near = swap(half_of(own, y), "x")
    far = swap(near, "y")
    return (own, twin, near, far, swap(near, "core"), swap(far, "core"))


def add(left, right):
    return (left.astype(F32) + right.astype(F32)).astype(BF16)


def reduce_grads(keep, send, y):
    back = swap(send, "core")
    other = add(keep[1], back[1])
    mine = add(keep[0], back[0])
    share = add(mine, swap(other, "x"))
    part = add(half_of(share, y), swap(half_of(share, 1 - y), "y"))
    part = lax.psum(part, "z")
    rest = swap(part, "y")
    ordered = jnp.where(
        y == 0, jnp.concatenate([part, rest], axis=-2), jnp.concatenate([rest, part], axis=-2)
    )
    return ordered.astype(F32)


def body(
    frames,
    cotangent,
    first_gain,
    first_shift,
    query_weight,
    query_bias,
    key_weight,
    value_weight,
    value_bias,
    out_weight,
    out_bias,
    second_gain,
    second_shift,
    up_weight,
    up_bias,
    down_weight,
    down_bias,
):
    x, y, core = lax.axis_index("x"), lax.axis_index("y"), lax.axis_index("core")
    shard = 2 * x + core
    place = jnp.stack([shard, y]).astype(jnp.int32)
    quarter, width = frames.shape[1:]
    share = width // SHARDS

    def to_clip(values):
        mine = lax.dynamic_index_in_dim(values, x, 0, keepdims=False)
        other = lax.dynamic_index_in_dim(values, 1 - x, 0, keepdims=False)
        return jnp.concatenate([mine, swap(other, "x")], axis=0).astype(F32)

    def from_clip(values):
        mine, other = values[:quarter], swap(values[quarter:], "x")
        return jnp.where(x == 0, jnp.stack([mine, other]), jnp.stack([other, mine]))

    small = jnp.stack(
        [first_gain, first_shift, query_bias, value_bias, out_bias, second_gain, second_shift, down_bias], axis=1
    )
    small = jnp.concatenate([small, up_bias.reshape(LAYERS, SHARDS, share)], axis=1)
    small = lax.all_gather(small, ("x", "core"), axis=0).astype(F32)
    vectors = jnp.transpose(small[:, :, :8], (1, 2, 0, 3)).reshape(LAYERS, 8, width)
    up_biases = jnp.transpose(small[:, :, 8:], (1, 0, 2, 3)).reshape(LAYERS, 1, SHARDS * width)

    stream = to_clip(frames)
    saved = []
    for layer in range(LAYERS):
        pack = jnp.concatenate(
            [
                jnp.stack([query_weight[layer], key_weight[layer], value_weight[layer], out_weight[layer]]),
                jnp.transpose(up_weight[layer].reshape(share, SHARDS, width), (1, 0, 2)),
                down_weight[layer].reshape(SHARDS, share, width),
            ],
            axis=0,
        )
        shares = gather_shares(pack, y)
        queries, keys, values = project_qkv(place, stream, vectors[layer], shares)
        keys_twin, values_twin = swap(keys, "core"), swap(values, "core")
        mixed, lse = attend(queries, keys, keys_twin, values, values_twin)
        attended, activated, slope, following = feed_forward(
            place, stream, mixed, vectors[layer], up_biases[layer], shares
        )
        saved.append(
            (shares, stream, queries, keys, keys_twin, values, values_twin, mixed, lse, attended, activated, slope)
        )
        stream = following
    output = from_clip(stream.astype(BF16))

    gradient = to_clip(cotangent)
    owned, sums = [None] * LAYERS, [None] * LAYERS
    for layer in reversed(range(LAYERS)):
        shares, stream, queries, keys, keys_twin, values, values_twin, mixed, lse, attended, activated, slope = saved[
            layer
        ]
        down = down_weight_grad(place, activated, gradient)
        hidden_grad, attended_grad, mixed_grad, feed_sums, up_sums = feed_back(
            place, gradient, slope, attended, vectors[layer], shares
        )
        feed_keep, feed_send = feed_weight_grads(
            place, hidden_grad, attended, attended_grad, mixed, vectors[layer]
        )
        dq, dkv_keep, dkv_send = attend_back(queries, keys, keys_twin, values, values_twin, lse, mixed_grad)
        dkv = add(dkv_keep, swap(dkv_send, "core"))
        qkv_sums, qkv_keep, qkv_send = qkv_weight_grads(place, stream, vectors[layer], dq, dkv)
        gradient, norm_sums = norm_back(place, stream, vectors[layer], attended_grad, dq, dkv, shares)
        owned[layer] = (
            reduce_grads(down[:2], down[2:], y),
            reduce_grads(feed_keep, feed_send, y),
            reduce_grads(qkv_keep, qkv_send, y),
        )
        sums[layer] = jnp.concatenate(
            [feed_sums + qkv_sums + norm_sums, up_sums.reshape(SHARDS, width)], axis=0
        )
    input_grad = from_clip(gradient.astype(BF16)).astype(F32)

    totals = lax.psum(jnp.stack(sums), ("z", "y", "x", "core"))
    own_vectors = lax.dynamic_slice_in_dim(totals[:, :8], shard * share, share, axis=2)
    own_up = lax.dynamic_slice_in_dim(
        totals[:, 8:].reshape(LAYERS, SHARDS * width), shard * width, width, axis=1
    )

    def both(part, block):
        return jnp.stack([owned[layer][part][block] for layer in range(LAYERS)])

    up_grad = jnp.stack(
        [
            jnp.transpose(owned[layer][1][1:], (1, 0, 2)).reshape(share, SHARDS * width)
            for layer in range(LAYERS)
        ]
    )
    down_grad = jnp.stack([owned[layer][0].reshape(width, width) for layer in range(LAYERS)])
    vector = [own_vectors[:, index] for index in range(8)]
    return (
        output,
        input_grad,
        vector[0],
        vector[1],
        both(2, 0),
        vector[2],
        both(2, 1),
        both(2, 2),
        vector[3],
        both(1, 0),
        vector[4],
        vector[5],
        vector[6],
        up_grad,
        own_up,
        down_grad,
        vector[7],
    )


def solution(mesh):
    groups = mesh.shape["rep"]
    finer = Mesh(mesh.devices.reshape(groups // 2, 2, 2, 2), ("z", "y", "x", "core"))
    rep, shard = ("z", "y"), ("x", "core")
    rows = P(rep, shard, None)
    vector, matrix = P(None, shard), P(None, shard, None)
    parameters = (
        vector,
        vector,
        matrix,
        vector,
        matrix,
        matrix,
        vector,
        matrix,
        vector,
        vector,
        vector,
        matrix,
        vector,
        matrix,
        vector,
    )
    return jax.shard_map(
        body,
        mesh=finer,
        in_specs=(rows, rows) + parameters,
        out_specs=(rows, rows) + parameters,
        check_vma=False,
    )
```

```python
import functools

import jax
import jax.numpy as jnp
from jax import lax
from jax.experimental import pallas as pl
from jax.experimental.pallas import tpu as pltpu
from jax.sharding import Mesh
from jax.sharding import PartitionSpec as P

HEAD = 64
LAYERS = 2
SHARDS = 4
EPSILON = 1e-05
SWAP = [(0, 1), (1, 0)]
F32 = jnp.float32
BF16 = jnp.bfloat16
NN = (((1,), (0,)), ((), ()))
NT = (((1,), (1,)), ((), ()))
TN = (((0,), (0,)), ((), ()))
VMEM_LIMIT = 56 * 1024 * 1024
SCALE = 0.0

QKV = ((0, slice(0, 3), 0),)
OUT = ((0, slice(0, 1), 0),)
UP = (((0, slice(1, 5), 0),), ((0, slice(1, 3), 0), (6, slice(0, 2), 2)))
DOWN = (((0, slice(5, 6), 0), (6, slice(0, 3), 1)), ((-6, slice(0, 4), 0),))


def dot(left, right, dims=NN):
    return lax.dot_general(left, right, dims, preferred_element_type=F32)


def swap(values, axis):
    return lax.ppermute(values, axis, SWAP)


def vmem_spec():
    return pl.BlockSpec(memory_space=pltpu.VMEM)


def any_spec():
    return pl.BlockSpec(memory_space=pl.ANY)


def smem_spec():
    return pl.BlockSpec(memory_space=pltpu.SMEM)


def cost(flops, bytes_accessed, transcendentals=0):
    return pl.CostEstimate(
        flops=int(SCALE * flops), bytes_accessed=int(SCALE * bytes_accessed), transcendentals=0
    )


def shaped(shape, dtype):
    return jax.ShapeDtypeStruct(shape, dtype)


def call(kernel, operands, in_specs, out_shape, out_specs, deps=(), **options):
    first, last = len(operands), len(operands) + len(deps)

    def ordered(*refs):
        kernel(*refs[:first], *refs[last:])

    return pl.pallas_call(
        ordered,
        in_specs=list(in_specs) + [any_spec()] * len(deps),
        out_shape=out_shape,
        out_specs=out_specs,
        compiler_params=pltpu.CompilerParams(vmem_limit_bytes=VMEM_LIMIT),
        **options,
    )(*operands, *deps)


def after(values, *deps):
    if isinstance(values, tuple):
        return lax.optimization_barrier(values + deps)[: len(values)]
    return lax.optimization_barrier((values,) + deps)[0]


def standardize(values):
    average = jnp.mean(values, axis=-1, keepdims=True)
    centered = values - average
    variance = jnp.mean(centered * centered, axis=-1, keepdims=True)
    inverse_scale = lax.rsqrt(variance + EPSILON)
    return centered * inverse_scale, inverse_scale


def norm_input_grad(grad_out, standard, inverse_scale, gain):
    grad_standard = grad_out * gain
    return inverse_scale * (
        grad_standard
        - jnp.mean(grad_standard, axis=-1, keepdims=True)
        - standard * jnp.mean(grad_standard * standard, axis=-1, keepdims=True)
    )


def column_sum(values):
    return jnp.sum(values.astype(F32), axis=0, keepdims=True)


def gelu_parts(hidden):
    density = jnp.exp(-0.5 * hidden * hidden)
    t = 1.0 / (1.0 + (0.3275911 * 0.7071067811865476) * jnp.abs(hidden))
    series = t * (
        0.127414796
        + t * (-0.142248368 + t * (0.7107068705 + t * (-0.7265760135 + t * 0.5307027145)))
    )
    tail = series * density
    phi = jnp.where(hidden >= 0.0, 1.0 - tail, tail)
    return hidden * phi, phi + (hidden * 0.3989422804014327) * density


def pieces_of(place_ref, refs):
    s, y = place_ref[0], place_ref[1]
    places = ((s, None), (s ^ 1, None), (s ^ 2, y), (s ^ 2, 1 - y), (s ^ 3, y), (s ^ 3, 1 - y))
    return [(ref, *place) for ref, place in zip(refs, places)]


def aligned(start, size):
    return pl.ds(start if isinstance(start, int) else pl.multiple_of(start, size), size)


def load_rows(refs, place_ref, groups, target, sems, rows):
    copies = []
    for first, blocks, block in groups:
        for piece, shard, half in pieces_of(place_ref, refs[first:]):
            start, size = shard * rows, rows
            if half is not None:
                size = rows // 2
                start = start + half * size
            place = target.at[pl.ds(block, blocks.stop - blocks.start), aligned(start, size), :]
            copies.append(pltpu.make_async_copy(piece.at[blocks], place, sems.at[len(copies)]))
    return copies


def load_down(refs, place_ref, groups, target, sems, rows):
    copies = []
    for first, blocks, block in groups:
        for piece, shard, half in pieces_of(place_ref, refs[first:]):
            at = pl.ds(shard * SHARDS + block, blocks.stop - blocks.start)
            place = target.at[at]
            if half is not None:
                size = rows // 2
                place = target.at[at, aligned(half * size, size)]
            copies.append(pltpu.make_async_copy(piece.at[blocks], place, sems.at[len(copies)]))
    return copies


def start_all(copies):
    for copy in copies:
        copy.start()


def wait_all(copies):
    for copy in copies:
        copy.wait()


def pack_kernel(jobs, outs_of, slices, place_ref, *refs):
    count = 1 + max(source for _, _, source, _, _ in jobs)
    sources, inputs, refs = refs[:count], refs[count : count + slices], refs[count + slices :]
    outs, picked, work, frames, sems = refs[: -3 - slices], refs[-3 - slices : -3], *refs[-3:]
    loads, stores = [], []
    for index, (chunk, block, source, layer, (rows, columns)) in enumerate(jobs):
        own, half = outs_of[chunk]
        size, width = outs[half].shape[1:]
        whole = sources[source].at[layer, pl.ds(rows, 2 * size), pl.ds(columns, width)]
        part = work.at[index, pl.ds(pl.multiple_of(place_ref[1] * size, size), size)]
        loads.append([pltpu.make_async_copy(whole, work.at[index], sems.at[0, index])])
        stores.append([pltpu.make_async_copy(part, outs[half].at[block], sems.at[1, index])])
        if own is not None:
            stores[-1].append(pltpu.make_async_copy(work.at[index], outs[own].at[block], sems.at[2, index]))
    for index, (source, target) in enumerate(zip(inputs, picked)):
        at = len(jobs) + index
        loads.append([pltpu.make_async_copy(source.at[1 - place_ref[2]], frames.at[index], sems.at[0, at])])
        stores.append([pltpu.make_async_copy(frames.at[index], target, sems.at[1, at])])
    for copies in loads:
        start_all(copies)
    for load, store in zip(loads, stores):
        wait_all(load)
        start_all(store)
    for copies in stores:
        wait_all(copies)


def pack_shares(place, sources, chunks, share, width, clips=(), deps=()):
    jobs = [
        (chunk, block) + place_of
        for chunk, (_, blocks) in enumerate(chunks)
        for block, place_of in enumerate(blocks)
    ]
    out_shape, outs_of = [], []
    for whole, blocks in chunks:
        outs_of.append((len(out_shape) if whole else None, len(out_shape) + whole))
        if whole:
            out_shape.append(shaped((len(blocks), share, width), BF16))
        out_shape.append(shaped((len(blocks), share // 2, width), BF16))
    out_shape += [shaped(clip.shape[1:], BF16) for clip in clips]
    count = len(jobs) + len(clips)
    return call(
        functools.partial(pack_kernel, jobs, outs_of, len(clips)),
        [place, *sources, *clips],
        [smem_spec()] + [any_spec()] * (len(sources) + len(clips)),
        tuple(out_shape),
        (any_spec(),) * len(out_shape),
        deps,
        scratch_shapes=[
            pltpu.VMEM((len(jobs), share, width), BF16),
            pltpu.VMEM((len(clips), clips[0].shape[1], width), BF16),
            pltpu.SemaphoreType.DMA((3, count)),
        ],
        cost_estimate=cost(0, 0),
        name="pack_shares",
    )


def project(layer, standard, vectors_ref, weights, queries_ref, keys_ref, values_ref, ready):
    normed = (standard * vectors_ref[layer, 0:1] + vectors_ref[layer, 1:2]).astype(BF16)
    ready()
    queries = (dot(normed, weights[0]) + vectors_ref[layer, 2:3]).astype(BF16)
    queries_ref[...] = queries * jnp.asarray(HEAD ** (-0.5), BF16)
    keys_ref[...] = dot(normed, weights[1]).astype(BF16)
    values_ref[...] = (dot(normed, weights[2]) + vectors_ref[layer, 3:4]).astype(BF16)


def first_qkv_kernel(place_ref, frames_ref, arrived_ref, vectors_ref, *refs):
    shares, (stream_ref, *outs, weights, sems) = refs[:-6], refs[-6:]
    copies = load_rows(shares, place_ref, QKV, weights, sems, weights.shape[1] // SHARDS)
    start_all(copies)
    quarter = arrived_ref.shape[0]
    stream_ref[:quarter] = frames_ref[place_ref[2]].astype(F32)
    stream_ref[quarter:] = arrived_ref[...].astype(F32)
    standard, _ = standardize(stream_ref[...])
    project(0, standard, vectors_ref, weights, *outs, lambda: wait_all(copies))


def qkv_kernel(layer, place_ref, stream_ref, vectors_ref, *refs):
    shares, (*outs, weights, sems) = refs[:-5], refs[-5:]
    copies = load_rows(shares, place_ref, QKV, weights, sems, weights.shape[1] // SHARDS)
    start_all(copies)
    standard, _ = standardize(stream_ref[...])
    project(layer, standard, vectors_ref, weights, *outs, lambda: wait_all(copies))


def qkv_options(rows, width, name):
    return dict(
        scratch_shapes=[pltpu.VMEM((3, width, width), BF16), pltpu.SemaphoreType.DMA((8,))],
        cost_estimate=cost(6 * rows * width * width, 10 * rows * width + 6 * width * width),
        name=name,
    )


def first_qkv(place, frames, arrived, vectors, shares, deps=()):
    rows, width = 2 * arrived.shape[0], arrived.shape[1]
    return call(
        first_qkv_kernel,
        [place, frames, arrived, vectors, *shares],
        [smem_spec()] + [vmem_spec()] * 3 + [any_spec()] * len(shares),
        (shaped((rows, width), F32),) + (shaped((rows, width), BF16),) * 3,
        (vmem_spec(),) * 4,
        deps,
        **qkv_options(rows, width, "first_qkv"),
    )


def next_qkv(layer, place, stream, vectors, shares, deps=()):
    rows, width = stream.shape
    return call(
        functools.partial(qkv_kernel, layer),
        [place, stream, vectors, *shares],
        [smem_spec()] + [vmem_spec()] * 2 + [any_spec()] * len(shares),
        (shaped((rows, width), BF16),) * 3,
        (vmem_spec(),) * 3,
        deps,
        **qkv_options(rows, width, "next_qkv"),
    )


def attention_kernel(q_ref, ko_ref, kt_ref, vo_ref, vt_ref, mixed_ref, lse_ref):
    queries_t = q_ref[...].T
    row = lax.broadcasted_iota(jnp.int32, queries_t.shape, 0)
    values_t = (vo_ref[...].T, vt_ref[...].T)
    outs = []
    for head in range(2):
        mine = (row >= head * HEAD) & (row < (head + 1) * HEAD)
        q_t = jnp.where(mine, queries_t, jnp.zeros_like(queries_t))
        scores = (dot(ko_ref[...], q_t), dot(kt_ref[...], q_t))
        peak = jnp.maximum(
            jnp.max(scores[0], axis=0, keepdims=True), jnp.max(scores[1], axis=0, keepdims=True)
        )
        weights = tuple(jnp.exp(part - peak) for part in scores)
        total = jnp.sum(weights[0], axis=0, keepdims=True) + jnp.sum(weights[1], axis=0, keepdims=True)
        lse_ref[0, head : head + 1, :] = peak + jnp.log(total)
        at = slice(head * HEAD, (head + 1) * HEAD)
        out = dot(values_t[0][at], weights[0].astype(BF16)) + dot(values_t[1][at], weights[1].astype(BF16))
        outs.append(out / total)
    mixed_ref[...] = jnp.concatenate(outs, axis=0).T.astype(BF16)


def attend(queries, keys, keys_twin, values, values_twin, deps=()):
    rows, width = queries.shape
    pairs = width // (2 * HEAD)
    block = pl.BlockSpec((rows, 2 * HEAD), lambda pair: (0, pair))
    return call(
        attention_kernel,
        [queries, keys, keys_twin, values, values_twin],
        [block] * 5,
        (shaped((rows, width), BF16), shaped((pairs, 8, rows), F32)),
        (block, pl.BlockSpec((1, 8, rows), lambda pair: (pair, 0, 0))),
        deps,
        grid=(pairs,),
        cost_estimate=cost(32 * rows * rows * width, 12 * rows * width, 4 * pairs * rows * rows),
        name="attend",
    )


def up_kernel(layer, place_ref, stream_ref, mixed_ref, vectors_ref, up_bias_ref, *refs):
    shares, (attended_ref, activated_ref, slope_ref, out_w, up_w, sems) = refs[:-6], refs[-6:]
    width = stream_ref.shape[1]
    share = width // SHARDS
    out_copies = load_rows(shares, place_ref, OUT, out_w, sems.at[0], share)
    up_copies = load_rows(shares, place_ref, UP[layer], up_w, sems.at[1], share)
    start_all(out_copies)
    start_all(up_copies)
    wait_all(out_copies)
    attended_ref[...] = stream_ref[...] + dot(mixed_ref[...], out_w[0]) + vectors_ref[layer, 4:5]
    standard, _ = standardize(attended_ref[...])
    second = (standard * vectors_ref[layer, 5:6] + vectors_ref[layer, 6:7]).astype(BF16)
    wait_all(up_copies)
    for block in range(SHARDS):
        at = slice(block * width, (block + 1) * width)
        hidden = dot(second, up_w[block]) + up_bias_ref[layer : layer + 1, at]
        activated, slope = gelu_parts(hidden)
        activated_ref[:, at] = activated.astype(BF16)
        slope_ref[:, at] = slope.astype(BF16)


def feed_up(layer, place, stream, mixed, vectors, up_bias, shares, deps=()):
    rows, width = stream.shape
    wide = SHARDS * width
    return call(
        functools.partial(up_kernel, layer),
        [place, stream, mixed, vectors, up_bias, *shares],
        [smem_spec()] + [vmem_spec()] * 4 + [any_spec()] * len(shares),
        (shaped((rows, width), F32), shaped((rows, wide), BF16), shaped((rows, wide), BF16)),
        (vmem_spec(),) * 3,
        deps,
        scratch_shapes=[
            pltpu.VMEM((1, width, width), BF16),
            pltpu.VMEM((4, width, width), BF16),
            pltpu.SemaphoreType.DMA((2, 12)),
        ],
        cost_estimate=cost(10 * rows * width * width, 24 * rows * width + 10 * width * width, rows * wide),
        name="feed_up",
    )


def down_kernel(layer, place_ref, attended_ref, activated_ref, vectors_ref, *refs):
    shares, (next_ref, down_w, sems) = refs[:-3], refs[-3:]
    width = attended_ref.shape[1]
    copies = load_down(shares, place_ref, DOWN[layer], down_w, sems, width // SHARDS)
    start_all(copies)
    next_ref[...] = attended_ref[...] + vectors_ref[layer, 7:8]
    wait_all(copies)
    next_ref[...] += dot(activated_ref[...], down_w[...].reshape(SHARDS * width, width))


def last_down_kernel(layer, place_ref, attended_ref, activated_ref, vectors_ref, *refs):
    shares, (mine_ref, other_ref, down_w, sems) = refs[:-4], refs[-4:]
    width = attended_ref.shape[1]
    copies = load_down(shares, place_ref, DOWN[layer], down_w, sems, width // SHARDS)
    start_all(copies)
    total = attended_ref[...] + vectors_ref[layer, 7:8]
    wait_all(copies)
    total += dot(activated_ref[...], down_w[...].reshape(SHARDS * width, width))
    half = mine_ref.shape[0]
    mine_ref[...] = total[:half].astype(BF16)
    other_ref[...] = total[half:].astype(BF16)


def feed_down(layer, place, attended, activated, vectors, shares, deps=()):
    rows, width = attended.shape
    last = layer == LAYERS - 1
    return call(
        functools.partial(last_down_kernel if last else down_kernel, layer),
        [place, attended, activated, vectors, *shares],
        [smem_spec()] + [vmem_spec()] * 3 + [any_spec()] * len(shares),
        (shaped((rows // 2, width), BF16),) * 2 if last else shaped((rows, width), F32),
        (vmem_spec(),) * 2 if last else vmem_spec(),
        deps,
        scratch_shapes=[
            pltpu.VMEM((4 * SHARDS, width // SHARDS, width), BF16),
            pltpu.SemaphoreType.DMA((12,)),
        ],
        cost_estimate=cost(8 * rows * width * width, 16 * rows * width + 8 * width * width),
        name="feed_down",
    )


def feed_scratch(width):
    return [
        pltpu.VMEM((1, width, width), BF16),
        pltpu.VMEM((4, width, width), BF16),
        pltpu.VMEM((4 * SHARDS, width // SHARDS, width), BF16),
        pltpu.SemaphoreType.DMA((3, 12)),
    ]


def feed_back_kernel(layer, place_ref, grad_ref, slope_ref, attended_ref, vectors_ref, *refs):
    shares, refs = refs[:-9], refs[-9:]
    hidden_ref, attended_grad_ref, mixed_grad_ref, sums_ref, up_sums_ref, out_w, up_w, down_w, sems = refs
    width = grad_ref.shape[1]
    share = width // SHARDS
    down_copies = load_down(shares, place_ref, DOWN[layer], down_w, sems.at[2], share)
    up_copies = load_rows(shares, place_ref, UP[layer], up_w, sems.at[1], share)
    out_copies = load_rows(shares, place_ref, OUT, out_w, sems.at[0], share)
    start_all(down_copies)
    start_all(up_copies)
    start_all(out_copies)
    branch = grad_ref[...].astype(BF16)
    sums_ref[...] = jnp.zeros_like(sums_ref)
    sums_ref[7:8] = column_sum(branch)
    wait_all(down_copies)
    wait_all(up_copies)
    second_grad = None
    for block in range(SHARDS):
        at = slice(block * width, (block + 1) * width)
        down = down_w[block * SHARDS : (block + 1) * SHARDS].reshape(width, width)
        hidden_grad = (dot(branch, down, NT) * slope_ref[:, at].astype(F32)).astype(BF16)
        hidden_ref[:, at] = hidden_grad
        up_sums_ref[:, at] = column_sum(hidden_grad)
        part = dot(hidden_grad, up_w[block], NT)
        second_grad = part if second_grad is None else second_grad + part
    standard, inverse = standardize(attended_ref[...])
    sums_ref[5:6] = column_sum(second_grad * standard)
    sums_ref[6:7] = column_sum(second_grad)
    attended_grad = grad_ref[...] + norm_input_grad(second_grad, standard, inverse, vectors_ref[layer, 5:6])
    attended_grad_ref[...] = attended_grad
    out_grad = attended_grad.astype(BF16)
    sums_ref[4:5] = column_sum(out_grad)
    wait_all(out_copies)
    mixed_grad_ref[...] = dot(out_grad, out_w[0], NT).astype(BF16)


def feed_back(layer, place, grad, slope, attended, vectors, shares, deps=()):
    rows, width = grad.shape
    wide = SHARDS * width
    return call(
        functools.partial(feed_back_kernel, layer),
        [place, grad, slope, attended, vectors, *shares],
        [smem_spec()] + [vmem_spec()] * 4 + [any_spec()] * len(shares),
        (
            shaped((rows, wide), BF16),
            shaped((rows, width), F32),
            shaped((rows, width), BF16),
            shaped((8, width), F32),
            shaped((1, wide), F32),
        ),
        (vmem_spec(),) * 5,
        deps,
        scratch_shapes=feed_scratch(width),
        cost_estimate=cost(18 * rows * width * width, 30 * rows * width + 18 * width * width),
        name="feed_back",
    )


def owners(place_ref, keep_ref, send_refs):
    s = place_ref[0]
    return (
        (s ^ 3, send_refs[2:]),
        (s ^ 1, send_refs[:2]),
        (s ^ 2, (keep_ref.at[1, 0], keep_ref.at[1, 1])),
        (s, (keep_ref.at[0, 0], keep_ref.at[0, 1])),
    )


def quarters(place_ref, split, rows):
    size = rows // 4
    near, inner = (place_ref[1], place_ref[3]) if split else (0, 0)
    for y in range(2):
        for z in range(2):
            start = (near ^ y) * (2 * size) + (inner ^ z) * size
            yield y, z, pl.ds(pl.multiple_of(start, size), size)


def run_steps(steps, work, sems):
    pending = [None, None]
    for index, (make, targets) in enumerate(steps):
        slot = index % 2
        if pending[slot] is not None:
            wait_all(pending[slot])
        work[slot] = make().astype(BF16).reshape(work.shape[1:])
        copies = [
            pltpu.make_async_copy(source, target, sems.at[slot, number])
            for number, (source, target) in enumerate(targets(work.at[slot]))
        ]
        start_all(copies)
        pending[slot] = copies
    for copies in pending:
        if copies is not None:
            wait_all(copies)


def by_rows(place_ref, split, keep_ref, send_refs, block):
    def targets(work):
        return [
            (work.at[shard, rows], target[y].at[z, block])
            for shard, target in owners(place_ref, keep_ref, send_refs)
            for y, z, rows in quarters(place_ref, split, work.shape[1])
        ]

    return targets


def whole_share(place_ref, split, target):
    def targets(work):
        return [
            (work.at[:, rows], target[y].at[z]) for y, z, rows in quarters(place_ref, split, work.shape[1])
        ]

    return targets


def down_grad_kernel(split, place_ref, activated_ref, grad_ref, keep_ref, *refs):
    send_refs, (work, sems) = refs[:4], refs[4:]
    width = grad_ref.shape[1]
    branch = grad_ref[...].astype(BF16)
    steps = []
    for shard, target in owners(place_ref, keep_ref, send_refs):
        at = pl.ds(pl.multiple_of(shard * width, width), width)
        steps.append(
            (lambda at=at: dot(activated_ref[:, at], branch, TN), whole_share(place_ref, split, target))
        )
    run_steps(steps, work, sems)


def grad_shapes(count, width):
    part = (2, count, width // SHARDS // 4, width)
    return (shaped((2, 2) + part, BF16),) + (shaped(part, BF16),) * 4


def grad_scratch(width):
    return [pltpu.VMEM((2, SHARDS, width // SHARDS, width), BF16), pltpu.SemaphoreType.DMA((2, 16))]


def down_weight_grad(place, split, activated, grad, deps=()):
    rows, width = grad.shape
    return call(
        functools.partial(down_grad_kernel, split),
        [place, activated, grad],
        [smem_spec()] + [vmem_spec()] * 2,
        grad_shapes(SHARDS, width),
        (any_spec(),) * 5,
        deps,
        scratch_shapes=grad_scratch(width),
        cost_estimate=cost(8 * rows * width * width, 12 * rows * width + 8 * width * width),
        name="down_weight_grad",
    )


def feed_grad_kernel(
    layer,
    split,
    place_ref,
    hidden_ref,
    attended_ref,
    attended_grad_ref,
    mixed_ref,
    vectors_ref,
    keep_ref,
    *refs,
):
    send_refs, (work, sems) = refs[:4], refs[4:]
    width = attended_ref.shape[1]
    standard, _ = standardize(attended_ref[...])
    second_t = (standard * vectors_ref[layer, 5:6] + vectors_ref[layer, 6:7]).astype(BF16).T
    steps = [
        (
            lambda: dot(mixed_ref[...], attended_grad_ref[...].astype(BF16), TN),
            by_rows(place_ref, split, keep_ref, send_refs, 0),
        )
    ]
    for block in range(SHARDS):
        at = slice(block * width, (block + 1) * width)
        steps.append(
            (lambda at=at: dot(second_t, hidden_ref[:, at]), by_rows(place_ref, split, keep_ref, send_refs, 1 + block))
        )
    run_steps(steps, work, sems)


def feed_weight_grads(layer, split, place, hidden_grad, attended, attended_grad, mixed, vectors, deps=()):
    rows, width = attended.shape
    return call(
        functools.partial(feed_grad_kernel, layer, split),
        [place, hidden_grad, attended, attended_grad, mixed, vectors],
        [smem_spec()] + [vmem_spec()] * 5,
        grad_shapes(1 + SHARDS, width),
        (any_spec(),) * 5,
        deps,
        scratch_shapes=grad_scratch(width),
        cost_estimate=cost(10 * rows * width * width, 20 * rows * width + 10 * width * width),
        name="feed_weight_grads",
    )


def qkv_grad_kernel(
    layer,
    split,
    place_ref,
    stream_ref,
    vectors_ref,
    dq_ref,
    dk_ref,
    dv_ref,
    dk_back_ref,
    dv_back_ref,
    sums_ref,
    total_ref,
    keep_ref,
    *refs,
):
    send_refs, (work, sems) = refs[:4], refs[4:]
    standard, _ = standardize(stream_ref[...])
    normed_t = (standard * vectors_ref[layer, 0:1] + vectors_ref[layer, 1:2]).astype(BF16).T
    total_ref[0] = (dk_ref[...].astype(F32) + dk_back_ref[...].astype(F32)).astype(BF16)
    total_ref[1] = (dv_ref[...].astype(F32) + dv_back_ref[...].astype(F32)).astype(BF16)
    sums_ref[...] = jnp.zeros_like(sums_ref)
    sums_ref[2:3] = column_sum(dq_ref[...])
    sums_ref[3:4] = column_sum(total_ref[1])
    makers = (
        lambda: dot(normed_t, dq_ref[...]),
        lambda: dot(normed_t, total_ref[0]),
        lambda: dot(normed_t, total_ref[1]),
    )
    run_steps(
        [(make, by_rows(place_ref, split, keep_ref, send_refs, block)) for block, make in enumerate(makers)],
        work,
        sems,
    )


def qkv_weight_grads(layer, split, place, stream, vectors, dq, dk, dv, dk_back, dv_back, deps=()):
    rows, width = stream.shape
    return call(
        functools.partial(qkv_grad_kernel, layer, split),
        [place, stream, vectors, dq, dk, dv, dk_back, dv_back],
        [smem_spec()] + [vmem_spec()] * 7,
        (shaped((8, width), F32), shaped((2, rows, width), BF16)) + grad_shapes(3, width),
        (vmem_spec(),) * 2 + (any_spec(),) * 5,
        deps,
        scratch_shapes=grad_scratch(width),
        cost_estimate=cost(6 * rows * width * width, 10 * rows * width + 6 * width * width),
        name="qkv_weight_grads",
    )


def attention_back_kernel(
    q_ref,
    ko_ref,
    kt_ref,
    vo_ref,
    vt_ref,
    lse_ref,
    out_grad_ref,
    dq_ref,
    dk_ref,
    dv_ref,
    dk_twin_ref,
    dv_twin_ref,
):
    queries = q_ref[...]
    out_grad = out_grad_ref[...]
    queries_t, out_grad_t = queries.T, out_grad.T
    row = lax.broadcasted_iota(jnp.int32, queries_t.shape, 0)
    lane = lax.broadcasted_iota(jnp.int32, queries.shape, 1)
    keys, values = (ko_ref, kt_ref), (vo_ref, vt_ref)
    keys_t = tuple(part[...].T for part in keys)
    key_grads, value_grads, query_grads = [None, None], [None, None], []
    for head in range(2):
        low, high = head * HEAD, (head + 1) * HEAD
        mine_t = (row >= low) & (row < high)
        mine = (lane >= low) & (lane < high)
        q_t = jnp.where(mine_t, queries_t, jnp.zeros_like(queries_t))
        o_t = jnp.where(mine_t, out_grad_t, jnp.zeros_like(queries_t))
        q_h = jnp.where(mine, queries, jnp.zeros_like(queries))
        o_h = jnp.where(mine, out_grad, jnp.zeros_like(queries))
        lse = lse_ref[0, head : head + 1, :]
        probability = [jnp.exp(dot(part[...], q_t) - lse) for part in keys]
        probability_grad = [dot(part[...], o_t) for part in values]
        inner = sum(
            jnp.sum(left * right, axis=0, keepdims=True)
            for left, right in zip(probability, probability_grad)
        )
        query_grad = None
        for index in range(2):
            score_grad = (probability[index] * (probability_grad[index] - inner)).astype(BF16)
            value_part = dot(probability[index].astype(BF16), o_h)
            key_part = dot(score_grad, q_h)
            query_part = dot(keys_t[index][low:high], score_grad)
            if head == 0:
                key_grads[index], value_grads[index] = key_part, value_part
            else:
                key_grads[index] += key_part
                value_grads[index] += value_part
            query_grad = query_part if index == 0 else query_grad + query_part
        query_grads.append(query_grad)
    dq_ref[...] = (jnp.concatenate(query_grads, axis=0).T * HEAD ** (-0.5)).astype(BF16)
    for ref, value in zip((dk_ref, dk_twin_ref, dv_ref, dv_twin_ref), key_grads + value_grads):
        ref[...] = value.astype(BF16)


def attend_back(queries, keys, keys_twin, values, values_twin, lse, out_grad, deps=()):
    rows, width = queries.shape
    pairs = width // (2 * HEAD)
    block = pl.BlockSpec((rows, 2 * HEAD), lambda pair: (0, pair))
    return call(
        attention_back_kernel,
        [queries, keys, keys_twin, values, values_twin, lse, out_grad],
        [block] * 5 + [pl.BlockSpec((1, 8, rows), lambda pair: (pair, 0, 0)), block],
        (shaped((rows, width), BF16),) * 5,
        (block,) * 5,
        deps,
        grid=(pairs,),
        cost_estimate=cost(80 * rows * rows * width, 24 * rows * width),
        name="attend_back",
    )


def norm_back_kernel(layer, place_ref, stream_ref, vectors_ref, attended_grad_ref, dq_ref, dkv_ref, *refs):
    shares, (grad_ref, sums_ref, weights, sems) = refs[:-4], refs[-4:]
    copies = load_rows(shares, place_ref, QKV, weights, sems, weights.shape[1] // SHARDS)
    start_all(copies)
    standard, inverse = standardize(stream_ref[...])
    wait_all(copies)
    normed_grad = (
        dot(dq_ref[...], weights[0], NT) + dot(dkv_ref[0], weights[1], NT) + dot(dkv_ref[1], weights[2], NT)
    )
    sums_ref[...] = jnp.zeros_like(sums_ref)
    sums_ref[0:1] = column_sum(normed_grad * standard)
    sums_ref[1:2] = column_sum(normed_grad)
    grad_ref[...] = attended_grad_ref[...] + norm_input_grad(
        normed_grad, standard, inverse, vectors_ref[layer, 0:1]
    )


def norm_back(layer, place, stream, vectors, attended_grad, dq, dkv, shares, deps=()):
    rows, width = stream.shape
    return call(
        functools.partial(norm_back_kernel, layer),
        [place, stream, vectors, attended_grad, dq, dkv, *shares],
        [smem_spec()] + [vmem_spec()] * 5 + [any_spec()] * len(shares),
        (shaped((rows, width), F32), shaped((8, width), F32)),
        (vmem_spec(),) * 2,
        deps,
        scratch_shapes=[pltpu.VMEM((3, width, width), BF16), pltpu.SemaphoreType.DMA((8,))],
        cost_estimate=cost(6 * rows * width * width, 18 * rows * width + 6 * width * width),
        name="norm_back",
    )


def finish_kernel(layer, split, pieces, places, place_ref, *refs):
    sources, refs = refs[: len(pieces)], refs[len(pieces) :]
    outs, (arrived, work, sems) = refs[:-3], refs[-3:]
    count = len(places)
    near, inner = (place_ref[1], place_ref[3]) if split else (0, 0)
    size, width = work.shape[1:]
    loads = []
    for index, (source, (start, _, _)) in enumerate(zip(sources, pieces)):
        at = pl.ds(index * count, count)
        loads.append(pltpu.make_async_copy(source.at[pl.ds(start, count)], arrived.at[at], sems.at[0, index]))
    start_all(loads)
    stores = []
    for number, (load, (_, y, z)) in enumerate(zip(loads, pieces)):
        load.wait()
        for block, (out, row, column) in enumerate(places):
            index = number * count + block
            work[index] = arrived[index].astype(F32)
            start = row + (near ^ y) * (2 * size) + (inner ^ z) * size
            target = outs[out].at[layer, aligned(start, size), pl.ds(column, width)]
            stores.append(pltpu.make_async_copy(work.at[index], target, sems.at[1, index]))
            stores[-1].start()
    wait_all(stores)


def finish(layer, split, sources, places, out_shapes, place, buffers=None, deps=()):
    size, width = sources[0][0].shape[-2:]
    count = 4 * len(places)
    operands = [place, *(source[0] for source in sources)]
    aliases = {}
    if buffers is not None:
        aliases = {len(operands) + index: index for index in range(len(buffers))}
        operands += list(buffers)
    first = 1 + len(sources)
    pieces = [source[1:] for source in sources]

    def kernel(*refs):
        finish_kernel(layer, split, pieces, places, *refs[:first], *refs[len(operands) :])

    return call(
        kernel,
        operands,
        [smem_spec()] + [any_spec()] * (len(operands) - 1),
        tuple(shaped(shape, F32) for shape in out_shapes),
        (any_spec(),) * len(out_shapes),
        deps,
        input_output_aliases=aliases,
        scratch_shapes=[
            pltpu.VMEM((count, size, width), BF16),
            pltpu.VMEM((count, size, width), F32),
            pltpu.SemaphoreType.DMA((2, count)),
        ],
        cost_estimate=cost(0, 6 * count * size * width),
        name="finish",
    )


def combine_kernel(plan, *refs):
    arrays = 1 + max(operand for segments in plan for _, terms in segments for operand, _ in terms)
    operands, outs, (work, sems, out_sems) = refs[:arrays], refs[arrays:-3], refs[-3:]
    jobs, copies, at = [], [], 0
    for out, segments in zip(outs, plan):
        place = 0
        for count, terms in segments:
            places = []
            for operand, start in terms:
                source = operands[operand].at[pl.ds(start, count)]
                copies.append(
                    pltpu.make_async_copy(source, work.at[pl.ds(at, count)], sems.at[len(copies)])
                )
                places.append((copies[-1], at))
                at += count
            jobs.append((out, place, count, places))
            place += count
    start_all(copies)
    stores = []
    for out, place, count, places in jobs:
        for copy, _ in places:
            copy.wait()
        first = places[0][1]
        if len(places) == 2:
            for index in range(count):
                work[first + index] += work[places[1][1] + index]
        elif len(places) > 2:
            for index in range(count):
                total = work[first + index].astype(F32)
                for _, start in places[1:]:
                    total += work[start + index].astype(F32)
                work[first + index] = total.astype(BF16)
        stores.append(
            pltpu.make_async_copy(
                work.at[pl.ds(first, count)], out.at[pl.ds(place, count)], out_sems.at[len(stores)]
            )
        )
        stores[-1].start()
    wait_all(stores)


def combine(outputs, deps=()):
    arrays, plan = [], []
    for segments in outputs:
        plan.append([])
        for count, terms in segments:
            named = []
            for array, start in terms:
                index = next((i for i, known in enumerate(arrays) if known is array), len(arrays))
                if index == len(arrays):
                    arrays.append(array)
                named.append((index, start))
            plan[-1].append((count, named))
    size, width = arrays[0].shape[1:]
    moves = [len(terms) for segments in plan for _, terms in segments]
    rows = sum(count * len(terms) for segments in plan for count, terms in segments)
    return call(
        functools.partial(combine_kernel, plan),
        arrays,
        [any_spec()] * len(arrays),
        tuple(shaped((sum(count for count, _ in segments), size, width), BF16) for segments in plan),
        (any_spec(),) * len(plan),
        deps,
        scratch_shapes=[
            pltpu.VMEM((rows, size, width), BF16),
            pltpu.SemaphoreType.DMA((sum(moves),)),
            pltpu.SemaphoreType.DMA((len(moves),)),
        ],
        cost_estimate=cost(0, 0),
        name="combine",
    )


PAIRS, MIRROR = [(0, 1), (1, 0), (2, 3), (3, 2)], [(0, 3), (3, 0), (1, 2), (2, 1)]


class Flow:
    def __init__(self, split, parts, *pins, last="spread"):
        keep, *send = parts
        self.split, self.count, self.last = split, keep.shape[3], last
        self.keep = keep.reshape((-1,) + keep.shape[-2:])
        send = after(tuple(send), *pins)
        self.back = [swap(part.reshape((-1,) + part.shape[-2:]), "core") for part in send]

    def sums(self, x, y, z, *arrivals):
        n = self.count
        terms = [(self.keep, (4 * x + 2 * y + z) * n), (self.back[2 * x + y], z * n)]
        return (n, terms + [(array, start + offset * n) for (array, start), offset in arrivals])

    def segments(self, stage):
        n = self.count
        if stage == "x":
            return {"x": [self.sums(1, y, z) for y in range(2) for z in range(2)]}
        if stage == "y":
            return {"y": [self.sums(0, 1, z, (self.x, 2 + z)) for z in range(2)]}
        if stage == "pair":
            if not self.split:
                return {"sum": [self.sums(0, 0, z, (self.x, z), (self.y, z)) for z in range(2)]}
            return {"pair": [self.sums(0, 0, 1, (self.x, 1), (self.y, 1))]}
        if stage == "mirror":
            if not self.split:
                return {}
            return {"mirror": [self.sums(0, 0, 0, (self.x, 0), (self.y, 0), (self.pair, 0))]}
        if stage == "after":
            if not self.split:
                return {"near": [(2 * n, [self.sum])]}
            whole = (n, [self.mirror_sent, self.mirror])
            return {"near": [whole], "spread": [whole]}
        if not self.split:
            return {}
        return {self.last: [(n, [self.rest if self.last == "spread" else self.part_z])]}

    def record(self, stage, channel, sent, arrived):
        if stage == "after":
            if channel == "near":
                self.part, self.rest = sent, arrived
            else:
                self.part_z = arrived
        elif stage == "last":
            self.rest_z = arrived
        else:
            setattr(self, channel, arrived)
            setattr(self, channel + "_sent", sent)

    def finish(self, layer, places, out_shapes, place, buffers=None, deps=()):
        n = self.count
        if self.split:
            sources = [(*self.part, 0, 0), (*self.part_z, 0, 1), (*self.rest, 1, 0), (*self.rest_z, 1, 1)]
        else:
            sources = [
                (array, start + z * n, y, z)
                for y, (array, start) in enumerate((self.part, self.rest))
                for z in range(2)
            ]
        return finish(layer, self.split, sources, places, out_shapes, place, buffers, deps)


class Totals:
    def __init__(self, split, values):
        self.split = split
        self.terms = [(values, 0), (swap(values, "core"), 0)]

    def segments(self, stage):
        if stage in ("pair", "mirror") and not self.split:
            return {"sum": [(1, self.terms)]} if stage == "pair" else {}
        return {stage: [(1, self.terms)]}

    def record(self, stage, channel, sent, arrived):
        self.terms = [arrived] if channel == "sum" else [sent, arrived]

    def done(self):
        return sum(array[start].astype(F32) for array, start in self.terms)


def exchange(steps, *pins):
    outputs, owners_of = {}, {}
    for flow, stage in steps:
        for channel, segments in flow.segments(stage).items():
            placed = outputs.setdefault(channel, [])
            start = sum(count for count, _ in placed)
            owners_of.setdefault(channel, []).append((flow, stage, start))
            placed += segments
    if not outputs:
        return pins[0], ()
    names, landed = list(outputs), []
    results = combine([outputs[name] for name in names], pins)
    for name, sent in zip(names, results):
        if name == "sum":
            arrived = lax.psum(sent, "z")
        elif name in ("pair", "spread", "mirror"):
            arrived = lax.ppermute(sent, "z", MIRROR if name == "mirror" else PAIRS)
        else:
            arrived = swap(sent, "y" if name == "near" else name)
        landed.append(arrived)
        for flow, stage, start in owners_of[name]:
            flow.record(stage, name, (sent, start), (arrived, start))
    return results[0], tuple(landed)


def body(
    frames,
    cotangent,
    first_gain,
    first_shift,
    query_weight,
    query_bias,
    key_weight,
    value_weight,
    value_bias,
    out_weight,
    out_bias,
    second_gain,
    second_shift,
    up_weight,
    up_bias,
    down_weight,
    down_bias,
):
    x, y, z, core = (lax.axis_index(axis) for axis in ("x", "y", "z", "core"))
    shard = 2 * x + core
    inner = jnp.where((z == 0) | (z == 3), 0, 1)
    place = jnp.stack([shard, y, x, inner]).astype(jnp.int32)
    quarter, width = frames.shape[1:]
    share = width // SHARDS
    split = lax.axis_size("z") == 4

    def blocks_of(layer):
        attention = [(source, layer, (0, 0)) for source in (0, 1, 2)]
        up = [(3, layer, (0, 0))] + [(4, layer, (0, block * width)) for block in range(SHARDS)]
        down = [(5, layer, (block * share, 0)) for block in range(SHARDS)]
        return attention, up, down

    sources = (query_weight, key_weight, value_weight, out_weight, up_weight, down_weight)
    (attention0, up0, down0), (attention1, up1, down1) = blocks_of(0), blocks_of(1)
    own0, half0, other_frames = pack_shares(
        place, sources[:3], [(True, attention0)], share, width, clips=(frames,)
    )
    near = {0: swap(half0, "x")}
    arrived_frames = swap(other_frames, "x")
    twin = {0: swap(own0, "core")}
    *packed, other_cotangent = pack_shares(
        place,
        sources,
        [
            (True, blocks)
            for blocks in (up0 + down0[:1], down0[1:], attention1, up1[:3], up1[3:], down1)
        ],
        share,
        width,
        clips=(cotangent,),
        deps=(half0,),
    )
    own, half = dict(enumerate([own0, *packed[0::2]])), dict(enumerate([half0, *packed[1::2]]))
    near[0] = after(near[0], half[1])
    far, near_twin, far_twin = {0: swap(near[0], "y")}, {0: swap(near[0], "core")}, {}

    small = jnp.stack(
        [first_gain, first_shift, query_bias, value_bias, out_bias, second_gain, second_shift, down_bias], axis=1
    )
    small = jnp.concatenate([small, up_bias.reshape(LAYERS, SHARDS, share)], axis=1)
    small = after(small, half0)
    pair = jnp.stack([small, swap(small, "core")])
    pieces = jnp.concatenate([pair, swap(pair, "x")], axis=0)
    small = jnp.stack(
        [lax.dynamic_index_in_dim(pieces, shard ^ index, 0, keepdims=False) for index in range(SHARDS)]
    ).astype(F32)
    vectors = jnp.transpose(small[:, :, :8], (1, 2, 0, 3)).reshape(LAYERS, 8, width)
    up_biases = jnp.transpose(small[:, :, 8:], (1, 0, 2, 3)).reshape(LAYERS, SHARDS * width)

    def fetch(chunk, *pins):
        near[chunk] = swap(after(half[chunk], *pins), "x")

    def spread(chunk, *pins):
        far[chunk] = swap(after(near[chunk], *pins), "y")

    def trade(chunk, *pins):
        twin[chunk] = swap(after(own[chunk], *pins), "core")

    def trade_near(chunk, *pins):
        near_twin[chunk] = swap(after(near[chunk], *pins), "core")

    def trade_far(chunk, *pins):
        far_twin[chunk] = swap(after(far[chunk], *pins), "core")

    def shares(chunk):
        return own[chunk], twin[chunk], near[chunk], far[chunk], near_twin[chunk], far_twin[chunk]

    trade_far(0)
    fetch(1, arrived_frames)
    for chunk in range(1, 7):
        trade(chunk, arrived_frames)
    stream0, queries0, keys0, values0 = first_qkv(
        place, frames, arrived_frames, vectors, shares(0), deps=tuple(twin[chunk] for chunk in range(1, 7))
    )
    qkv0 = shares(0)
    keys0, values0 = after((keys0, values0), near[1])
    keys_twin0, values_twin0 = swap(keys0, "core"), swap(values0, "core")
    fetch(2, keys0)
    spread(1, keys0)
    trade_near(1, keys0)
    mixed0, lse0 = attend(queries0, keys0, keys_twin0, values0, values_twin0, deps=(near_twin[1],))
    trade_far(1, mixed0)
    fetch(3, near[2], mixed0)
    spread(2, mixed0)
    trade_near(2, mixed0)
    attended0, activated0, slope0 = feed_up(
        0, place, stream0, mixed0, vectors, up_biases, shares(1), deps=(near_twin[2],)
    )
    trade_far(2, activated0)
    fetch(4, near[3], activated0)
    spread(3, activated0)
    trade_near(3, activated0)
    second0 = shares(1) + shares(2)
    stream1 = feed_down(0, place, attended0, activated0, vectors, second0, deps=(near_twin[3],))
    trade_far(3, stream1)
    fetch(5, near[4], stream1)
    spread(4, stream1)
    trade_near(4, stream1)
    qkv1 = shares(3)
    queries1, keys1, values1 = next_qkv(1, place, stream1, vectors, qkv1, deps=(near_twin[4],))
    keys1, values1 = after((keys1, values1), near[5], far[4])
    keys_twin1, values_twin1 = swap(keys1, "core"), swap(values1, "core")
    fetch(6, near[5], keys1)
    spread(5, keys1)
    trade_near(5, keys1)
    trade_far(4, keys1)
    mixed1, lse1 = attend(
        queries1, keys1, keys_twin1, values1, values_twin1, deps=(near_twin[5], far_twin[4])
    )
    trade_far(5, mixed1)
    spread(6, mixed1)
    trade_near(6, mixed1)
    arrived_cotangent = swap(after(other_cotangent, near[6]), "x")
    late = shares(4) + shares(5)
    attended1, activated1, slope1 = feed_up(
        1, place, stream1, mixed1, vectors, up_biases, late, deps=(near_twin[6],)
    )
    mine_cotangent = lax.dynamic_index_in_dim(cotangent, x, 0, keepdims=False)
    pieces = after((mine_cotangent, arrived_cotangent), attended1)
    gradient = jnp.concatenate(pieces, axis=0).astype(F32)
    down1 = Flow(split, down_weight_grad(place, split, activated1, gradient), far[6])
    trade_far(6, down1.keep)
    output_mine, output_other = feed_down(1, place, attended1, activated1, vectors, shares(6))
    late += shares(6)

    def by_clip(mine, other):
        return jnp.where(x == 0, jnp.stack([mine, other]), jnp.stack([other, mine]))

    output_other = swap(output_other, "x")

    def square(row_blocks, column_blocks):
        return (LAYERS, row_blocks * share, column_blocks * width)

    down_places, down_shapes = [(0, block * share, 0) for block in range(SHARDS)], [square(SHARDS, 1)]
    feed_places = [(0, 0, 0)] + [(1, 0, block * width) for block in range(SHARDS)]
    feed_shapes = [square(1, 1), square(1, SHARDS)]
    qkv_places, qkv_shapes = [(block, 0, 0) for block in range(3)], [square(1, 1)] * 3

    pin, landed = exchange([(down1, "x")], output_mine, *down1.back)
    hidden_grad, attended_grad, mixed_grad, feed_sums1, up_sums1 = feed_back(
        1, place, gradient, slope1, attended1, vectors, late, deps=(pin,)
    )
    parts = feed_weight_grads(1, split, place, hidden_grad, attended1, attended_grad, mixed1, vectors)
    feed1 = Flow(split, parts, *landed, output_other)
    output = by_clip(output_mine, output_other)
    pin, (near, far) = exchange([(down1, "y"), (feed1, "x")], *feed1.back)
    dq, dk, dv, dk_twin, dv_twin = attend_back(
        queries1, keys1, keys_twin1, values1, values_twin1, lse1, mixed_grad, deps=(pin,)
    )
    dk_twin, dv_twin = after((dk_twin, dv_twin), near)
    dk_back, dv_back = swap(dk_twin, "core"), swap(dv_twin, "core")
    pin, landed = exchange([(down1, "pair")], dq)
    qkv_sums1, dkv, *parts = qkv_weight_grads(
        1, split, place, stream1, vectors, dq, dk, dv, dk_back, dv_back, deps=(pin,)
    )
    gradient, norm_sums1 = norm_back(
        1, place, stream1, vectors, attended_grad, dq, dkv, qkv1, deps=(parts[0],)
    )
    qkv_1 = Flow(split, parts, far, *landed)
    pin, landed = exchange([(qkv_1, "x"), (feed1, "y"), (down1, "mirror")], gradient, *qkv_1.back)

    parts = down_weight_grad(place, split, activated0, gradient, deps=(pin,))
    hidden_grad, attended_grad, mixed_grad, feed_sums0, up_sums0 = feed_back(
        0, place, gradient, slope0, attended0, vectors, second0, deps=(parts[0],)
    )
    down0 = Flow(split, parts, mixed_grad, *landed, last="near")
    steps = [(down0, "x"), (qkv_1, "y"), (down1, "after"), (feed1, "pair")]
    pin, landed = exchange(steps, mixed_grad, *down0.back)
    parts = feed_weight_grads(
        0, split, place, hidden_grad, attended0, attended_grad, mixed0, vectors, deps=(pin,)
    )
    dq, dk, dv, dk_twin, dv_twin = attend_back(
        queries0, keys0, keys_twin0, values0, values_twin0, lse0, mixed_grad, deps=(parts[0],)
    )
    dk_twin, dv_twin = after((dk_twin, dv_twin), *landed)
    dk_back, dv_back = swap(dk_twin, "core"), swap(dv_twin, "core")
    feed0 = Flow(split, parts, dq, *landed, last="near")
    steps = [(feed0, "x"), (down0, "y"), (down1, "last"), (qkv_1, "pair"), (feed1, "mirror")]
    pin, (far, *landed) = exchange(steps, dq, *feed0.back)
    qkv_sums0, dkv, *parts = qkv_weight_grads(
        0, split, place, stream0, vectors, dq, dk, dv, dk_back, dv_back, deps=(pin,)
    )
    gradient, norm_sums0 = norm_back(
        0, place, stream0, vectors, attended_grad, dq, dkv, qkv0, deps=(parts[0],)
    )
    qkv_0 = Flow(split, parts, gradient, *landed, last="near")
    sums = jnp.concatenate(
        [
            part
            for feed, qkv, norm, up in (
                (feed_sums0, qkv_sums0, norm_sums0, up_sums0),
                (feed_sums1, qkv_sums1, norm_sums1, up_sums1),
            )
            for part in (feed + qkv + norm, up.reshape(SHARDS, width))
        ]
    ).astype(BF16)
    sums = jnp.pad(sums, ((0, share // 4 - sums.shape[0]), (0, 0)))
    totals = Totals(split, sums[None])
    steps = [(qkv_0, "x"), (totals, "x"), (down0, "pair"), (feed1, "after")]
    pin, landed = exchange(steps, gradient, *qkv_0.back)
    down_out = down1.finish(1, down_places, down_shapes, place, deps=(pin,))
    pin, landed = exchange([(feed0, "y"), (down0, "mirror"), (feed1, "last")], down_out[0])
    input_other = swap(after(gradient[quarter:].astype(BF16), pin), "x")
    steps = [(qkv_0, "y"), (totals, "y"), (feed0, "pair"), (down0, "after"), (qkv_1, "mirror")]
    pin, landed = exchange(steps, pin)
    feed_out = feed1.finish(1, feed_places, feed_shapes, place, deps=(pin, input_other))
    input_grad = by_clip(gradient[:quarter], input_other.astype(F32))
    steps = [(qkv_0, "pair"), (totals, "pair"), (feed0, "mirror"), (down0, "last"), (qkv_1, "after")]
    pin, landed = exchange(steps, feed_out[0])
    steps = [(qkv_0, "mirror"), (totals, "mirror"), (feed0, "after"), (qkv_1, "last")]
    pin, landed = exchange(steps, pin)
    (down_out,) = down0.finish(0, down_places, down_shapes, place, down_out, deps=(pin,))
    pin, landed = exchange([(qkv_0, "after"), (feed0, "last")], down_out)
    totals = totals.done()[: LAYERS * (8 + SHARDS)].reshape(LAYERS, 8 + SHARDS, width)
    qkv_out = qkv_1.finish(1, qkv_places, qkv_shapes, place, deps=(pin,))
    pin, landed = exchange([(qkv_0, "last")], qkv_out[0])
    out_out, up_out = feed0.finish(0, feed_places, feed_shapes, place, feed_out, deps=(pin,))
    query_out, key_out, value_out = qkv_0.finish(0, qkv_places, qkv_shapes, place, qkv_out, deps=(out_out,))

    own_vectors = lax.dynamic_slice_in_dim(totals[:, :8], shard * share, share, axis=2)
    own_up = lax.dynamic_slice_in_dim(
        totals[:, 8:].reshape(LAYERS, SHARDS * width), shard * width, width, axis=1
    )
    vector = [own_vectors[:, index] for index in range(8)]
    return (
        output,
        input_grad,
        vector[0],
        vector[1],
        query_out,
        vector[2],
        key_out,
        value_out,
        vector[3],
        out_out,
        vector[4],
        vector[5],
        vector[6],
        up_out,
        own_up,
        down_out,
        vector[7],
    )


def solution(mesh):
    groups = mesh.shape["rep"]
    finer = Mesh(mesh.devices.reshape(groups // 2, 2, 2, 2), ("z", "y", "x", "core"))
    rep, shard = ("z", "y"), ("x", "core")
    rows = P(rep, shard, None)
    vector, matrix = P(None, shard), P(None, shard, None)
    parameters = (
        vector,
        vector,
        matrix,
        vector,
        matrix,
        matrix,
        vector,
        matrix,
        vector,
        vector,
        vector,
        matrix,
        vector,
        matrix,
        vector,
    )
    return jax.shard_map(
        body,
        mesh=finer,
        in_specs=(rows, rows) + parameters,
        out_specs=(rows, rows) + parameters,
        check_vma=False,
    )
```

```python
import functools

import jax
import jax.numpy as jnp
from jax import lax
from jax.experimental import pallas as pl
from jax.experimental.pallas import tpu as pltpu
from jax.sharding import Mesh
from jax.sharding import PartitionSpec as P

HEAD = 64
LAYERS = 2
SHARDS = 4
EPSILON = 1e-05
SWAP = [(0, 1), (1, 0)]
F32 = jnp.float32
BF16 = jnp.bfloat16
NN = (((1,), (0,)), ((), ()))
NT = (((1,), (1,)), ((), ()))
TN = (((0,), (0,)), ((), ()))
VMEM_LIMIT = 40 * 1024 * 1024
SCALE = 0.0

QKV = ((0, slice(0, 3), 0),)
OUT = ((0, slice(0, 1), 0),)
UP = (((0, slice(1, 5), 0),), ((0, slice(1, 3), 0), (6, slice(0, 2), 2)))
DOWN = (((0, slice(5, 6), 0), (6, slice(0, 3), 1)), ((-6, slice(0, 4), 0),))


def dot(left, right, dims=NN):
    return lax.dot_general(left, right, dims, preferred_element_type=F32)


def swap(values, axis):
    return lax.ppermute(values, axis, SWAP)


def vmem_spec():
    return pl.BlockSpec(memory_space=pltpu.VMEM)


def any_spec():
    return pl.BlockSpec(memory_space=pl.ANY)


def hbm_spec():
    return pl.BlockSpec(memory_space=pltpu.HBM)


def smem_spec():
    return pl.BlockSpec(memory_space=pltpu.SMEM)


def cost(flops, bytes_accessed, transcendentals=0):
    return pl.CostEstimate(
        flops=int(SCALE * flops), bytes_accessed=int(SCALE * bytes_accessed), transcendentals=0
    )


def shaped(shape, dtype):
    return jax.ShapeDtypeStruct(shape, dtype)


def call(kernel, operands, in_specs, out_shape, out_specs, deps=(), **options):
    def placed(array, spec):
        if spec.memory_space == pltpu.HBM:
            return pltpu.with_memory_space_constraint(array, pltpu.HBM)
        return array

    def result(shape, spec):
        return pltpu.HBM(shape.shape, shape.dtype) if spec.memory_space == pltpu.HBM else shape

    if isinstance(out_shape, tuple):
        out_shape = tuple(map(result, out_shape, out_specs))
    if deps:
        operands = [after(operands[0], *deps), *operands[1:]]
    return pl.pallas_call(
        kernel,
        in_specs=list(in_specs),
        out_shape=out_shape,
        out_specs=out_specs,
        compiler_params=pltpu.CompilerParams(vmem_limit_bytes=VMEM_LIMIT),
        **options,
    )(*map(placed, operands, in_specs))


def after(values, *deps):
    if isinstance(values, tuple):
        return lax.optimization_barrier(values + deps)[: len(values)]
    return lax.optimization_barrier((values,) + deps)[0]


def standardize(values):
    average = jnp.mean(values, axis=-1, keepdims=True)
    centered = values - average
    variance = jnp.mean(centered * centered, axis=-1, keepdims=True)
    inverse_scale = lax.rsqrt(variance + EPSILON)
    return centered * inverse_scale, inverse_scale


def norm_input_grad(grad_out, standard, inverse_scale, gain):
    grad_standard = grad_out * gain
    return inverse_scale * (
        grad_standard
        - jnp.mean(grad_standard, axis=-1, keepdims=True)
        - standard * jnp.mean(grad_standard * standard, axis=-1, keepdims=True)
    )


def column_sum(values):
    return jnp.sum(values.astype(F32), axis=0, keepdims=True)


def gelu_parts(hidden):
    density = jnp.exp(-0.5 * hidden * hidden)
    t = 1.0 / (1.0 + (0.3275911 * 0.7071067811865476) * jnp.abs(hidden))
    series = t * (
        0.127414796
        + t * (-0.142248368 + t * (0.7107068705 + t * (-0.7265760135 + t * 0.5307027145)))
    )
    tail = series * density
    phi = jnp.where(hidden >= 0.0, 1.0 - tail, tail)
    return hidden * phi, phi + (hidden * 0.3989422804014327) * density


def pieces_of(place_ref, refs):
    s, y = place_ref[0], place_ref[1]
    places = ((s, None), (s ^ 1, None), (s ^ 2, y), (s ^ 2, 1 - y), (s ^ 3, y), (s ^ 3, 1 - y))
    return [(ref, *place) for ref, place in zip(refs, places)]


def aligned(start, size):
    return pl.ds(start if isinstance(start, int) else pl.multiple_of(start, size), size)


def load_rows(refs, place_ref, groups, target, sems, rows):
    copies = []
    for first, blocks, block in groups:
        for piece, shard, half in pieces_of(place_ref, refs[first:]):
            start, size = shard * rows, rows
            if half is not None:
                size = rows // 2
                start = start + half * size
            place = target.at[pl.ds(block, blocks.stop - blocks.start), aligned(start, size), :]
            copies.append(pltpu.make_async_copy(piece.at[blocks], place, sems.at[len(copies)]))
    return copies


def load_down(refs, place_ref, groups, target, sems, rows):
    copies = []
    for first, blocks, block in groups:
        for piece, shard, half in pieces_of(place_ref, refs[first:]):
            at = pl.ds(shard * SHARDS + block, blocks.stop - blocks.start)
            place = target.at[at]
            if half is not None:
                size = rows // 2
                place = target.at[at, aligned(half * size, size)]
            copies.append(pltpu.make_async_copy(piece.at[blocks], place, sems.at[len(copies)]))
    return copies


def start_all(copies):
    for copy in copies:
        copy.start()


def wait_all(copies):
    for copy in copies:
        copy.wait()


def pack_kernel(jobs, outs_of, slices, place_ref, *refs):
    count = 1 + max(source for _, _, source, _, _ in jobs)
    sources, inputs, refs = refs[:count], refs[count : count + slices], refs[count + slices :]
    outs, picked, work, frames, sems = refs[: -3 - slices], refs[-3 - slices : -3], *refs[-3:]
    loads, stores = [], []
    for index, (chunk, block, source, layer, (rows, columns)) in enumerate(jobs):
        own, half = outs_of[chunk]
        size, width = outs[half].shape[1:]
        whole = sources[source].at[layer, pl.ds(rows, 2 * size), pl.ds(columns, width)]
        part = work.at[index, pl.ds(pl.multiple_of(place_ref[1] * size, size), size)]
        loads.append([pltpu.make_async_copy(whole, work.at[index], sems.at[0, index])])
        stores.append([pltpu.make_async_copy(part, outs[half].at[block], sems.at[1, index])])
        if own is not None:
            stores[-1].append(pltpu.make_async_copy(work.at[index], outs[own].at[block], sems.at[2, index]))
    for index, (source, target) in enumerate(zip(inputs, picked)):
        at = len(jobs) + index
        loads.append([pltpu.make_async_copy(source.at[1 - place_ref[2]], frames.at[index], sems.at[0, at])])
        stores.append([pltpu.make_async_copy(frames.at[index], target, sems.at[1, at])])
    for copies in loads:
        start_all(copies)
    for load, store in zip(loads, stores):
        wait_all(load)
        start_all(store)
    for copies in stores:
        wait_all(copies)


def pack_shares(place, sources, chunks, share, width, clips=(), deps=()):
    jobs = [
        (chunk, block) + place_of
        for chunk, (_, blocks) in enumerate(chunks)
        for block, place_of in enumerate(blocks)
    ]
    out_shape, outs_of = [], []
    for whole, blocks in chunks:
        outs_of.append((len(out_shape) if whole else None, len(out_shape) + whole))
        if whole:
            out_shape.append(shaped((len(blocks), share, width), BF16))
        out_shape.append(shaped((len(blocks), share // 2, width), BF16))
    out_shape += [shaped(clip.shape[1:], BF16) for clip in clips]
    count = len(jobs) + len(clips)
    return call(
        functools.partial(pack_kernel, jobs, outs_of, len(clips)),
        [place, *sources, *clips],
        [smem_spec()] + [hbm_spec()] * (len(sources) + len(clips)),
        tuple(out_shape),
        (hbm_spec(),) * len(out_shape),
        deps,
        scratch_shapes=[
            pltpu.VMEM((len(jobs), share, width), BF16),
            pltpu.VMEM((len(clips), clips[0].shape[1], width), BF16),
            pltpu.SemaphoreType.DMA((3, count)),
        ],
        cost_estimate=cost(0, 0),
        name="pack_shares",
    )


def project(layer, standard, vectors_ref, weights, queries_ref, keys_ref, values_ref, ready):
    normed = (standard * vectors_ref[layer, 0:1] + vectors_ref[layer, 1:2]).astype(BF16)
    ready()
    queries = (dot(normed, weights[0]) + vectors_ref[layer, 2:3]).astype(BF16)
    queries_ref[...] = queries * jnp.asarray(HEAD ** (-0.5), BF16)
    keys_ref[...] = dot(normed, weights[1]).astype(BF16)
    values_ref[...] = (dot(normed, weights[2]) + vectors_ref[layer, 3:4]).astype(BF16)


def first_qkv_kernel(place_ref, frames_ref, arrived_ref, vectors_ref, *refs):
    shares, (stream_ref, *outs, weights, sems) = refs[:-6], refs[-6:]
    copies = load_rows(shares, place_ref, QKV, weights, sems, weights.shape[1] // SHARDS)
    start_all(copies)
    quarter = arrived_ref.shape[0]
    stream_ref[:quarter] = frames_ref[place_ref[2]].astype(F32)
    stream_ref[quarter:] = arrived_ref[...].astype(F32)
    standard, _ = standardize(stream_ref[...])
    project(0, standard, vectors_ref, weights, *outs, lambda: wait_all(copies))


def qkv_kernel(layer, place_ref, stream_ref, vectors_ref, *refs):
    shares, (*outs, weights, sems) = refs[:-5], refs[-5:]
    copies = load_rows(shares, place_ref, QKV, weights, sems, weights.shape[1] // SHARDS)
    start_all(copies)
    standard, _ = standardize(stream_ref[...])
    project(layer, standard, vectors_ref, weights, *outs, lambda: wait_all(copies))


def qkv_options(rows, width, name):
    return dict(
        scratch_shapes=[pltpu.VMEM((3, width, width), BF16), pltpu.SemaphoreType.DMA((8,))],
        cost_estimate=cost(6 * rows * width * width, 10 * rows * width + 6 * width * width),
        name=name,
    )


def first_qkv(place, frames, arrived, vectors, shares, deps=()):
    rows, width = 2 * arrived.shape[0], arrived.shape[1]
    return call(
        first_qkv_kernel,
        [place, frames, arrived, vectors, *shares],
        [smem_spec()] + [vmem_spec()] * 3 + [hbm_spec()] * len(shares),
        (shaped((rows, width), F32),) + (shaped((rows, width), BF16),) * 3,
        (vmem_spec(),) * 4,
        deps,
        **qkv_options(rows, width, "first_qkv"),
    )


def next_qkv(layer, place, stream, vectors, shares, deps=()):
    rows, width = stream.shape
    return call(
        functools.partial(qkv_kernel, layer),
        [place, stream, vectors, *shares],
        [smem_spec()] + [vmem_spec()] * 2 + [hbm_spec()] * len(shares),
        (shaped((rows, width), BF16),) * 3,
        (vmem_spec(),) * 3,
        deps,
        **qkv_options(rows, width, "next_qkv"),
    )


def attention_kernel(q_ref, ko_ref, kt_ref, vo_ref, vt_ref, mixed_ref, lse_ref):
    queries_t = q_ref[...].T
    row = lax.broadcasted_iota(jnp.int32, queries_t.shape, 0)
    values_t = (vo_ref[...].T, vt_ref[...].T)
    outs = []
    for head in range(2):
        mine = (row >= head * HEAD) & (row < (head + 1) * HEAD)
        q_t = jnp.where(mine, queries_t, jnp.zeros_like(queries_t))
        scores = (dot(ko_ref[...], q_t), dot(kt_ref[...], q_t))
        peak = jnp.maximum(
            jnp.max(scores[0], axis=0, keepdims=True), jnp.max(scores[1], axis=0, keepdims=True)
        )
        weights = tuple(jnp.exp(part - peak) for part in scores)
        total = jnp.sum(weights[0], axis=0, keepdims=True) + jnp.sum(weights[1], axis=0, keepdims=True)
        lse_ref[0, head : head + 1, :] = peak + jnp.log(total)
        at = slice(head * HEAD, (head + 1) * HEAD)
        out = dot(values_t[0][at], weights[0].astype(BF16)) + dot(values_t[1][at], weights[1].astype(BF16))
        outs.append(out / total)
    mixed_ref[...] = jnp.concatenate(outs, axis=0).T.astype(BF16)


def attend(queries, keys, keys_twin, values, values_twin, deps=()):
    rows, width = queries.shape
    pairs = width // (2 * HEAD)
    block = pl.BlockSpec((rows, 2 * HEAD), lambda pair: (0, pair))
    return call(
        attention_kernel,
        [queries, keys, keys_twin, values, values_twin],
        [block] * 5,
        (shaped((rows, width), BF16), shaped((pairs, 8, rows), F32)),
        (block, pl.BlockSpec((1, 8, rows), lambda pair: (pair, 0, 0))),
        deps,
        grid=(pairs,),
        cost_estimate=cost(32 * rows * rows * width, 12 * rows * width, 4 * pairs * rows * rows),
        name="attend",
    )


def up_kernel(layer, place_ref, stream_ref, mixed_ref, vectors_ref, up_bias_ref, *refs):
    shares, (attended_ref, activated_ref, slope_ref, out_w, up_w, sems) = refs[:-6], refs[-6:]
    width = stream_ref.shape[1]
    share = width // SHARDS
    out_copies = load_rows(shares, place_ref, OUT, out_w, sems.at[0], share)
    up_copies = load_rows(shares, place_ref, UP[layer], up_w, sems.at[1], share)
    start_all(out_copies)
    start_all(up_copies)
    wait_all(out_copies)
    attended_ref[...] = stream_ref[...] + dot(mixed_ref[...], out_w[0]) + vectors_ref[layer, 4:5]
    standard, _ = standardize(attended_ref[...])
    second = (standard * vectors_ref[layer, 5:6] + vectors_ref[layer, 6:7]).astype(BF16)
    wait_all(up_copies)
    for block in range(SHARDS):
        at = slice(block * width, (block + 1) * width)
        hidden = dot(second, up_w[block]) + up_bias_ref[layer : layer + 1, at]
        activated, slope = gelu_parts(hidden)
        activated_ref[:, at] = activated.astype(BF16)
        slope_ref[:, at] = slope.astype(BF16)


def feed_up(layer, place, stream, mixed, vectors, up_bias, shares, deps=()):
    rows, width = stream.shape
    wide = SHARDS * width
    return call(
        functools.partial(up_kernel, layer),
        [place, stream, mixed, vectors, up_bias, *shares],
        [smem_spec()] + [vmem_spec()] * 4 + [hbm_spec()] * len(shares),
        (shaped((rows, width), F32), shaped((rows, wide), BF16), shaped((rows, wide), BF16)),
        (vmem_spec(),) * 3,
        deps,
        scratch_shapes=[
            pltpu.VMEM((1, width, width), BF16),
            pltpu.VMEM((4, width, width), BF16),
            pltpu.SemaphoreType.DMA((2, 12)),
        ],
        cost_estimate=cost(10 * rows * width * width, 24 * rows * width + 10 * width * width, rows * wide),
        name="feed_up",
    )


def down_kernel(layer, place_ref, attended_ref, activated_ref, vectors_ref, *refs):
    shares, (next_ref, down_w, sems) = refs[:-3], refs[-3:]
    width = attended_ref.shape[1]
    copies = load_down(shares, place_ref, DOWN[layer], down_w, sems, width // SHARDS)
    start_all(copies)
    next_ref[...] = attended_ref[...] + vectors_ref[layer, 7:8]
    wait_all(copies)
    next_ref[...] += dot(activated_ref[...], down_w[...].reshape(SHARDS * width, width))


def last_down_kernel(layer, place_ref, attended_ref, activated_ref, vectors_ref, *refs):
    shares, (mine_ref, other_ref, down_w, sems) = refs[:-4], refs[-4:]
    width = attended_ref.shape[1]
    copies = load_down(shares, place_ref, DOWN[layer], down_w, sems, width // SHARDS)
    start_all(copies)
    total = attended_ref[...] + vectors_ref[layer, 7:8]
    wait_all(copies)
    total += dot(activated_ref[...], down_w[...].reshape(SHARDS * width, width))
    half = mine_ref.shape[0]
    mine_ref[...] = total[:half].astype(BF16)
    other_ref[...] = total[half:].astype(BF16)


def feed_down(layer, place, attended, activated, vectors, shares, deps=()):
    rows, width = attended.shape
    last = layer == LAYERS - 1
    return call(
        functools.partial(last_down_kernel if last else down_kernel, layer),
        [place, attended, activated, vectors, *shares],
        [smem_spec()] + [vmem_spec()] * 3 + [hbm_spec()] * len(shares),
        (shaped((rows // 2, width), BF16),) * 2 if last else shaped((rows, width), F32),
        (vmem_spec(),) * 2 if last else vmem_spec(),
        deps,
        scratch_shapes=[
            pltpu.VMEM((4 * SHARDS, width // SHARDS, width), BF16),
            pltpu.SemaphoreType.DMA((12,)),
        ],
        cost_estimate=cost(8 * rows * width * width, 16 * rows * width + 8 * width * width),
        name="feed_down",
    )


def feed_scratch(width):
    return [
        pltpu.VMEM((1, width, width), BF16),
        pltpu.VMEM((4, width, width), BF16),
        pltpu.VMEM((4 * SHARDS, width // SHARDS, width), BF16),
        pltpu.SemaphoreType.DMA((3, 12)),
    ]


def feed_back_kernel(layer, place_ref, grad_ref, slope_ref, attended_ref, vectors_ref, *refs):
    shares, refs = refs[:-9], refs[-9:]
    hidden_ref, attended_grad_ref, mixed_grad_ref, sums_ref, up_sums_ref, out_w, up_w, down_w, sems = refs
    width = grad_ref.shape[1]
    share = width // SHARDS
    down_copies = load_down(shares, place_ref, DOWN[layer], down_w, sems.at[2], share)
    up_copies = load_rows(shares, place_ref, UP[layer], up_w, sems.at[1], share)
    out_copies = load_rows(shares, place_ref, OUT, out_w, sems.at[0], share)
    start_all(down_copies)
    start_all(up_copies)
    start_all(out_copies)
    branch = grad_ref[...].astype(BF16)
    sums_ref[...] = jnp.zeros_like(sums_ref)
    sums_ref[7:8] = column_sum(branch)
    wait_all(down_copies)
    wait_all(up_copies)
    second_grad = None
    for block in range(SHARDS):
        at = slice(block * width, (block + 1) * width)
        down = down_w[block * SHARDS : (block + 1) * SHARDS].reshape(width, width)
        hidden_grad = (dot(branch, down, NT) * slope_ref[:, at].astype(F32)).astype(BF16)
        hidden_ref[:, at] = hidden_grad
        up_sums_ref[:, at] = column_sum(hidden_grad)
        part = dot(hidden_grad, up_w[block], NT)
        second_grad = part if second_grad is None else second_grad + part
    standard, inverse = standardize(attended_ref[...])
    sums_ref[5:6] = column_sum(second_grad * standard)
    sums_ref[6:7] = column_sum(second_grad)
    attended_grad = grad_ref[...] + norm_input_grad(second_grad, standard, inverse, vectors_ref[layer, 5:6])
    attended_grad_ref[...] = attended_grad
    out_grad = attended_grad.astype(BF16)
    sums_ref[4:5] = column_sum(out_grad)
    wait_all(out_copies)
    mixed_grad_ref[...] = dot(out_grad, out_w[0], NT).astype(BF16)


def feed_back(layer, place, grad, slope, attended, vectors, shares, deps=()):
    rows, width = grad.shape
    wide = SHARDS * width
    return call(
        functools.partial(feed_back_kernel, layer),
        [place, grad, slope, attended, vectors, *shares],
        [smem_spec()] + [vmem_spec()] * 4 + [hbm_spec()] * len(shares),
        (
            shaped((rows, wide), BF16),
            shaped((rows, width), F32),
            shaped((rows, width), BF16),
            shaped((8, width), F32),
            shaped((1, wide), F32),
        ),
        (vmem_spec(),) * 5,
        deps,
        scratch_shapes=feed_scratch(width),
        cost_estimate=cost(18 * rows * width * width, 30 * rows * width + 18 * width * width),
        name="feed_back",
    )


def owners(place_ref, keep_ref, send_refs):
    s = place_ref[0]
    return (
        (s ^ 3, send_refs[2:]),
        (s ^ 1, send_refs[:2]),
        (s ^ 2, (keep_ref.at[1, 0], keep_ref.at[1, 1])),
        (s, (keep_ref.at[0, 0], keep_ref.at[0, 1])),
    )


def quarters(place_ref, split, rows):
    size = rows // 4
    near, inner = (place_ref[1], place_ref[3]) if split else (0, 0)
    for y in range(2):
        for z in range(2):
            start = (near ^ y) * (2 * size) + (inner ^ z) * size
            yield y, z, pl.ds(pl.multiple_of(start, size), size)


def run_steps(steps, work, sems):
    pending = [None, None]
    for index, (make, targets) in enumerate(steps):
        slot = index % 2
        if pending[slot] is not None:
            wait_all(pending[slot])
        work[slot] = make().astype(BF16).reshape(work.shape[1:])
        copies = [
            pltpu.make_async_copy(source, target, sems.at[slot, number])
            for number, (source, target) in enumerate(targets(work.at[slot]))
        ]
        start_all(copies)
        pending[slot] = copies
    for copies in pending:
        if copies is not None:
            wait_all(copies)


def by_rows(place_ref, split, keep_ref, send_refs, block):
    def targets(work):
        return [
            (work.at[shard, rows], target[y].at[z, block])
            for shard, target in owners(place_ref, keep_ref, send_refs)
            for y, z, rows in quarters(place_ref, split, work.shape[1])
        ]

    return targets


def whole_share(place_ref, split, target):
    def targets(work):
        return [
            (work.at[:, rows], target[y].at[z]) for y, z, rows in quarters(place_ref, split, work.shape[1])
        ]

    return targets


def down_grad_kernel(split, place_ref, activated_ref, grad_ref, keep_ref, *refs):
    send_refs, (work, sems) = refs[:4], refs[4:]
    width = grad_ref.shape[1]
    branch = grad_ref[...].astype(BF16)
    steps = []
    for shard, target in owners(place_ref, keep_ref, send_refs):
        at = pl.ds(pl.multiple_of(shard * width, width), width)
        steps.append(
            (lambda at=at: dot(activated_ref[:, at], branch, TN), whole_share(place_ref, split, target))
        )
    run_steps(steps, work, sems)


def grad_shapes(count, width):
    part = (2, count, width // SHARDS // 4, width)
    return (shaped((2, 2) + part, BF16),) + (shaped(part, BF16),) * 4


def grad_scratch(width):
    return [pltpu.VMEM((2, SHARDS, width // SHARDS, width), BF16), pltpu.SemaphoreType.DMA((2, 16))]


def down_weight_grad(place, split, activated, grad, deps=()):
    rows, width = grad.shape
    return call(
        functools.partial(down_grad_kernel, split),
        [place, activated, grad],
        [smem_spec()] + [vmem_spec()] * 2,
        grad_shapes(SHARDS, width),
        (hbm_spec(),) * 5,
        deps,
        scratch_shapes=grad_scratch(width),
        cost_estimate=cost(8 * rows * width * width, 12 * rows * width + 8 * width * width),
        name="down_weight_grad",
    )


def feed_grad_kernel(
    layer,
    split,
    place_ref,
    hidden_ref,
    attended_ref,
    attended_grad_ref,
    mixed_ref,
    vectors_ref,
    keep_ref,
    *refs,
):
    send_refs, (work, sems) = refs[:4], refs[4:]
    width = attended_ref.shape[1]
    standard, _ = standardize(attended_ref[...])
    second_t = (standard * vectors_ref[layer, 5:6] + vectors_ref[layer, 6:7]).astype(BF16).T
    steps = [
        (
            lambda: dot(mixed_ref[...], attended_grad_ref[...].astype(BF16), TN),
            by_rows(place_ref, split, keep_ref, send_refs, 0),
        )
    ]
    for block in range(SHARDS):
        at = slice(block * width, (block + 1) * width)
        steps.append(
            (lambda at=at: dot(second_t, hidden_ref[:, at]), by_rows(place_ref, split, keep_ref, send_refs, 1 + block))
        )
    run_steps(steps, work, sems)


def feed_weight_grads(layer, split, place, hidden_grad, attended, attended_grad, mixed, vectors, deps=()):
    rows, width = attended.shape
    return call(
        functools.partial(feed_grad_kernel, layer, split),
        [place, hidden_grad, attended, attended_grad, mixed, vectors],
        [smem_spec()] + [vmem_spec()] * 5,
        grad_shapes(1 + SHARDS, width),
        (hbm_spec(),) * 5,
        deps,
        scratch_shapes=grad_scratch(width),
        cost_estimate=cost(10 * rows * width * width, 20 * rows * width + 10 * width * width),
        name="feed_weight_grads",
    )


def qkv_grad_kernel(
    layer,
    split,
    place_ref,
    stream_ref,
    vectors_ref,
    dq_ref,
    dk_ref,
    dv_ref,
    dk_back_ref,
    dv_back_ref,
    sums_ref,
    total_ref,
    keep_ref,
    *refs,
):
    send_refs, (work, sems) = refs[:4], refs[4:]
    standard, _ = standardize(stream_ref[...])
    normed_t = (standard * vectors_ref[layer, 0:1] + vectors_ref[layer, 1:2]).astype(BF16).T
    total_ref[0] = (dk_ref[...].astype(F32) + dk_back_ref[...].astype(F32)).astype(BF16)
    total_ref[1] = (dv_ref[...].astype(F32) + dv_back_ref[...].astype(F32)).astype(BF16)
    sums_ref[...] = jnp.zeros_like(sums_ref)
    sums_ref[2:3] = column_sum(dq_ref[...])
    sums_ref[3:4] = column_sum(total_ref[1])
    makers = (
        lambda: dot(normed_t, dq_ref[...]),
        lambda: dot(normed_t, total_ref[0]),
        lambda: dot(normed_t, total_ref[1]),
    )
    run_steps(
        [(make, by_rows(place_ref, split, keep_ref, send_refs, block)) for block, make in enumerate(makers)],
        work,
        sems,
    )


def qkv_weight_grads(layer, split, place, stream, vectors, dq, dk, dv, dk_back, dv_back, deps=()):
    rows, width = stream.shape
    return call(
        functools.partial(qkv_grad_kernel, layer, split),
        [place, stream, vectors, dq, dk, dv, dk_back, dv_back],
        [smem_spec()] + [vmem_spec()] * 7,
        (shaped((8, width), F32), shaped((2, rows, width), BF16)) + grad_shapes(3, width),
        (vmem_spec(),) * 2 + (hbm_spec(),) * 5,
        deps,
        scratch_shapes=grad_scratch(width),
        cost_estimate=cost(6 * rows * width * width, 10 * rows * width + 6 * width * width),
        name="qkv_weight_grads",
    )


def attention_back_kernel(
    q_ref,
    ko_ref,
    kt_ref,
    vo_ref,
    vt_ref,
    lse_ref,
    out_grad_ref,
    dq_ref,
    dk_ref,
    dv_ref,
    dk_twin_ref,
    dv_twin_ref,
):
    queries = q_ref[...]
    out_grad = out_grad_ref[...]
    queries_t, out_grad_t = queries.T, out_grad.T
    row = lax.broadcasted_iota(jnp.int32, queries_t.shape, 0)
    lane = lax.broadcasted_iota(jnp.int32, queries.shape, 1)
    keys, values = (ko_ref, kt_ref), (vo_ref, vt_ref)
    keys_t = tuple(part[...].T for part in keys)
    key_grads, value_grads, query_grads = [None, None], [None, None], []
    for head in range(2):
        low, high = head * HEAD, (head + 1) * HEAD
        mine_t = (row >= low) & (row < high)
        mine = (lane >= low) & (lane < high)
        q_t = jnp.where(mine_t, queries_t, jnp.zeros_like(queries_t))
        o_t = jnp.where(mine_t, out_grad_t, jnp.zeros_like(queries_t))
        q_h = jnp.where(mine, queries, jnp.zeros_like(queries))
        o_h = jnp.where(mine, out_grad, jnp.zeros_like(queries))
        lse = lse_ref[0, head : head + 1, :]
        probability = [jnp.exp(dot(part[...], q_t) - lse) for part in keys]
        probability_grad = [dot(part[...], o_t) for part in values]
        inner = sum(
            jnp.sum(left * right, axis=0, keepdims=True)
            for left, right in zip(probability, probability_grad)
        )
        query_grad = None
        for index in range(2):
            score_grad = (probability[index] * (probability_grad[index] - inner)).astype(BF16)
            value_part = dot(probability[index].astype(BF16), o_h)
            key_part = dot(score_grad, q_h)
            query_part = dot(keys_t[index][low:high], score_grad)
            if head == 0:
                key_grads[index], value_grads[index] = key_part, value_part
            else:
                key_grads[index] += key_part
                value_grads[index] += value_part
            query_grad = query_part if index == 0 else query_grad + query_part
        query_grads.append(query_grad)
    dq_ref[...] = (jnp.concatenate(query_grads, axis=0).T * HEAD ** (-0.5)).astype(BF16)
    for ref, value in zip((dk_ref, dk_twin_ref, dv_ref, dv_twin_ref), key_grads + value_grads):
        ref[...] = value.astype(BF16)


def attend_back(queries, keys, keys_twin, values, values_twin, lse, out_grad, deps=()):
    rows, width = queries.shape
    pairs = width // (2 * HEAD)
    block = pl.BlockSpec((rows, 2 * HEAD), lambda pair: (0, pair))
    return call(
        attention_back_kernel,
        [queries, keys, keys_twin, values, values_twin, lse, out_grad],
        [block] * 5 + [pl.BlockSpec((1, 8, rows), lambda pair: (pair, 0, 0)), block],
        (shaped((rows, width), BF16),) * 5,
        (block,) * 5,
        deps,
        grid=(pairs,),
        cost_estimate=cost(80 * rows * rows * width, 24 * rows * width),
        name="attend_back",
    )


def norm_back_kernel(layer, place_ref, stream_ref, vectors_ref, attended_grad_ref, dq_ref, dkv_ref, *refs):
    shares, (grad_ref, sums_ref, weights, sems) = refs[:-4], refs[-4:]
    copies = load_rows(shares, place_ref, QKV, weights, sems, weights.shape[1] // SHARDS)
    start_all(copies)
    standard, inverse = standardize(stream_ref[...])
    wait_all(copies)
    normed_grad = (
        dot(dq_ref[...], weights[0], NT) + dot(dkv_ref[0], weights[1], NT) + dot(dkv_ref[1], weights[2], NT)
    )
    sums_ref[...] = jnp.zeros_like(sums_ref)
    sums_ref[0:1] = column_sum(normed_grad * standard)
    sums_ref[1:2] = column_sum(normed_grad)
    grad_ref[...] = attended_grad_ref[...] + norm_input_grad(
        normed_grad, standard, inverse, vectors_ref[layer, 0:1]
    )


def norm_back(layer, place, stream, vectors, attended_grad, dq, dkv, shares, deps=()):
    rows, width = stream.shape
    return call(
        functools.partial(norm_back_kernel, layer),
        [place, stream, vectors, attended_grad, dq, dkv, *shares],
        [smem_spec()] + [vmem_spec()] * 5 + [hbm_spec()] * len(shares),
        (shaped((rows, width), F32), shaped((8, width), F32)),
        (vmem_spec(),) * 2,
        deps,
        scratch_shapes=[pltpu.VMEM((3, width, width), BF16), pltpu.SemaphoreType.DMA((8,))],
        cost_estimate=cost(6 * rows * width * width, 18 * rows * width + 6 * width * width),
        name="norm_back",
    )


def finish_kernel(layer, split, pieces, places, place_ref, *refs):
    sources, refs = refs[: len(pieces)], refs[len(pieces) :]
    outs, (arrived, work, sems) = refs[:-3], refs[-3:]
    count = len(places)
    near, inner = (place_ref[1], place_ref[3]) if split else (0, 0)
    size, width = work.shape[1:]
    loads = []
    for index, (source, (start, _, _)) in enumerate(zip(sources, pieces)):
        at = pl.ds(index * count, count)
        loads.append(pltpu.make_async_copy(source.at[pl.ds(start, count)], arrived.at[at], sems.at[0, index]))
    start_all(loads)
    stores = []
    for number, (load, (_, y, z)) in enumerate(zip(loads, pieces)):
        load.wait()
        for block, (out, row, column) in enumerate(places):
            index = number * count + block
            work[index] = arrived[index].astype(F32)
            start = row + (near ^ y) * (2 * size) + (inner ^ z) * size
            target = outs[out].at[layer, aligned(start, size), pl.ds(column, width)]
            stores.append(pltpu.make_async_copy(work.at[index], target, sems.at[1, index]))
            stores[-1].start()
    wait_all(stores)


def finish(layer, split, sources, places, out_shapes, place, buffers=None, deps=()):
    size, width = sources[0][0].shape[-2:]
    count = 4 * len(places)
    operands = [place, *(source[0] for source in sources)]
    aliases = {}
    if buffers is not None:
        aliases = {len(operands) + index: index for index in range(len(buffers))}
        operands += list(buffers)
    first = 1 + len(sources)
    pieces = [source[1:] for source in sources]

    def kernel(*refs):
        finish_kernel(layer, split, pieces, places, *refs[:first], *refs[len(operands) :])

    return call(
        kernel,
        operands,
        [smem_spec()] + [hbm_spec()] * (len(operands) - 1),
        tuple(shaped(shape, F32) for shape in out_shapes),
        (hbm_spec(),) * len(out_shapes),
        deps,
        input_output_aliases=aliases,
        scratch_shapes=[
            pltpu.VMEM((count, size, width), BF16),
            pltpu.VMEM((count, size, width), F32),
            pltpu.SemaphoreType.DMA((2, count)),
        ],
        cost_estimate=cost(0, 6 * count * size * width),
        name="finish",
    )


def combine_kernel(plan, *refs):
    arrays = 1 + max(operand for segments in plan for _, terms in segments for operand, _ in terms)
    operands, outs, (work, sems, out_sems) = refs[:arrays], refs[arrays:-3], refs[-3:]
    jobs, copies, at = [], [], 0
    for out, segments in zip(outs, plan):
        place = 0
        for count, terms in segments:
            places = []
            for operand, start in terms:
                source = operands[operand].at[pl.ds(start, count)]
                copies.append(
                    pltpu.make_async_copy(source, work.at[pl.ds(at, count)], sems.at[len(copies)])
                )
                places.append((copies[-1], at))
                at += count
            jobs.append((out, place, count, places))
            place += count
    start_all(copies)
    stores = []
    for out, place, count, places in jobs:
        for copy, _ in places:
            copy.wait()
        first = places[0][1]
        if len(places) == 2:
            for index in range(count):
                work[first + index] += work[places[1][1] + index]
        elif len(places) > 2:
            for index in range(count):
                total = work[first + index].astype(F32)
                for _, start in places[1:]:
                    total += work[start + index].astype(F32)
                work[first + index] = total.astype(BF16)
        stores.append(
            pltpu.make_async_copy(
                work.at[pl.ds(first, count)], out.at[pl.ds(place, count)], out_sems.at[len(stores)]
            )
        )
        stores[-1].start()
    wait_all(stores)


def combine(outputs, deps=()):
    arrays, plan = [], []
    for segments in outputs:
        plan.append([])
        for count, terms in segments:
            named = []
            for array, start in terms:
                index = next((i for i, known in enumerate(arrays) if known is array), len(arrays))
                if index == len(arrays):
                    arrays.append(array)
                named.append((index, start))
            plan[-1].append((count, named))
    size, width = arrays[0].shape[1:]
    moves = [len(terms) for segments in plan for _, terms in segments]
    rows = sum(count * len(terms) for segments in plan for count, terms in segments)
    return call(
        functools.partial(combine_kernel, plan),
        arrays,
        [hbm_spec()] * len(arrays),
        tuple(shaped((sum(count for count, _ in segments), size, width), BF16) for segments in plan),
        (hbm_spec(),) * len(plan),
        deps,
        scratch_shapes=[
            pltpu.VMEM((rows, size, width), BF16),
            pltpu.SemaphoreType.DMA((sum(moves),)),
            pltpu.SemaphoreType.DMA((len(moves),)),
        ],
        cost_estimate=cost(0, 0),
        name="combine",
    )


PAIRS, MIRROR = [(0, 1), (1, 0), (2, 3), (3, 2)], [(0, 3), (3, 0), (1, 2), (2, 1)]


class Flow:
    def __init__(self, split, parts, *pins, last="spread"):
        keep, *send = parts
        self.split, self.count, self.last = split, keep.shape[3], last
        self.keep = keep.reshape((-1,) + keep.shape[-2:])
        send = after(tuple(send), *pins)
        self.back = [swap(part.reshape((-1,) + part.shape[-2:]), "core") for part in send]

    def sums(self, x, y, z, *arrivals):
        n = self.count
        terms = [(self.keep, (4 * x + 2 * y + z) * n), (self.back[2 * x + y], z * n)]
        return (n, terms + [(array, start + offset * n) for (array, start), offset in arrivals])

    def segments(self, stage):
        n = self.count
        if stage == "x":
            return {"x": [self.sums(1, y, z) for y in range(2) for z in range(2)]}
        if stage == "y":
            return {"y": [self.sums(0, 1, z, (self.x, 2 + z)) for z in range(2)]}
        if stage == "pair":
            if not self.split:
                return {"sum": [self.sums(0, 0, z, (self.x, z), (self.y, z)) for z in range(2)]}
            return {"pair": [self.sums(0, 0, 1, (self.x, 1), (self.y, 1))]}
        if stage == "mirror":
            if not self.split:
                return {}
            return {"mirror": [self.sums(0, 0, 0, (self.x, 0), (self.y, 0), (self.pair, 0))]}
        if stage == "after":
            if not self.split:
                return {"near": [(2 * n, [self.sum])]}
            whole = (n, [self.mirror_sent, self.mirror])
            return {channel: [whole] for channel in ("near", "spread", "diagonal")[: 3 if self.last is None else 2]}
        if not self.split or self.last is None:
            return {}
        return {self.last: [(n, [self.rest if self.last == "spread" else self.part_z])]}

    def record(self, stage, channel, sent, arrived):
        if stage == "after":
            if channel == "near":
                self.part, self.rest = sent, arrived
            elif channel == "spread":
                self.part_z = arrived
            else:
                self.rest_z = arrived
        elif stage == "last":
            self.rest_z = arrived
        else:
            setattr(self, channel, arrived)
            setattr(self, channel + "_sent", sent)

    def finish(self, layer, places, out_shapes, place, buffers=None, deps=()):
        n = self.count
        if self.split:
            sources = [(*self.part, 0, 0), (*self.part_z, 0, 1), (*self.rest, 1, 0), (*self.rest_z, 1, 1)]
        else:
            sources = [
                (array, start + z * n, y, z)
                for y, (array, start) in enumerate((self.part, self.rest))
                for z in range(2)
            ]
        return finish(layer, self.split, sources, places, out_shapes, place, buffers, deps)


class Totals:
    def __init__(self, split, values):
        self.split = split
        self.terms = [(values, 0), (swap(values, "core"), 0)]

    def segments(self, stage):
        if stage in ("pair", "mirror") and not self.split:
            return {"sum": [(1, self.terms)]} if stage == "pair" else {}
        return {stage: [(1, self.terms)]}

    def record(self, stage, channel, sent, arrived):
        self.terms = [arrived] if channel == "sum" else [sent, arrived]

    def done(self):
        return sum(array[start].astype(F32) for array, start in self.terms)


def exchange(steps, *pins):
    outputs, owners_of = {}, {}
    for flow, stage in steps:
        for channel, segments in flow.segments(stage).items():
            placed = outputs.setdefault(channel, [])
            start = sum(count for count, _ in placed)
            owners_of.setdefault(channel, []).append((flow, stage, start))
            placed += segments
    if not outputs:
        return pins[0], ()
    names, landed = list(outputs), []
    results = combine([outputs[name] for name in names], pins)
    for name, sent in zip(names, results):
        if name == "sum":
            arrived = lax.psum(sent, "z")
        elif name == "diagonal":
            both = [(2 * left + y, 2 * right + 1 - y) for left, right in PAIRS for y in range(2)]
            arrived = lax.ppermute(sent, ("z", "y"), both)
        elif name in ("pair", "spread", "mirror"):
            arrived = lax.ppermute(sent, "z", MIRROR if name == "mirror" else PAIRS)
        else:
            arrived = swap(sent, "y" if name == "near" else name)
        landed.append(arrived)
        for flow, stage, start in owners_of[name]:
            flow.record(stage, name, (sent, start), (arrived, start))
    return results[0], tuple(landed)


def body(
    frames,
    cotangent,
    first_gain,
    first_shift,
    query_weight,
    query_bias,
    key_weight,
    value_weight,
    value_bias,
    out_weight,
    out_bias,
    second_gain,
    second_shift,
    up_weight,
    up_bias,
    down_weight,
    down_bias,
):
    x, y, z, core = (lax.axis_index(axis) for axis in ("x", "y", "z", "core"))
    shard = 2 * x + core
    inner = jnp.where((z == 0) | (z == 3), 0, 1)
    place = jnp.stack([shard, y, x, inner]).astype(jnp.int32)
    quarter, width = frames.shape[1:]
    share = width // SHARDS
    split = lax.axis_size("z") == 4

    def blocks_of(layer):
        attention = [(source, layer, (0, 0)) for source in (0, 1, 2)]
        up = [(3, layer, (0, 0))] + [(4, layer, (0, block * width)) for block in range(SHARDS)]
        down = [(5, layer, (block * share, 0)) for block in range(SHARDS)]
        return attention, up, down

    sources = (query_weight, key_weight, value_weight, out_weight, up_weight, down_weight)
    (attention0, up0, down0), (attention1, up1, down1) = blocks_of(0), blocks_of(1)
    own0, half0, other_frames = pack_shares(
        place, sources[:3], [(True, attention0)], share, width, clips=(frames,)
    )
    near = {0: swap(half0, "x")}
    arrived_frames = swap(other_frames, "x")
    twin = {0: swap(own0, "core")}
    *packed, other_cotangent = pack_shares(
        place,
        sources,
        [
            (True, blocks)
            for blocks in (up0 + down0[:1], down0[1:], attention1, up1[:3], up1[3:], down1)
        ],
        share,
        width,
        clips=(cotangent,),
        deps=(half0,),
    )
    own, half = dict(enumerate([own0, *packed[0::2]])), dict(enumerate([half0, *packed[1::2]]))
    near[0] = after(near[0], half[1])
    far, near_twin, far_twin = {0: swap(near[0], "y")}, {0: swap(near[0], "core")}, {}

    small = jnp.stack(
        [first_gain, first_shift, query_bias, value_bias, out_bias, second_gain, second_shift, down_bias], axis=1
    )
    small = jnp.concatenate([small, up_bias.reshape(LAYERS, SHARDS, share)], axis=1)
    small = after(small, half0)
    pair = jnp.stack([small, swap(small, "core")])
    pieces = jnp.concatenate([pair, swap(pair, "x")], axis=0)
    small = jnp.stack(
        [lax.dynamic_index_in_dim(pieces, shard ^ index, 0, keepdims=False) for index in range(SHARDS)]
    ).astype(F32)
    vectors = jnp.transpose(small[:, :, :8], (1, 2, 0, 3)).reshape(LAYERS, 8, width)
    up_biases = jnp.transpose(small[:, :, 8:], (1, 0, 2, 3)).reshape(LAYERS, SHARDS * width)

    def fetch(chunk, *pins):
        near[chunk] = swap(after(half[chunk], *pins), "x")

    def spread(chunk, *pins):
        far[chunk] = swap(after(near[chunk], *pins), "y")

    def trade(chunk, *pins):
        twin[chunk] = swap(after(own[chunk], *pins), "core")

    def trade_near(chunk, *pins):
        near_twin[chunk] = swap(after(near[chunk], *pins), "core")

    def trade_far(chunk, *pins):
        far_twin[chunk] = swap(after(far[chunk], *pins), "core")

    def shares(chunk):
        return own[chunk], twin[chunk], near[chunk], far[chunk], near_twin[chunk], far_twin[chunk]

    trade_far(0)
    fetch(1, arrived_frames)
    for chunk in range(1, 7):
        trade(chunk, arrived_frames)
    stream0, queries0, keys0, values0 = first_qkv(
        place, frames, arrived_frames, vectors, shares(0), deps=tuple(twin[chunk] for chunk in range(1, 7))
    )
    qkv0 = shares(0)
    keys0, values0 = after((keys0, values0), near[1])
    keys_twin0, values_twin0 = swap(keys0, "core"), swap(values0, "core")
    fetch(2, keys0)
    spread(1, keys0)
    trade_near(1, keys0)
    mixed0, lse0 = attend(queries0, keys0, keys_twin0, values0, values_twin0, deps=(near_twin[1],))
    trade_far(1, mixed0)
    fetch(3, near[2], mixed0)
    spread(2, mixed0)
    trade_near(2, mixed0)
    attended0, activated0, slope0 = feed_up(
        0, place, stream0, mixed0, vectors, up_biases, shares(1), deps=(near_twin[2],)
    )
    trade_far(2, activated0)
    fetch(4, near[3], activated0)
    spread(3, activated0)
    trade_near(3, activated0)
    second0 = shares(1) + shares(2)
    stream1 = feed_down(0, place, attended0, activated0, vectors, second0, deps=(near_twin[3],))
    trade_far(3, stream1)
    fetch(5, near[4], stream1)
    spread(4, stream1)
    trade_near(4, stream1)
    qkv1 = shares(3)
    queries1, keys1, values1 = next_qkv(1, place, stream1, vectors, qkv1, deps=(near_twin[4],))
    keys1, values1 = after((keys1, values1), near[5], far[4])
    keys_twin1, values_twin1 = swap(keys1, "core"), swap(values1, "core")
    fetch(6, near[5], keys1)
    spread(5, keys1)
    trade_near(5, keys1)
    trade_far(4, keys1)
    mixed1, lse1 = attend(
        queries1, keys1, keys_twin1, values1, values_twin1, deps=(near_twin[5], far_twin[4])
    )
    trade_far(5, mixed1)
    spread(6, mixed1)
    trade_near(6, mixed1)
    arrived_cotangent = swap(after(other_cotangent, near[6]), "x")
    late = shares(4) + shares(5)
    attended1, activated1, slope1 = feed_up(
        1, place, stream1, mixed1, vectors, up_biases, late, deps=(near_twin[6],)
    )
    mine_cotangent = lax.dynamic_index_in_dim(cotangent, x, 0, keepdims=False)
    pieces = after((mine_cotangent, arrived_cotangent), attended1)
    gradient = jnp.concatenate(pieces, axis=0).astype(F32)
    down1 = Flow(split, down_weight_grad(place, split, activated1, gradient), far[6])
    trade_far(6, down1.keep)
    output_mine, output_other = feed_down(1, place, attended1, activated1, vectors, shares(6))
    late += shares(6)

    def by_clip(mine, other):
        return jnp.where(x == 0, jnp.stack([mine, other]), jnp.stack([other, mine]))

    def square(row_blocks, column_blocks):
        return (LAYERS, row_blocks * share, column_blocks * width)

    down_places, down_shapes = [(0, block * share, 0) for block in range(SHARDS)], [square(SHARDS, 1)]
    feed_places = [(0, 0, 0)] + [(1, 0, block * width) for block in range(SHARDS)]
    feed_shapes = [square(1, 1), square(1, SHARDS)]
    qkv_places, qkv_shapes = [(block, 0, 0) for block in range(3)], [square(1, 1)] * 3

    pin, landed = exchange([(down1, "x")], output_mine, *down1.back)
    hidden_grad, attended_grad, mixed_grad, feed_sums1, up_sums1 = feed_back(
        1, place, gradient, slope1, attended1, vectors, late, deps=(pin,)
    )
    parts = feed_weight_grads(1, split, place, hidden_grad, attended1, attended_grad, mixed1, vectors)
    feed1 = Flow(split, parts, *landed)
    pin, (near, far) = exchange([(down1, "y"), (feed1, "x")], *feed1.back)
    dq, dk, dv, dk_twin, dv_twin = attend_back(
        queries1, keys1, keys_twin1, values1, values_twin1, lse1, mixed_grad, deps=(pin,)
    )
    dk_twin, dv_twin = after((dk_twin, dv_twin), near)
    dk_back, dv_back = swap(dk_twin, "core"), swap(dv_twin, "core")
    pin, landed = exchange([(down1, "pair")], dq)
    qkv_sums1, dkv, *parts = qkv_weight_grads(
        1, split, place, stream1, vectors, dq, dk, dv, dk_back, dv_back, deps=(pin,)
    )
    gradient, norm_sums1 = norm_back(
        1, place, stream1, vectors, attended_grad, dq, dkv, qkv1, deps=(parts[0],)
    )
    qkv_1 = Flow(split, parts, far, *landed, last=None)
    pin, landed = exchange([(qkv_1, "x"), (feed1, "y"), (down1, "mirror")], gradient, *qkv_1.back)

    parts = down_weight_grad(place, split, activated0, gradient, deps=(pin,))
    hidden_grad, attended_grad, mixed_grad, feed_sums0, up_sums0 = feed_back(
        0, place, gradient, slope0, attended0, vectors, second0, deps=(parts[0],)
    )
    down0 = Flow(split, parts, mixed_grad, *landed, last="near")
    steps = [(down0, "x"), (qkv_1, "y"), (down1, "after"), (feed1, "pair")]
    pin, landed = exchange(steps, mixed_grad, *down0.back)
    parts = feed_weight_grads(
        0, split, place, hidden_grad, attended0, attended_grad, mixed0, vectors, deps=(pin,)
    )
    dq, dk, dv, dk_twin, dv_twin = attend_back(
        queries0, keys0, keys_twin0, values0, values_twin0, lse0, mixed_grad, deps=(parts[0],)
    )
    dk_twin, dv_twin = after((dk_twin, dv_twin), *landed)
    dk_back, dv_back = swap(dk_twin, "core"), swap(dv_twin, "core")
    feed0 = Flow(split, parts, dq, *landed, last=None)
    steps = [(feed0, "x"), (down0, "y"), (down1, "last"), (qkv_1, "pair"), (feed1, "mirror")]
    pin, (far, *landed) = exchange(steps, dq, *feed0.back)
    qkv_sums0, dkv, *parts = qkv_weight_grads(
        0, split, place, stream0, vectors, dq, dk, dv, dk_back, dv_back, deps=(pin,)
    )
    gradient, norm_sums0 = norm_back(
        0, place, stream0, vectors, attended_grad, dq, dkv, qkv0, deps=(parts[0],)
    )
    qkv_0 = Flow(split, parts, gradient, *landed, last=None)
    sums = jnp.concatenate(
        [
            part
            for feed, qkv, norm, up in (
                (feed_sums0, qkv_sums0, norm_sums0, up_sums0),
                (feed_sums1, qkv_sums1, norm_sums1, up_sums1),
            )
            for part in (feed + qkv + norm, up.reshape(SHARDS, width))
        ]
    ).astype(BF16)
    sums = jnp.pad(sums, ((0, share // 4 - sums.shape[0]), (0, 0)))
    totals = Totals(split, sums[None])
    steps = [(qkv_0, "x"), (totals, "x"), (down0, "pair"), (feed1, "after")]
    pin, landed = exchange(steps, gradient, *qkv_0.back)
    down_out = down1.finish(1, down_places, down_shapes, place, deps=(pin,))
    pin, landed = exchange([(feed0, "y"), (down0, "mirror"), (feed1, "last")], down_out[0])
    input_other = swap(after(gradient[quarter:].astype(BF16), pin), "x")
    steps = [(qkv_0, "y"), (totals, "y"), (feed0, "pair"), (down0, "after")]
    pin, landed = exchange(steps, pin)
    output_other = swap(after(output_other, pin), "x")
    feed_out = feed1.finish(1, feed_places, feed_shapes, place, deps=(pin, input_other))
    input_grad = by_clip(gradient[:quarter], input_other.astype(F32))
    steps = [(qkv_0, "pair"), (totals, "pair"), (feed0, "mirror"), (down0, "last")]
    pin, landed = exchange(steps, feed_out[0], output_other)
    output = by_clip(output_mine, output_other)
    steps = [(qkv_0, "mirror"), (totals, "mirror"), (feed0, "after"), (qkv_1, "mirror")]
    pin, landed = exchange(steps, pin)
    (down_out,) = down0.finish(0, down_places, down_shapes, place, down_out, deps=(pin,))
    pin, landed = exchange([(qkv_0, "after"), (qkv_1, "after")], down_out)
    totals = totals.done()[: LAYERS * (8 + SHARDS)].reshape(LAYERS, 8 + SHARDS, width)
    out_out, up_out = feed0.finish(0, feed_places, feed_shapes, place, feed_out, deps=(pin,))
    qkv_out = qkv_1.finish(1, qkv_places, qkv_shapes, place, deps=(out_out,))
    query_out, key_out, value_out = qkv_0.finish(0, qkv_places, qkv_shapes, place, qkv_out)

    own_vectors = lax.dynamic_slice_in_dim(totals[:, :8], shard * share, share, axis=2)
    own_up = lax.dynamic_slice_in_dim(
        totals[:, 8:].reshape(LAYERS, SHARDS * width), shard * width, width, axis=1
    )
    vector = [own_vectors[:, index] for index in range(8)]
    return (
        output,
        input_grad,
        vector[0],
        vector[1],
        query_out,
        vector[2],
        key_out,
        value_out,
        vector[3],
        out_out,
        vector[4],
        vector[5],
        vector[6],
        up_out,
        own_up,
        down_out,
        vector[7],
    )


def solution(mesh):
    groups = mesh.shape["rep"]
    finer = Mesh(mesh.devices.reshape(groups // 2, 2, 2, 2), ("z", "y", "x", "core"))
    rep, shard = ("z", "y"), ("x", "core")
    rows = P(rep, shard, None)
    vector, matrix = P(None, shard), P(None, shard, None)
    parameters = (
        vector,
        vector,
        matrix,
        vector,
        matrix,
        matrix,
        vector,
        matrix,
        vector,
        vector,
        vector,
        matrix,
        vector,
        matrix,
        vector,
    )
    return jax.shard_map(
        body,
        mesh=finer,
        in_specs=(rows, rows) + parameters,
        out_specs=(rows, rows) + parameters,
        check_vma=False,
    )
```

```python
import functools

import jax
import jax.numpy as jnp
from jax import lax
from jax.experimental import pallas as pl
from jax.experimental.pallas import tpu as pltpu
from jax.sharding import Mesh
from jax.sharding import PartitionSpec as P

HEAD = 64
LAYERS = 2
SHARDS = 4
EPSILON = 1e-05
SWAP = [(0, 1), (1, 0)]
F32 = jnp.float32
BF16 = jnp.bfloat16
NN = (((1,), (0,)), ((), ()))
NT = (((1,), (1,)), ((), ()))
TN = (((0,), (0,)), ((), ()))
VMEM_LIMIT = 40 * 1024 * 1024
SCALE = 0.0

QKV = ((0, slice(0, 3), 0),)
OUT = ((0, slice(0, 1), 0),)
UP = (((0, slice(1, 5), 0),), ((0, slice(1, 3), 0), (6, slice(0, 2), 2)))
DOWN = (((0, slice(5, 6), 0), (6, slice(0, 3), 1)), ((-6, slice(0, 4), 0),))


def dot(left, right, dims=NN):
    return lax.dot_general(left, right, dims, preferred_element_type=F32)


def swap(values, axis):
    return lax.ppermute(values, axis, SWAP)


def vmem_spec():
    return pl.BlockSpec(memory_space=pltpu.VMEM)


def any_spec():
    return pl.BlockSpec(memory_space=pl.ANY)


def hbm_spec():
    return pl.BlockSpec(memory_space=pltpu.HBM)


def smem_spec():
    return pl.BlockSpec(memory_space=pltpu.SMEM)


def cost(flops, bytes_accessed, transcendentals=0):
    return pl.CostEstimate(
        flops=int(SCALE * flops), bytes_accessed=int(SCALE * bytes_accessed), transcendentals=0
    )


def shaped(shape, dtype):
    return jax.ShapeDtypeStruct(shape, dtype)


def call(kernel, operands, in_specs, out_shape, out_specs, deps=(), **options):
    def placed(array, spec):
        if spec.memory_space == pltpu.HBM:
            return pltpu.with_memory_space_constraint(array, pltpu.HBM)
        return array

    def result(shape, spec):
        return pltpu.HBM(shape.shape, shape.dtype) if spec.memory_space == pltpu.HBM else shape

    if isinstance(out_shape, tuple):
        out_shape = tuple(map(result, out_shape, out_specs))
    if deps:
        operands = [after(operands[0], *deps), *operands[1:]]
    return pl.pallas_call(
        kernel,
        in_specs=list(in_specs),
        out_shape=out_shape,
        out_specs=out_specs,
        compiler_params=pltpu.CompilerParams(vmem_limit_bytes=VMEM_LIMIT),
        **options,
    )(*map(placed, operands, in_specs))


def after(values, *deps):
    if isinstance(values, tuple):
        return lax.optimization_barrier(values + deps)[: len(values)]
    return lax.optimization_barrier((values,) + deps)[0]


def standardize(values):
    average = jnp.mean(values, axis=-1, keepdims=True)
    centered = values - average
    variance = jnp.mean(centered * centered, axis=-1, keepdims=True)
    inverse_scale = lax.rsqrt(variance + EPSILON)
    return centered * inverse_scale, inverse_scale


def norm_input_grad(grad_out, standard, inverse_scale, gain):
    grad_standard = grad_out * gain
    return inverse_scale * (
        grad_standard
        - jnp.mean(grad_standard, axis=-1, keepdims=True)
        - standard * jnp.mean(grad_standard * standard, axis=-1, keepdims=True)
    )


def column_sum(values):
    return jnp.sum(values.astype(F32), axis=0, keepdims=True)


def gelu_parts(hidden):
    density = jnp.exp(-0.5 * hidden * hidden)
    t = 1.0 / (1.0 + (0.3275911 * 0.7071067811865476) * jnp.abs(hidden))
    series = t * (
        0.127414796
        + t * (-0.142248368 + t * (0.7107068705 + t * (-0.7265760135 + t * 0.5307027145)))
    )
    tail = series * density
    phi = jnp.where(hidden >= 0.0, 1.0 - tail, tail)
    return hidden * phi, phi + (hidden * 0.3989422804014327) * density


def pieces_of(place_ref, refs):
    s, y = place_ref[0], place_ref[1]
    places = ((s, None), (s ^ 1, None), (s ^ 2, y), (s ^ 2, 1 - y), (s ^ 3, y), (s ^ 3, 1 - y))
    return [(ref, *place) for ref, place in zip(refs, places)]


def aligned(start, size):
    return pl.ds(start if isinstance(start, int) else pl.multiple_of(start, size), size)


def load_rows(refs, place_ref, groups, target, sems, rows):
    copies = []
    for first, blocks, block in groups:
        for piece, shard, half in pieces_of(place_ref, refs[first:]):
            start, size = shard * rows, rows
            if half is not None:
                size = rows // 2
                start = start + half * size
            place = target.at[pl.ds(block, blocks.stop - blocks.start), aligned(start, size), :]
            copies.append(pltpu.make_async_copy(piece.at[blocks], place, sems.at[len(copies)]))
    return copies


def load_down(refs, place_ref, groups, target, sems, rows):
    copies = []
    for first, blocks, block in groups:
        for piece, shard, half in pieces_of(place_ref, refs[first:]):
            at = pl.ds(shard * SHARDS + block, blocks.stop - blocks.start)
            place = target.at[at]
            if half is not None:
                size = rows // 2
                place = target.at[at, aligned(half * size, size)]
            copies.append(pltpu.make_async_copy(piece.at[blocks], place, sems.at[len(copies)]))
    return copies


def start_all(copies):
    for copy in copies:
        copy.start()


def wait_all(copies):
    for copy in copies:
        copy.wait()


def pack_kernel(jobs, outs_of, slices, place_ref, *refs):
    count = 1 + max(source for _, _, source, _, _ in jobs)
    sources, inputs, refs = refs[:count], refs[count : count + slices], refs[count + slices :]
    outs, picked, work, frames, sems = refs[: -3 - slices], refs[-3 - slices : -3], *refs[-3:]
    loads, stores = [], []
    for index, (chunk, block, source, layer, (rows, columns)) in enumerate(jobs):
        own, half = outs_of[chunk]
        size, width = outs[half].shape[1:]
        whole = sources[source].at[layer, pl.ds(rows, 2 * size), pl.ds(columns, width)]
        part = work.at[index, pl.ds(pl.multiple_of(place_ref[1] * size, size), size)]
        loads.append([pltpu.make_async_copy(whole, work.at[index], sems.at[0, index])])
        stores.append([pltpu.make_async_copy(part, outs[half].at[block], sems.at[1, index])])
        if own is not None:
            stores[-1].append(pltpu.make_async_copy(work.at[index], outs[own].at[block], sems.at[2, index]))
    for index, (source, target) in enumerate(zip(inputs, picked)):
        at = len(jobs) + index
        loads.append([pltpu.make_async_copy(source.at[1 - place_ref[2]], frames.at[index], sems.at[0, at])])
        stores.append([pltpu.make_async_copy(frames.at[index], target, sems.at[1, at])])
    for copies in loads:
        start_all(copies)
    for load, store in zip(loads, stores):
        wait_all(load)
        start_all(store)
    for copies in stores:
        wait_all(copies)


def pack_shares(place, sources, chunks, share, width, clips=(), deps=()):
    jobs = [
        (chunk, block) + place_of
        for chunk, (_, blocks) in enumerate(chunks)
        for block, place_of in enumerate(blocks)
    ]
    out_shape, outs_of = [], []
    for whole, blocks in chunks:
        outs_of.append((len(out_shape) if whole else None, len(out_shape) + whole))
        if whole:
            out_shape.append(shaped((len(blocks), share, width), BF16))
        out_shape.append(shaped((len(blocks), share // 2, width), BF16))
    out_shape += [shaped(clip.shape[1:], BF16) for clip in clips]
    count = len(jobs) + len(clips)
    return call(
        functools.partial(pack_kernel, jobs, outs_of, len(clips)),
        [place, *sources, *clips],
        [smem_spec()] + [hbm_spec()] * (len(sources) + len(clips)),
        tuple(out_shape),
        (hbm_spec(),) * len(out_shape),
        deps,
        scratch_shapes=[
            pltpu.VMEM((len(jobs), share, width), BF16),
            pltpu.VMEM((len(clips), clips[0].shape[1], width), BF16),
            pltpu.SemaphoreType.DMA((3, count)),
        ],
        cost_estimate=cost(0, 0),
        name="pack_shares",
    )


def project(layer, standard, vectors_ref, weights, queries_ref, keys_ref, values_ref, ready):
    normed = (standard * vectors_ref[layer, 0:1] + vectors_ref[layer, 1:2]).astype(BF16)
    ready()
    queries = (dot(normed, weights[0]) + vectors_ref[layer, 2:3]).astype(BF16)
    queries_ref[...] = queries * jnp.asarray(HEAD ** (-0.5), BF16)
    keys_ref[...] = dot(normed, weights[1]).astype(BF16)
    values_ref[...] = (dot(normed, weights[2]) + vectors_ref[layer, 3:4]).astype(BF16)


def first_qkv_kernel(place_ref, frames_ref, arrived_ref, vectors_ref, *refs):
    shares, (stream_ref, *outs, weights, sems) = refs[:-6], refs[-6:]
    copies = load_rows(shares, place_ref, QKV, weights, sems, weights.shape[1] // SHARDS)
    start_all(copies)
    quarter = arrived_ref.shape[0]
    stream_ref[:quarter] = frames_ref[place_ref[2]].astype(F32)
    stream_ref[quarter:] = arrived_ref[...].astype(F32)
    standard, _ = standardize(stream_ref[...])
    project(0, standard, vectors_ref, weights, *outs, lambda: wait_all(copies))


def qkv_kernel(layer, place_ref, stream_ref, vectors_ref, *refs):
    shares, (*outs, weights, sems) = refs[:-5], refs[-5:]
    copies = load_rows(shares, place_ref, QKV, weights, sems, weights.shape[1] // SHARDS)
    start_all(copies)
    standard, _ = standardize(stream_ref[...])
    project(layer, standard, vectors_ref, weights, *outs, lambda: wait_all(copies))


def qkv_options(rows, width, name):
    return dict(
        scratch_shapes=[pltpu.VMEM((3, width, width), BF16), pltpu.SemaphoreType.DMA((8,))],
        cost_estimate=cost(6 * rows * width * width, 10 * rows * width + 6 * width * width),
        name=name,
    )


def first_qkv(place, frames, arrived, vectors, shares, deps=()):
    rows, width = 2 * arrived.shape[0], arrived.shape[1]
    return call(
        first_qkv_kernel,
        [place, frames, arrived, vectors, *shares],
        [smem_spec()] + [vmem_spec()] * 3 + [hbm_spec()] * len(shares),
        (shaped((rows, width), F32),) + (shaped((rows, width), BF16),) * 3,
        (vmem_spec(),) * 4,
        deps,
        **qkv_options(rows, width, "first_qkv"),
    )


def next_qkv(layer, place, stream, vectors, shares, deps=()):
    rows, width = stream.shape
    return call(
        functools.partial(qkv_kernel, layer),
        [place, stream, vectors, *shares],
        [smem_spec()] + [vmem_spec()] * 2 + [hbm_spec()] * len(shares),
        (shaped((rows, width), BF16),) * 3,
        (vmem_spec(),) * 3,
        deps,
        **qkv_options(rows, width, "next_qkv"),
    )


def attention_kernel(q_ref, ko_ref, kt_ref, vo_ref, vt_ref, mixed_ref, lse_ref):
    queries_t = q_ref[...].T
    row = lax.broadcasted_iota(jnp.int32, queries_t.shape, 0)
    values_t = (vo_ref[...].T, vt_ref[...].T)
    outs = []
    for head in range(2):
        mine = (row >= head * HEAD) & (row < (head + 1) * HEAD)
        q_t = jnp.where(mine, queries_t, jnp.zeros_like(queries_t))
        scores = (dot(ko_ref[...], q_t), dot(kt_ref[...], q_t))
        peak = jnp.maximum(
            jnp.max(scores[0], axis=0, keepdims=True), jnp.max(scores[1], axis=0, keepdims=True)
        )
        weights = tuple(jnp.exp(part - peak) for part in scores)
        total = jnp.sum(weights[0], axis=0, keepdims=True) + jnp.sum(weights[1], axis=0, keepdims=True)
        lse_ref[0, head : head + 1, :] = peak + jnp.log(total)
        at = slice(head * HEAD, (head + 1) * HEAD)
        out = dot(values_t[0][at], weights[0].astype(BF16)) + dot(values_t[1][at], weights[1].astype(BF16))
        outs.append(out / total)
    mixed_ref[...] = jnp.concatenate(outs, axis=0).T.astype(BF16)


def attend(queries, keys, keys_twin, values, values_twin, deps=()):
    rows, width = queries.shape
    pairs = width // (2 * HEAD)
    block = pl.BlockSpec((rows, 2 * HEAD), lambda pair: (0, pair))
    return call(
        attention_kernel,
        [queries, keys, keys_twin, values, values_twin],
        [block] * 5,
        (shaped((rows, width), BF16), shaped((pairs, 8, rows), F32)),
        (block, pl.BlockSpec((1, 8, rows), lambda pair: (pair, 0, 0))),
        deps,
        grid=(pairs,),
        cost_estimate=cost(32 * rows * rows * width, 12 * rows * width, 4 * pairs * rows * rows),
        name="attend",
    )


def up_kernel(layer, place_ref, stream_ref, mixed_ref, vectors_ref, up_bias_ref, *refs):
    shares, (attended_ref, activated_ref, slope_ref, out_w, up_w, sems) = refs[:-6], refs[-6:]
    width = stream_ref.shape[1]
    share = width // SHARDS
    out_copies = load_rows(shares, place_ref, OUT, out_w, sems.at[0], share)
    up_copies = load_rows(shares, place_ref, UP[layer], up_w, sems.at[1], share)
    start_all(out_copies)
    start_all(up_copies)
    wait_all(out_copies)
    attended_ref[...] = stream_ref[...] + dot(mixed_ref[...], out_w[0]) + vectors_ref[layer, 4:5]
    standard, _ = standardize(attended_ref[...])
    second = (standard * vectors_ref[layer, 5:6] + vectors_ref[layer, 6:7]).astype(BF16)
    wait_all(up_copies)
    for block in range(SHARDS):
        at = slice(block * width, (block + 1) * width)
        hidden = dot(second, up_w[block]) + up_bias_ref[layer : layer + 1, at]
        activated, slope = gelu_parts(hidden)
        activated_ref[:, at] = activated.astype(BF16)
        slope_ref[:, at] = slope.astype(BF16)


def feed_up(layer, place, stream, mixed, vectors, up_bias, shares, deps=()):
    rows, width = stream.shape
    wide = SHARDS * width
    return call(
        functools.partial(up_kernel, layer),
        [place, stream, mixed, vectors, up_bias, *shares],
        [smem_spec()] + [vmem_spec()] * 4 + [hbm_spec()] * len(shares),
        (shaped((rows, width), F32), shaped((rows, wide), BF16), shaped((rows, wide), BF16)),
        (vmem_spec(),) * 3,
        deps,
        scratch_shapes=[
            pltpu.VMEM((1, width, width), BF16),
            pltpu.VMEM((4, width, width), BF16),
            pltpu.SemaphoreType.DMA((2, 12)),
        ],
        cost_estimate=cost(10 * rows * width * width, 24 * rows * width + 10 * width * width, rows * wide),
        name="feed_up",
    )


def down_kernel(layer, place_ref, attended_ref, activated_ref, vectors_ref, *refs):
    shares, (next_ref, down_w, sems) = refs[:-3], refs[-3:]
    width = attended_ref.shape[1]
    copies = load_down(shares, place_ref, DOWN[layer], down_w, sems, width // SHARDS)
    start_all(copies)
    next_ref[...] = attended_ref[...] + vectors_ref[layer, 7:8]
    wait_all(copies)
    next_ref[...] += dot(activated_ref[...], down_w[...].reshape(SHARDS * width, width))


def last_down_kernel(layer, place_ref, attended_ref, activated_ref, vectors_ref, *refs):
    shares, (mine_ref, other_ref, down_w, sems) = refs[:-4], refs[-4:]
    width = attended_ref.shape[1]
    copies = load_down(shares, place_ref, DOWN[layer], down_w, sems, width // SHARDS)
    start_all(copies)
    total = attended_ref[...] + vectors_ref[layer, 7:8]
    wait_all(copies)
    total += dot(activated_ref[...], down_w[...].reshape(SHARDS * width, width))
    half = mine_ref.shape[0]
    mine_ref[...] = total[:half].astype(BF16)
    other_ref[...] = total[half:].astype(BF16)


def feed_down(layer, place, attended, activated, vectors, shares, deps=()):
    rows, width = attended.shape
    last = layer == LAYERS - 1
    return call(
        functools.partial(last_down_kernel if last else down_kernel, layer),
        [place, attended, activated, vectors, *shares],
        [smem_spec()] + [vmem_spec()] * 3 + [hbm_spec()] * len(shares),
        (shaped((rows // 2, width), BF16),) * 2 if last else shaped((rows, width), F32),
        (vmem_spec(),) * 2 if last else vmem_spec(),
        deps,
        scratch_shapes=[
            pltpu.VMEM((4 * SHARDS, width // SHARDS, width), BF16),
            pltpu.SemaphoreType.DMA((12,)),
        ],
        cost_estimate=cost(8 * rows * width * width, 16 * rows * width + 8 * width * width),
        name="feed_down",
    )


def feed_scratch(width):
    return [
        pltpu.VMEM((1, width, width), BF16),
        pltpu.VMEM((4, width, width), BF16),
        pltpu.VMEM((4 * SHARDS, width // SHARDS, width), BF16),
        pltpu.SemaphoreType.DMA((3, 12)),
    ]


def feed_back_kernel(layer, place_ref, grad_ref, slope_ref, attended_ref, vectors_ref, *refs):
    shares, refs = refs[:-9], refs[-9:]
    hidden_ref, attended_grad_ref, mixed_grad_ref, sums_ref, up_sums_ref, out_w, up_w, down_w, sems = refs
    width = grad_ref.shape[1]
    share = width // SHARDS
    down_copies = load_down(shares, place_ref, DOWN[layer], down_w, sems.at[2], share)
    up_copies = load_rows(shares, place_ref, UP[layer], up_w, sems.at[1], share)
    out_copies = load_rows(shares, place_ref, OUT, out_w, sems.at[0], share)
    start_all(down_copies)
    start_all(up_copies)
    start_all(out_copies)
    branch = grad_ref[...].astype(BF16)
    sums_ref[...] = jnp.zeros_like(sums_ref)
    sums_ref[7:8] = column_sum(branch)
    wait_all(down_copies)
    wait_all(up_copies)
    second_grad = None
    for block in range(SHARDS):
        at = slice(block * width, (block + 1) * width)
        down = down_w[block * SHARDS : (block + 1) * SHARDS].reshape(width, width)
        hidden_grad = (dot(branch, down, NT) * slope_ref[:, at].astype(F32)).astype(BF16)
        hidden_ref[:, at] = hidden_grad
        up_sums_ref[:, at] = column_sum(hidden_grad)
        part = dot(hidden_grad, up_w[block], NT)
        second_grad = part if second_grad is None else second_grad + part
    standard, inverse = standardize(attended_ref[...])
    sums_ref[5:6] = column_sum(second_grad * standard)
    sums_ref[6:7] = column_sum(second_grad)
    attended_grad = grad_ref[...] + norm_input_grad(second_grad, standard, inverse, vectors_ref[layer, 5:6])
    attended_grad_ref[...] = attended_grad
    out_grad = attended_grad.astype(BF16)
    sums_ref[4:5] = column_sum(out_grad)
    wait_all(out_copies)
    mixed_grad_ref[...] = dot(out_grad, out_w[0], NT).astype(BF16)


def feed_back(layer, place, grad, slope, attended, vectors, shares, deps=()):
    rows, width = grad.shape
    wide = SHARDS * width
    return call(
        functools.partial(feed_back_kernel, layer),
        [place, grad, slope, attended, vectors, *shares],
        [smem_spec()] + [vmem_spec()] * 4 + [hbm_spec()] * len(shares),
        (
            shaped((rows, wide), BF16),
            shaped((rows, width), F32),
            shaped((rows, width), BF16),
            shaped((8, width), F32),
            shaped((1, wide), F32),
        ),
        (vmem_spec(),) * 5,
        deps,
        scratch_shapes=feed_scratch(width),
        cost_estimate=cost(18 * rows * width * width, 30 * rows * width + 18 * width * width),
        name="feed_back",
    )


def owners(place_ref, keep_ref, send_refs):
    s = place_ref[0]
    return (
        (s ^ 3, send_refs[2:]),
        (s ^ 1, send_refs[:2]),
        (s ^ 2, (keep_ref.at[1, 0], keep_ref.at[1, 1])),
        (s, (keep_ref.at[0, 0], keep_ref.at[0, 1])),
    )


def quarters(place_ref, split, rows):
    size = rows // 4
    near, inner = (place_ref[1], place_ref[3]) if split else (0, 0)
    for y in range(2):
        for z in range(2):
            start = (near ^ y) * (2 * size) + (inner ^ z) * size
            yield y, z, pl.ds(pl.multiple_of(start, size), size)


def run_steps(steps, work, sems):
    pending = [None, None]
    for index, (make, targets) in enumerate(steps):
        slot = index % 2
        if pending[slot] is not None:
            wait_all(pending[slot])
        work[slot] = make().astype(BF16).reshape(work.shape[1:])
        copies = [
            pltpu.make_async_copy(source, target, sems.at[slot, number])
            for number, (source, target) in enumerate(targets(work.at[slot]))
        ]
        start_all(copies)
        pending[slot] = copies
    for copies in pending:
        if copies is not None:
            wait_all(copies)


def by_rows(place_ref, split, keep_ref, send_refs, block):
    def targets(work):
        return [
            (work.at[shard, rows], target[y].at[z, block])
            for shard, target in owners(place_ref, keep_ref, send_refs)
            for y, z, rows in quarters(place_ref, split, work.shape[1])
        ]

    return targets


def whole_share(place_ref, split, target):
    def targets(work):
        return [
            (work.at[:, rows], target[y].at[z]) for y, z, rows in quarters(place_ref, split, work.shape[1])
        ]

    return targets


def down_grad_kernel(split, place_ref, activated_ref, grad_ref, keep_ref, *refs):
    send_refs, (work, sems) = refs[:4], refs[4:]
    width = grad_ref.shape[1]
    branch = grad_ref[...].astype(BF16)
    steps = []
    for shard, target in owners(place_ref, keep_ref, send_refs):
        at = pl.ds(pl.multiple_of(shard * width, width), width)
        steps.append(
            (lambda at=at: dot(activated_ref[:, at], branch, TN), whole_share(place_ref, split, target))
        )
    run_steps(steps, work, sems)


def grad_shapes(count, width):
    part = (2, count, width // SHARDS // 4, width)
    return (shaped((2, 2) + part, BF16),) + (shaped(part, BF16),) * 4


def grad_scratch(width):
    return [pltpu.VMEM((2, SHARDS, width // SHARDS, width), BF16), pltpu.SemaphoreType.DMA((2, 16))]


def down_weight_grad(place, split, activated, grad, deps=()):
    rows, width = grad.shape
    return call(
        functools.partial(down_grad_kernel, split),
        [place, activated, grad],
        [smem_spec()] + [vmem_spec()] * 2,
        grad_shapes(SHARDS, width),
        (hbm_spec(),) * 5,
        deps,
        scratch_shapes=grad_scratch(width),
        cost_estimate=cost(8 * rows * width * width, 12 * rows * width + 8 * width * width),
        name="down_weight_grad",
    )


def feed_grad_kernel(
    layer,
    split,
    place_ref,
    hidden_ref,
    attended_ref,
    attended_grad_ref,
    mixed_ref,
    vectors_ref,
    keep_ref,
    *refs,
):
    send_refs, (work, sems) = refs[:4], refs[4:]
    width = attended_ref.shape[1]
    standard, _ = standardize(attended_ref[...])
    second_t = (standard * vectors_ref[layer, 5:6] + vectors_ref[layer, 6:7]).astype(BF16).T
    steps = [
        (
            lambda: dot(mixed_ref[...], attended_grad_ref[...].astype(BF16), TN),
            by_rows(place_ref, split, keep_ref, send_refs, 0),
        )
    ]
    for block in range(SHARDS):
        at = slice(block * width, (block + 1) * width)
        steps.append(
            (lambda at=at: dot(second_t, hidden_ref[:, at]), by_rows(place_ref, split, keep_ref, send_refs, 1 + block))
        )
    run_steps(steps, work, sems)


def feed_weight_grads(layer, split, place, hidden_grad, attended, attended_grad, mixed, vectors, deps=()):
    rows, width = attended.shape
    return call(
        functools.partial(feed_grad_kernel, layer, split),
        [place, hidden_grad, attended, attended_grad, mixed, vectors],
        [smem_spec()] + [vmem_spec()] * 5,
        grad_shapes(1 + SHARDS, width),
        (hbm_spec(),) * 5,
        deps,
        scratch_shapes=grad_scratch(width),
        cost_estimate=cost(10 * rows * width * width, 20 * rows * width + 10 * width * width),
        name="feed_weight_grads",
    )


def qkv_grad_kernel(
    layer,
    split,
    place_ref,
    stream_ref,
    vectors_ref,
    dq_ref,
    dk_ref,
    dv_ref,
    dk_back_ref,
    dv_back_ref,
    sums_ref,
    total_ref,
    keep_ref,
    *refs,
):
    send_refs, (work, sems) = refs[:4], refs[4:]
    standard, _ = standardize(stream_ref[...])
    normed_t = (standard * vectors_ref[layer, 0:1] + vectors_ref[layer, 1:2]).astype(BF16).T
    total_ref[0] = (dk_ref[...].astype(F32) + dk_back_ref[...].astype(F32)).astype(BF16)
    total_ref[1] = (dv_ref[...].astype(F32) + dv_back_ref[...].astype(F32)).astype(BF16)
    sums_ref[...] = jnp.zeros_like(sums_ref)
    sums_ref[2:3] = column_sum(dq_ref[...])
    sums_ref[3:4] = column_sum(total_ref[1])
    makers = (
        lambda: dot(normed_t, dq_ref[...]),
        lambda: dot(normed_t, total_ref[0]),
        lambda: dot(normed_t, total_ref[1]),
    )
    run_steps(
        [(make, by_rows(place_ref, split, keep_ref, send_refs, block)) for block, make in enumerate(makers)],
        work,
        sems,
    )


def qkv_weight_grads(layer, split, place, stream, vectors, dq, dk, dv, dk_back, dv_back, deps=()):
    rows, width = stream.shape
    return call(
        functools.partial(qkv_grad_kernel, layer, split),
        [place, stream, vectors, dq, dk, dv, dk_back, dv_back],
        [smem_spec()] + [vmem_spec()] * 7,
        (shaped((8, width), F32), shaped((2, rows, width), BF16)) + grad_shapes(3, width),
        (vmem_spec(),) * 2 + (hbm_spec(),) * 5,
        deps,
        scratch_shapes=grad_scratch(width),
        cost_estimate=cost(6 * rows * width * width, 10 * rows * width + 6 * width * width),
        name="qkv_weight_grads",
    )


def attention_back_kernel(
    q_ref,
    ko_ref,
    kt_ref,
    vo_ref,
    vt_ref,
    lse_ref,
    out_grad_ref,
    dq_ref,
    dk_ref,
    dv_ref,
    dk_twin_ref,
    dv_twin_ref,
):
    queries = q_ref[...]
    out_grad = out_grad_ref[...]
    queries_t, out_grad_t = queries.T, out_grad.T
    row = lax.broadcasted_iota(jnp.int32, queries_t.shape, 0)
    lane = lax.broadcasted_iota(jnp.int32, queries.shape, 1)
    keys, values = (ko_ref, kt_ref), (vo_ref, vt_ref)
    keys_t = tuple(part[...].T for part in keys)
    key_grads, value_grads, query_grads = [None, None], [None, None], []
    for head in range(2):
        low, high = head * HEAD, (head + 1) * HEAD
        mine_t = (row >= low) & (row < high)
        mine = (lane >= low) & (lane < high)
        q_t = jnp.where(mine_t, queries_t, jnp.zeros_like(queries_t))
        o_t = jnp.where(mine_t, out_grad_t, jnp.zeros_like(queries_t))
        q_h = jnp.where(mine, queries, jnp.zeros_like(queries))
        o_h = jnp.where(mine, out_grad, jnp.zeros_like(queries))
        lse = lse_ref[0, head : head + 1, :]
        probability = [jnp.exp(dot(part[...], q_t) - lse) for part in keys]
        probability_grad = [dot(part[...], o_t) for part in values]
        inner = sum(
            jnp.sum(left * right, axis=0, keepdims=True)
            for left, right in zip(probability, probability_grad)
        )
        query_grad = None
        for index in range(2):
            score_grad = (probability[index] * (probability_grad[index] - inner)).astype(BF16)
            value_part = dot(probability[index].astype(BF16), o_h)
            key_part = dot(score_grad, q_h)
            query_part = dot(keys_t[index][low:high], score_grad)
            if head == 0:
                key_grads[index], value_grads[index] = key_part, value_part
            else:
                key_grads[index] += key_part
                value_grads[index] += value_part
            query_grad = query_part if index == 0 else query_grad + query_part
        query_grads.append(query_grad)
    dq_ref[...] = (jnp.concatenate(query_grads, axis=0).T * HEAD ** (-0.5)).astype(BF16)
    for ref, value in zip((dk_ref, dk_twin_ref, dv_ref, dv_twin_ref), key_grads + value_grads):
        ref[...] = value.astype(BF16)


def attend_back(queries, keys, keys_twin, values, values_twin, lse, out_grad, deps=()):
    rows, width = queries.shape
    pairs = width // (2 * HEAD)
    block = pl.BlockSpec((rows, 2 * HEAD), lambda pair: (0, pair))
    return call(
        attention_back_kernel,
        [queries, keys, keys_twin, values, values_twin, lse, out_grad],
        [block] * 5 + [pl.BlockSpec((1, 8, rows), lambda pair: (pair, 0, 0)), block],
        (shaped((rows, width), BF16),) * 5,
        (block,) * 5,
        deps,
        grid=(pairs,),
        cost_estimate=cost(80 * rows * rows * width, 24 * rows * width),
        name="attend_back",
    )


def norm_back_kernel(layer, place_ref, stream_ref, vectors_ref, attended_grad_ref, dq_ref, dkv_ref, *refs):
    shares, (grad_ref, sums_ref, weights, sems) = refs[:-4], refs[-4:]
    copies = load_rows(shares, place_ref, QKV, weights, sems, weights.shape[1] // SHARDS)
    start_all(copies)
    standard, inverse = standardize(stream_ref[...])
    wait_all(copies)
    normed_grad = (
        dot(dq_ref[...], weights[0], NT) + dot(dkv_ref[0], weights[1], NT) + dot(dkv_ref[1], weights[2], NT)
    )
    sums_ref[...] = jnp.zeros_like(sums_ref)
    sums_ref[0:1] = column_sum(normed_grad * standard)
    sums_ref[1:2] = column_sum(normed_grad)
    grad_ref[...] = attended_grad_ref[...] + norm_input_grad(
        normed_grad, standard, inverse, vectors_ref[layer, 0:1]
    )


def norm_back(layer, place, stream, vectors, attended_grad, dq, dkv, shares, deps=()):
    rows, width = stream.shape
    return call(
        functools.partial(norm_back_kernel, layer),
        [place, stream, vectors, attended_grad, dq, dkv, *shares],
        [smem_spec()] + [vmem_spec()] * 5 + [hbm_spec()] * len(shares),
        (shaped((rows, width), F32), shaped((8, width), F32)),
        (vmem_spec(),) * 2,
        deps,
        scratch_shapes=[pltpu.VMEM((3, width, width), BF16), pltpu.SemaphoreType.DMA((8,))],
        cost_estimate=cost(6 * rows * width * width, 18 * rows * width + 6 * width * width),
        name="norm_back",
    )


def finish_kernel(layer, split, pieces, places, place_ref, *refs):
    sources, refs = refs[: len(pieces)], refs[len(pieces) :]
    outs, (arrived, work, sems) = refs[:-3], refs[-3:]
    count = len(places)
    near, inner = (place_ref[1], place_ref[3]) if split else (0, 0)
    size, width = work.shape[1:]
    loads = []
    for index, (source, (start, _, _)) in enumerate(zip(sources, pieces)):
        at = pl.ds(index * count, count)
        loads.append(pltpu.make_async_copy(source.at[pl.ds(start, count)], arrived.at[at], sems.at[0, index]))
    start_all(loads)
    stores = []
    for number, (load, (_, y, z)) in enumerate(zip(loads, pieces)):
        load.wait()
        for block, (out, row, column) in enumerate(places):
            index = number * count + block
            work[index] = arrived[index].astype(F32)
            start = row + (near ^ y) * (2 * size) + (inner ^ z) * size
            target = outs[out].at[layer, aligned(start, size), pl.ds(column, width)]
            stores.append(pltpu.make_async_copy(work.at[index], target, sems.at[1, index]))
            stores[-1].start()
    wait_all(stores)


def finish(layer, split, sources, places, out_shapes, place, buffers=None, deps=()):
    size, width = sources[0][0].shape[-2:]
    count = 4 * len(places)
    operands = [place, *(source[0] for source in sources)]
    aliases = {}
    if buffers is not None:
        aliases = {len(operands) + index: index for index in range(len(buffers))}
        operands += list(buffers)
    first = 1 + len(sources)
    pieces = [source[1:] for source in sources]

    def kernel(*refs):
        finish_kernel(layer, split, pieces, places, *refs[:first], *refs[len(operands) :])

    return call(
        kernel,
        operands,
        [smem_spec()] + [hbm_spec()] * (len(operands) - 1),
        tuple(shaped(shape, F32) for shape in out_shapes),
        (hbm_spec(),) * len(out_shapes),
        deps,
        input_output_aliases=aliases,
        scratch_shapes=[
            pltpu.VMEM((count, size, width), BF16),
            pltpu.VMEM((count, size, width), F32),
            pltpu.SemaphoreType.DMA((2, count)),
        ],
        cost_estimate=cost(0, 6 * count * size * width),
        name="finish",
    )


def combine_kernel(plan, *refs):
    arrays = 1 + max(operand for segments in plan for _, terms in segments for operand, _ in terms)
    operands, outs, (work, sems, out_sems) = refs[:arrays], refs[arrays:-3], refs[-3:]
    jobs, copies, at = [], [], 0
    for out, segments in zip(outs, plan):
        place = 0
        for count, terms in segments:
            places = []
            for operand, start in terms:
                source = operands[operand].at[pl.ds(start, count)]
                copies.append(
                    pltpu.make_async_copy(source, work.at[pl.ds(at, count)], sems.at[len(copies)])
                )
                places.append((copies[-1], at))
                at += count
            jobs.append((out, place, count, places))
            place += count
    start_all(copies)
    stores = []
    for out, place, count, places in jobs:
        for copy, _ in places:
            copy.wait()
        first = places[0][1]
        if len(places) == 2:
            for index in range(count):
                work[first + index] += work[places[1][1] + index]
        elif len(places) > 2:
            for index in range(count):
                total = work[first + index].astype(F32)
                for _, start in places[1:]:
                    total += work[start + index].astype(F32)
                work[first + index] = total.astype(BF16)
        stores.append(
            pltpu.make_async_copy(
                work.at[pl.ds(first, count)], out.at[pl.ds(place, count)], out_sems.at[len(stores)]
            )
        )
        stores[-1].start()
    wait_all(stores)


def combine(outputs, deps=()):
    arrays, plan = [], []
    for segments in outputs:
        plan.append([])
        for count, terms in segments:
            named = []
            for array, start in terms:
                index = next((i for i, known in enumerate(arrays) if known is array), len(arrays))
                if index == len(arrays):
                    arrays.append(array)
                named.append((index, start))
            plan[-1].append((count, named))
    size, width = arrays[0].shape[1:]
    moves = [len(terms) for segments in plan for _, terms in segments]
    rows = sum(count * len(terms) for segments in plan for count, terms in segments)
    return call(
        functools.partial(combine_kernel, plan),
        arrays,
        [hbm_spec()] * len(arrays),
        tuple(shaped((sum(count for count, _ in segments), size, width), BF16) for segments in plan),
        (hbm_spec(),) * len(plan),
        deps,
        scratch_shapes=[
            pltpu.VMEM((rows, size, width), BF16),
            pltpu.SemaphoreType.DMA((sum(moves),)),
            pltpu.SemaphoreType.DMA((len(moves),)),
        ],
        cost_estimate=cost(0, 0),
        name="combine",
    )


PAIRS, MIRROR = [(0, 1), (1, 0), (2, 3), (3, 2)], [(0, 3), (3, 0), (1, 2), (2, 1)]


class Flow:
    def __init__(self, split, parts, *pins, last="spread"):
        keep, *send = parts
        self.split, self.count, self.last = split, keep.shape[3], last
        self.keep = keep.reshape((-1,) + keep.shape[-2:])
        send = after(tuple(send), *pins)
        self.back = [swap(part.reshape((-1,) + part.shape[-2:]), "core") for part in send]

    def sums(self, x, y, z, *arrivals):
        n = self.count
        terms = [(self.keep, (4 * x + 2 * y + z) * n), (self.back[2 * x + y], z * n)]
        return (n, terms + [(array, start + offset * n) for (array, start), offset in arrivals])

    def segments(self, stage):
        n = self.count
        if stage == "x":
            return {"x": [self.sums(1, y, z) for y in range(2) for z in range(2)]}
        if stage == "y":
            return {"y": [self.sums(0, 1, z, (self.x, 2 + z)) for z in range(2)]}
        if stage == "pair":
            if not self.split:
                return {"sum": [self.sums(0, 0, z, (self.x, z), (self.y, z)) for z in range(2)]}
            return {"pair": [self.sums(0, 0, 1, (self.x, 1), (self.y, 1))]}
        if stage == "mirror":
            if not self.split:
                return {}
            return {"mirror": [self.sums(0, 0, 0, (self.x, 0), (self.y, 0), (self.pair, 0))]}
        if stage == "after":
            if not self.split:
                return {"near": [(2 * n, [self.sum])]}
            whole = (n, [self.mirror_sent, self.mirror])
            return {channel: [whole] for channel in ("near", "spread", "diagonal")[: 3 if self.last is None else 2]}
        if not self.split or self.last is None:
            return {}
        return {self.last: [(n, [self.rest if self.last == "spread" else self.part_z])]}

    def record(self, stage, channel, sent, arrived):
        if stage == "after":
            if channel == "near":
                self.part, self.rest = sent, arrived
            elif channel == "spread":
                self.part_z = arrived
            else:
                self.rest_z = arrived
        elif stage == "last":
            self.rest_z = arrived
        else:
            setattr(self, channel, arrived)
            setattr(self, channel + "_sent", sent)

    def finish(self, layer, places, out_shapes, place, buffers=None, deps=()):
        n = self.count
        if self.split:
            sources = [(*self.part, 0, 0), (*self.part_z, 0, 1), (*self.rest, 1, 0), (*self.rest_z, 1, 1)]
        else:
            sources = [
                (array, start + z * n, y, z)
                for y, (array, start) in enumerate((self.part, self.rest))
                for z in range(2)
            ]
        return finish(layer, self.split, sources, places, out_shapes, place, buffers, deps)


class Totals:
    def __init__(self, split, values):
        self.split = split
        self.terms = [(values, 0), (swap(values, "core"), 0)]

    def segments(self, stage):
        if stage in ("pair", "mirror") and not self.split:
            return {"sum": [(1, self.terms)]} if stage == "pair" else {}
        return {stage: [(1, self.terms)]}

    def record(self, stage, channel, sent, arrived):
        self.terms = [arrived] if channel == "sum" else [sent, arrived]

    def done(self):
        return sum(array[start].astype(F32) for array, start in self.terms)


def exchange(steps, *pins):
    outputs, owners_of = {}, {}
    for flow, stage in steps:
        for channel, segments in flow.segments(stage).items():
            placed = outputs.setdefault(channel, [])
            start = sum(count for count, _ in placed)
            owners_of.setdefault(channel, []).append((flow, stage, start))
            placed += segments
    if not outputs:
        return pins[0], ()
    names, landed = list(outputs), []
    results = combine([outputs[name] for name in names], pins)
    for name, sent in zip(names, results):
        if name == "sum":
            arrived = lax.psum(sent, "z")
        elif name == "diagonal":
            both = [(2 * left + y, 2 * right + 1 - y) for left, right in PAIRS for y in range(2)]
            arrived = lax.ppermute(sent, ("z", "y"), both)
        elif name in ("pair", "spread", "mirror"):
            arrived = lax.ppermute(sent, "z", MIRROR if name == "mirror" else PAIRS)
        else:
            arrived = swap(sent, "y" if name == "near" else name)
        landed.append(arrived)
        for flow, stage, start in owners_of[name]:
            flow.record(stage, name, (sent, start), (arrived, start))
    return results[0], tuple(landed)


def body(
    frames,
    cotangent,
    first_gain,
    first_shift,
    query_weight,
    query_bias,
    key_weight,
    value_weight,
    value_bias,
    out_weight,
    out_bias,
    second_gain,
    second_shift,
    up_weight,
    up_bias,
    down_weight,
    down_bias,
):
    x, y, z, core = (lax.axis_index(axis) for axis in ("x", "y", "z", "core"))
    shard = 2 * x + core
    inner = jnp.where((z == 0) | (z == 3), 0, 1)
    place = jnp.stack([shard, y, x, inner]).astype(jnp.int32)
    quarter, width = frames.shape[1:]
    share = width // SHARDS
    split = lax.axis_size("z") == 4

    def blocks_of(layer):
        attention = [(source, layer, (0, 0)) for source in (0, 1, 2)]
        up = [(3, layer, (0, 0))] + [(4, layer, (0, block * width)) for block in range(SHARDS)]
        down = [(5, layer, (block * share, 0)) for block in range(SHARDS)]
        return attention, up, down

    sources = (query_weight, key_weight, value_weight, out_weight, up_weight, down_weight)
    (attention0, up0, down0), (attention1, up1, down1) = blocks_of(0), blocks_of(1)
    own0, half0, other_frames = pack_shares(
        place, sources[:3], [(True, attention0)], share, width, clips=(frames,)
    )
    near = {0: swap(half0, "x")}
    arrived_frames = swap(other_frames, "x")
    twin = {0: swap(own0, "core")}
    *packed, other_cotangent = pack_shares(
        place,
        sources,
        [
            (True, blocks)
            for blocks in (up0 + down0[:1], down0[1:], attention1, up1[:3], up1[3:], down1)
        ],
        share,
        width,
        clips=(cotangent,),
        deps=(half0,),
    )
    own, half = dict(enumerate([own0, *packed[0::2]])), dict(enumerate([half0, *packed[1::2]]))
    near[0] = after(near[0], half[1])
    far, near_twin, far_twin = {0: swap(near[0], "y")}, {0: swap(near[0], "core")}, {}

    small = jnp.stack(
        [first_gain, first_shift, query_bias, value_bias, out_bias, second_gain, second_shift, down_bias], axis=1
    )
    small = jnp.concatenate([small, up_bias.reshape(LAYERS, SHARDS, share)], axis=1)
    small = after(small, half0)
    pair = jnp.stack([small, swap(small, "core")])
    pieces = jnp.concatenate([pair, swap(pair, "x")], axis=0)
    small = jnp.stack(
        [lax.dynamic_index_in_dim(pieces, shard ^ index, 0, keepdims=False) for index in range(SHARDS)]
    ).astype(F32)
    vectors = jnp.transpose(small[:, :, :8], (1, 2, 0, 3)).reshape(LAYERS, 8, width)
    up_biases = jnp.transpose(small[:, :, 8:], (1, 0, 2, 3)).reshape(LAYERS, SHARDS * width)

    def fetch(chunk, *pins):
        near[chunk] = swap(after(half[chunk], *pins), "x")

    def spread(chunk, *pins):
        far[chunk] = swap(after(near[chunk], *pins), "y")

    def trade(chunk, *pins):
        twin[chunk] = swap(after(own[chunk], *pins), "core")

    def trade_near(chunk, *pins):
        near_twin[chunk] = swap(after(near[chunk], *pins), "core")

    def trade_far(chunk, *pins):
        far_twin[chunk] = swap(after(far[chunk], *pins), "core")

    def shares(chunk):
        return own[chunk], twin[chunk], near[chunk], far[chunk], near_twin[chunk], far_twin[chunk]

    trade_far(0)
    fetch(1, arrived_frames)
    for chunk in range(1, 7):
        trade(chunk, arrived_frames)
    stream0, queries0, keys0, values0 = first_qkv(
        place, frames, arrived_frames, vectors, shares(0), deps=tuple(twin[chunk] for chunk in range(1, 7))
    )
    qkv0 = shares(0)
    keys0, values0 = after((keys0, values0), near[1])
    keys_twin0, values_twin0 = swap(keys0, "core"), swap(values0, "core")
    fetch(2, keys0)
    spread(1, keys0)
    trade_near(1, keys0)
    mixed0, lse0 = attend(queries0, keys0, keys_twin0, values0, values_twin0, deps=(near_twin[1],))
    trade_far(1, mixed0)
    fetch(3, near[2], mixed0)
    spread(2, mixed0)
    trade_near(2, mixed0)
    attended0, activated0, slope0 = feed_up(
        0, place, stream0, mixed0, vectors, up_biases, shares(1), deps=(near_twin[2],)
    )
    trade_far(2, activated0)
    fetch(4, near[3], activated0)
    spread(3, activated0)
    trade_near(3, activated0)
    second0 = shares(1) + shares(2)
    stream1 = feed_down(0, place, attended0, activated0, vectors, second0, deps=(near_twin[3],))
    trade_far(3, stream1)
    fetch(5, near[4], stream1)
    spread(4, stream1)
    trade_near(4, stream1)
    qkv1 = shares(3)
    queries1, keys1, values1 = next_qkv(1, place, stream1, vectors, qkv1, deps=(near_twin[4],))
    keys1, values1 = after((keys1, values1), near[5], far[4])
    keys_twin1, values_twin1 = swap(keys1, "core"), swap(values1, "core")
    fetch(6, near[5], keys1)
    spread(5, keys1)
    trade_near(5, keys1)
    trade_far(4, keys1)
    mixed1, lse1 = attend(
        queries1, keys1, keys_twin1, values1, values_twin1, deps=(near_twin[5], far_twin[4])
    )
    trade_far(5, mixed1)
    spread(6, mixed1)
    trade_near(6, mixed1)
    arrived_cotangent = swap(after(other_cotangent, near[6]), "x")
    late = shares(4) + shares(5)
    attended1, activated1, slope1 = feed_up(
        1, place, stream1, mixed1, vectors, up_biases, late, deps=(near_twin[6],)
    )
    mine_cotangent = lax.dynamic_index_in_dim(cotangent, x, 0, keepdims=False)
    pieces = after((mine_cotangent, arrived_cotangent), attended1)
    gradient = jnp.concatenate(pieces, axis=0).astype(F32)
    down1 = Flow(split, down_weight_grad(place, split, activated1, gradient), far[6])
    trade_far(6, down1.keep)
    output_mine, output_other = feed_down(1, place, attended1, activated1, vectors, shares(6))
    late += shares(6)

    def by_clip(mine, other):
        return jnp.where(x == 0, jnp.stack([mine, other]), jnp.stack([other, mine]))

    def square(row_blocks, column_blocks):
        return (LAYERS, row_blocks * share, column_blocks * width)

    down_places, down_shapes = [(0, block * share, 0) for block in range(SHARDS)], [square(SHARDS, 1)]
    feed_places = [(0, 0, 0)] + [(1, 0, block * width) for block in range(SHARDS)]
    feed_shapes = [square(1, 1), square(1, SHARDS)]
    qkv_places, qkv_shapes = [(block, 0, 0) for block in range(3)], [square(1, 1)] * 3

    pin, landed = exchange([(down1, "x")], output_mine, *down1.back)
    hidden_grad, attended_grad, mixed_grad, feed_sums1, up_sums1 = feed_back(
        1, place, gradient, slope1, attended1, vectors, late, deps=(pin,)
    )
    parts = feed_weight_grads(1, split, place, hidden_grad, attended1, attended_grad, mixed1, vectors)
    feed1 = Flow(split, parts)
    pin, (near, far) = exchange([(down1, "y"), (feed1, "x")], *feed1.back)
    dq, dk, dv, dk_twin, dv_twin = attend_back(
        queries1, keys1, keys_twin1, values1, values_twin1, lse1, mixed_grad, deps=(pin,)
    )
    dk_twin, dv_twin = after((dk_twin, dv_twin), near)
    dk_back, dv_back = swap(dk_twin, "core"), swap(dv_twin, "core")
    pin, landed = exchange([(down1, "pair")], dq)
    qkv_sums1, dkv, *parts = qkv_weight_grads(
        1, split, place, stream1, vectors, dq, dk, dv, dk_back, dv_back, deps=(pin,)
    )
    gradient, norm_sums1 = norm_back(
        1, place, stream1, vectors, attended_grad, dq, dkv, qkv1, deps=(parts[0],)
    )
    qkv_1 = Flow(split, parts, far, *landed, last=None)
    pin, landed = exchange([(qkv_1, "x"), (feed1, "y"), (down1, "mirror")], gradient, *qkv_1.back)

    parts = down_weight_grad(place, split, activated0, gradient, deps=(pin,))
    hidden_grad, attended_grad, mixed_grad, feed_sums0, up_sums0 = feed_back(
        0, place, gradient, slope0, attended0, vectors, second0, deps=(parts[0],)
    )
    down0 = Flow(split, parts, mixed_grad, *landed, last="near")
    steps = [(down0, "x"), (qkv_1, "y"), (down1, "after"), (feed1, "pair")]
    pin, landed = exchange(steps, mixed_grad, *down0.back)
    parts = feed_weight_grads(
        0, split, place, hidden_grad, attended0, attended_grad, mixed0, vectors, deps=(pin,)
    )
    dq, dk, dv, dk_twin, dv_twin = attend_back(
        queries0, keys0, keys_twin0, values0, values_twin0, lse0, mixed_grad, deps=(parts[0],)
    )
    dk_twin, dv_twin = after((dk_twin, dv_twin), *landed)
    dk_back, dv_back = swap(dk_twin, "core"), swap(dv_twin, "core")
    feed0 = Flow(split, parts, dq, *landed, last=None)
    steps = [(feed0, "x"), (down0, "y"), (down1, "last"), (qkv_1, "pair"), (feed1, "mirror")]
    pin, (far, *landed) = exchange(steps, dq, *feed0.back)
    qkv_sums0, dkv, *parts = qkv_weight_grads(
        0, split, place, stream0, vectors, dq, dk, dv, dk_back, dv_back, deps=(pin,)
    )
    gradient, norm_sums0 = norm_back(
        0, place, stream0, vectors, attended_grad, dq, dkv, qkv0, deps=(parts[0],)
    )
    qkv_0 = Flow(split, parts, gradient, *landed, last=None)
    sums = jnp.concatenate(
        [
            part
            for feed, qkv, norm, up in (
                (feed_sums0, qkv_sums0, norm_sums0, up_sums0),
                (feed_sums1, qkv_sums1, norm_sums1, up_sums1),
            )
            for part in (feed + qkv + norm, up.reshape(SHARDS, width))
        ]
    ).astype(BF16)
    sums = jnp.pad(sums, ((0, share // 4 - sums.shape[0]), (0, 0)))
    totals = Totals(split, sums[None])
    steps = [(qkv_0, "x"), (totals, "x"), (down0, "pair"), (feed1, "after")]
    pin, landed = exchange(steps, gradient, *qkv_0.back)
    down_out = down1.finish(1, down_places, down_shapes, place, deps=(pin,))
    pin, landed = exchange([(feed0, "y"), (down0, "mirror"), (feed1, "last")], down_out[0])
    input_other = swap(after(gradient[quarter:].astype(BF16), pin), "x")
    steps = [(qkv_0, "y"), (totals, "y"), (feed0, "pair"), (down0, "after")]
    pin, landed = exchange(steps, pin)
    output_other = swap(after(output_other, pin), "x")
    feed_out = feed1.finish(1, feed_places, feed_shapes, place, deps=(pin, input_other))
    input_grad = by_clip(gradient[:quarter], input_other.astype(F32))
    steps = [(qkv_0, "pair"), (totals, "pair"), (feed0, "mirror"), (down0, "last")]
    pin, landed = exchange(steps, feed_out[0], output_other)
    output = by_clip(output_mine, output_other)
    steps = [(qkv_0, "mirror"), (totals, "mirror"), (feed0, "after"), (qkv_1, "mirror")]
    pin, landed = exchange(steps, pin)
    (down_out,) = down0.finish(0, down_places, down_shapes, place, down_out, deps=(pin,))
    pin, landed = exchange([(qkv_0, "after"), (qkv_1, "after")], down_out)
    totals = totals.done()[: LAYERS * (8 + SHARDS)].reshape(LAYERS, 8 + SHARDS, width)
    out_out, up_out = feed0.finish(0, feed_places, feed_shapes, place, feed_out, deps=(pin,))
    qkv_out = qkv_1.finish(1, qkv_places, qkv_shapes, place, deps=(out_out,))
    query_out, key_out, value_out = qkv_0.finish(0, qkv_places, qkv_shapes, place, qkv_out)

    own_vectors = lax.dynamic_slice_in_dim(totals[:, :8], shard * share, share, axis=2)
    own_up = lax.dynamic_slice_in_dim(
        totals[:, 8:].reshape(LAYERS, SHARDS * width), shard * width, width, axis=1
    )
    vector = [own_vectors[:, index] for index in range(8)]
    return (
        output,
        input_grad,
        vector[0],
        vector[1],
        query_out,
        vector[2],
        key_out,
        value_out,
        vector[3],
        out_out,
        vector[4],
        vector[5],
        vector[6],
        up_out,
        own_up,
        down_out,
        vector[7],
    )


def solution(mesh):
    groups = mesh.shape["rep"]
    finer = Mesh(mesh.devices.reshape(groups // 2, 2, 2, 2), ("z", "y", "x", "core"))
    rep, shard = ("z", "y"), ("x", "core")
    rows = P(rep, shard, None)
    vector, matrix = P(None, shard), P(None, shard, None)
    parameters = (
        vector,
        vector,
        matrix,
        vector,
        matrix,
        matrix,
        vector,
        matrix,
        vector,
        vector,
        vector,
        matrix,
        vector,
        matrix,
        vector,
    )
    return jax.shard_map(
        body,
        mesh=finer,
        in_specs=(rows, rows) + parameters,
        out_specs=(rows, rows) + parameters,
        check_vma=False,
    )
```

```python
import functools

import jax
import jax.numpy as jnp
from jax import lax
from jax.experimental import pallas as pl
from jax.experimental.pallas import tpu as pltpu
from jax.sharding import Mesh
from jax.sharding import PartitionSpec as P

HEAD = 64
LAYERS = 2
SHARDS = 4
EPSILON = 1e-05
SWAP = [(0, 1), (1, 0)]
F32 = jnp.float32
BF16 = jnp.bfloat16
NN = (((1,), (0,)), ((), ()))
NT = (((1,), (1,)), ((), ()))
TN = (((0,), (0,)), ((), ()))
VMEM_LIMIT = 40 * 1024 * 1024
SCALE = 0.0

QKV = ((0, slice(0, 3), 0),)
OUT = ((0, slice(0, 1), 0),)
UP = (((0, slice(1, 5), 0),), ((0, slice(1, 3), 0), (6, slice(0, 2), 2)))
DOWN = (((0, slice(5, 6), 0), (6, slice(0, 3), 1)), ((-6, slice(0, 4), 0),))


def dot(left, right, dims=NN):
    return lax.dot_general(left, right, dims, preferred_element_type=F32)


def swap(values, axis):
    return lax.ppermute(values, axis, SWAP)


def vmem_spec():
    return pl.BlockSpec(memory_space=pltpu.VMEM)


def any_spec():
    return pl.BlockSpec(memory_space=pl.ANY)


def hbm_spec():
    return pl.BlockSpec(memory_space=pltpu.HBM)


def smem_spec():
    return pl.BlockSpec(memory_space=pltpu.SMEM)


def cost(flops, bytes_accessed, transcendentals=0):
    return pl.CostEstimate(
        flops=int(SCALE * flops), bytes_accessed=int(SCALE * bytes_accessed), transcendentals=0
    )


def shaped(shape, dtype):
    return jax.ShapeDtypeStruct(shape, dtype)


def call(kernel, operands, in_specs, out_shape, out_specs, deps=(), **options):
    def placed(array, spec):
        if spec.memory_space == pltpu.HBM:
            return pltpu.with_memory_space_constraint(array, pltpu.HBM)
        return array

    def result(shape, spec):
        return pltpu.HBM(shape.shape, shape.dtype) if spec.memory_space == pltpu.HBM else shape

    if isinstance(out_shape, tuple):
        out_shape = tuple(map(result, out_shape, out_specs))
    if deps:
        operands = [after(operands[0], *deps), *operands[1:]]
    return pl.pallas_call(
        kernel,
        in_specs=list(in_specs),
        out_shape=out_shape,
        out_specs=out_specs,
        compiler_params=pltpu.CompilerParams(vmem_limit_bytes=VMEM_LIMIT),
        **options,
    )(*map(placed, operands, in_specs))


def after(values, *deps):
    if isinstance(values, tuple):
        return lax.optimization_barrier(values + deps)[: len(values)]
    return lax.optimization_barrier((values,) + deps)[0]


def standardize(values):
    average = jnp.mean(values, axis=-1, keepdims=True)
    centered = values - average
    variance = jnp.mean(centered * centered, axis=-1, keepdims=True)
    inverse_scale = lax.rsqrt(variance + EPSILON)
    return centered * inverse_scale, inverse_scale


def norm_input_grad(grad_out, standard, inverse_scale, gain):
    grad_standard = grad_out * gain
    return inverse_scale * (
        grad_standard
        - jnp.mean(grad_standard, axis=-1, keepdims=True)
        - standard * jnp.mean(grad_standard * standard, axis=-1, keepdims=True)
    )


def column_sum(values):
    return jnp.sum(values.astype(F32), axis=0, keepdims=True)


def gelu_parts(hidden):
    density = jnp.exp(-0.5 * hidden * hidden)
    t = 1.0 / (1.0 + (0.3275911 * 0.7071067811865476) * jnp.abs(hidden))
    series = t * (
        0.127414796
        + t * (-0.142248368 + t * (0.7107068705 + t * (-0.7265760135 + t * 0.5307027145)))
    )
    tail = series * density
    phi = jnp.where(hidden >= 0.0, 1.0 - tail, tail)
    return hidden * phi, phi + (hidden * 0.3989422804014327) * density


def pieces_of(place_ref, refs):
    s, y = place_ref[0], place_ref[1]
    places = ((s, None), (s ^ 1, None), (s ^ 2, y), (s ^ 2, 1 - y), (s ^ 3, y), (s ^ 3, 1 - y))
    return [(ref, *place) for ref, place in zip(refs, places)]


def aligned(start, size):
    return pl.ds(start if isinstance(start, int) else pl.multiple_of(start, size), size)


def load_rows(refs, place_ref, groups, target, sems, rows):
    copies = []
    for first, blocks, block in groups:
        for piece, shard, half in pieces_of(place_ref, refs[first:]):
            start, size = shard * rows, rows
            if half is not None:
                size = rows // 2
                start = start + half * size
            place = target.at[pl.ds(block, blocks.stop - blocks.start), aligned(start, size), :]
            copies.append(pltpu.make_async_copy(piece.at[blocks], place, sems.at[len(copies)]))
    return copies


def load_down(refs, place_ref, groups, target, sems, rows):
    copies = []
    for first, blocks, block in groups:
        for piece, shard, half in pieces_of(place_ref, refs[first:]):
            at = pl.ds(shard * SHARDS + block, blocks.stop - blocks.start)
            place = target.at[at]
            if half is not None:
                size = rows // 2
                place = target.at[at, aligned(half * size, size)]
            copies.append(pltpu.make_async_copy(piece.at[blocks], place, sems.at[len(copies)]))
    return copies


def start_all(copies):
    for copy in copies:
        copy.start()


def wait_all(copies):
    for copy in copies:
        copy.wait()


def pack_kernel(jobs, outs_of, slices, place_ref, *refs):
    count = 1 + max(source for _, _, source, _, _ in jobs)
    sources, inputs, refs = refs[:count], refs[count : count + slices], refs[count + slices :]
    outs, picked, work, frames, sems = refs[: -3 - slices], refs[-3 - slices : -3], *refs[-3:]
    loads, stores = [], []
    for index, (chunk, block, source, layer, (rows, columns)) in enumerate(jobs):
        own, half = outs_of[chunk]
        size, width = outs[half].shape[1:]
        whole = sources[source].at[layer, pl.ds(rows, 2 * size), pl.ds(columns, width)]
        part = work.at[index, pl.ds(pl.multiple_of(place_ref[1] * size, size), size)]
        loads.append([pltpu.make_async_copy(whole, work.at[index], sems.at[0, index])])
        stores.append([pltpu.make_async_copy(part, outs[half].at[block], sems.at[1, index])])
        if own is not None:
            stores[-1].append(pltpu.make_async_copy(work.at[index], outs[own].at[block], sems.at[2, index]))
    for index, (source, target) in enumerate(zip(inputs, picked)):
        at = len(jobs) + index
        loads.append([pltpu.make_async_copy(source.at[1 - place_ref[2]], frames.at[index], sems.at[0, at])])
        stores.append([pltpu.make_async_copy(frames.at[index], target, sems.at[1, at])])
    for copies in loads:
        start_all(copies)
    for load, store in zip(loads, stores):
        wait_all(load)
        start_all(store)
    for copies in stores:
        wait_all(copies)


def pack_shares(place, sources, chunks, share, width, clips=(), deps=()):
    jobs = [
        (chunk, block) + place_of
        for chunk, (_, blocks) in enumerate(chunks)
        for block, place_of in enumerate(blocks)
    ]
    out_shape, outs_of = [], []
    for whole, blocks in chunks:
        outs_of.append((len(out_shape) if whole else None, len(out_shape) + whole))
        if whole:
            out_shape.append(shaped((len(blocks), share, width), BF16))
        out_shape.append(shaped((len(blocks), share // 2, width), BF16))
    out_shape += [shaped(clip.shape[1:], BF16) for clip in clips]
    count = len(jobs) + len(clips)
    return call(
        functools.partial(pack_kernel, jobs, outs_of, len(clips)),
        [place, *sources, *clips],
        [smem_spec()] + [hbm_spec()] * (len(sources) + len(clips)),
        tuple(out_shape),
        (hbm_spec(),) * len(out_shape),
        deps,
        scratch_shapes=[
            pltpu.VMEM((len(jobs), share, width), BF16),
            pltpu.VMEM((len(clips), clips[0].shape[1], width), BF16),
            pltpu.SemaphoreType.DMA((3, count)),
        ],
        cost_estimate=cost(0, 0),
        name="pack_shares",
    )


def project(layer, standard, vectors_ref, weights, queries_ref, keys_ref, values_ref, ready):
    normed = (standard * vectors_ref[layer, 0:1] + vectors_ref[layer, 1:2]).astype(BF16)
    ready()
    queries = (dot(normed, weights[0]) + vectors_ref[layer, 2:3]).astype(BF16)
    queries_ref[...] = queries * jnp.asarray(HEAD ** (-0.5), BF16)
    keys_ref[...] = dot(normed, weights[1]).astype(BF16)
    values_ref[...] = (dot(normed, weights[2]) + vectors_ref[layer, 3:4]).astype(BF16)


def first_qkv_kernel(place_ref, frames_ref, arrived_ref, vectors_ref, *refs):
    shares, (stream_ref, *outs, weights, sems) = refs[:-6], refs[-6:]
    copies = load_rows(shares, place_ref, QKV, weights, sems, weights.shape[1] // SHARDS)
    start_all(copies)
    quarter = arrived_ref.shape[0]
    stream_ref[:quarter] = frames_ref[place_ref[2]].astype(F32)
    stream_ref[quarter:] = arrived_ref[...].astype(F32)
    standard, _ = standardize(stream_ref[...])
    project(0, standard, vectors_ref, weights, *outs, lambda: wait_all(copies))


def qkv_kernel(layer, place_ref, stream_ref, vectors_ref, *refs):
    shares, (*outs, weights, sems) = refs[:-5], refs[-5:]
    copies = load_rows(shares, place_ref, QKV, weights, sems, weights.shape[1] // SHARDS)
    start_all(copies)
    standard, _ = standardize(stream_ref[...])
    project(layer, standard, vectors_ref, weights, *outs, lambda: wait_all(copies))


def qkv_options(rows, width, name):
    return dict(
        scratch_shapes=[pltpu.VMEM((3, width, width), BF16), pltpu.SemaphoreType.DMA((8,))],
        cost_estimate=cost(6 * rows * width * width, 10 * rows * width + 6 * width * width),
        name=name,
    )


def first_qkv(place, frames, arrived, vectors, shares, deps=()):
    rows, width = 2 * arrived.shape[0], arrived.shape[1]
    return call(
        first_qkv_kernel,
        [place, frames, arrived, vectors, *shares],
        [smem_spec()] + [vmem_spec()] * 3 + [hbm_spec()] * len(shares),
        (shaped((rows, width), F32),) + (shaped((rows, width), BF16),) * 3,
        (vmem_spec(),) * 4,
        deps,
        **qkv_options(rows, width, "first_qkv"),
    )


def next_qkv(layer, place, stream, vectors, shares, deps=()):
    rows, width = stream.shape
    return call(
        functools.partial(qkv_kernel, layer),
        [place, stream, vectors, *shares],
        [smem_spec()] + [vmem_spec()] * 2 + [hbm_spec()] * len(shares),
        (shaped((rows, width), BF16),) * 3,
        (vmem_spec(),) * 3,
        deps,
        **qkv_options(rows, width, "next_qkv"),
    )


def attention_kernel(q_ref, ko_ref, kt_ref, vo_ref, vt_ref, mixed_ref, lse_ref):
    queries_t = q_ref[...].T
    row = lax.broadcasted_iota(jnp.int32, queries_t.shape, 0)
    values_t = (vo_ref[...].T, vt_ref[...].T)
    outs = []
    for head in range(2):
        mine = (row >= head * HEAD) & (row < (head + 1) * HEAD)
        q_t = jnp.where(mine, queries_t, jnp.zeros_like(queries_t))
        scores = (dot(ko_ref[...], q_t), dot(kt_ref[...], q_t))
        peak = jnp.maximum(
            jnp.max(scores[0], axis=0, keepdims=True), jnp.max(scores[1], axis=0, keepdims=True)
        )
        weights = tuple(jnp.exp(part - peak) for part in scores)
        total = jnp.sum(weights[0], axis=0, keepdims=True) + jnp.sum(weights[1], axis=0, keepdims=True)
        lse_ref[0, head : head + 1, :] = peak + jnp.log(total)
        at = slice(head * HEAD, (head + 1) * HEAD)
        out = dot(values_t[0][at], weights[0].astype(BF16)) + dot(values_t[1][at], weights[1].astype(BF16))
        outs.append(out / total)
    mixed_ref[...] = jnp.concatenate(outs, axis=0).T.astype(BF16)


def attend(queries, keys, keys_twin, values, values_twin, deps=()):
    rows, width = queries.shape
    pairs = width // (2 * HEAD)
    block = pl.BlockSpec((rows, 2 * HEAD), lambda pair: (0, pair))
    return call(
        attention_kernel,
        [queries, keys, keys_twin, values, values_twin],
        [block] * 5,
        (shaped((rows, width), BF16), shaped((pairs, 8, rows), F32)),
        (block, pl.BlockSpec((1, 8, rows), lambda pair: (pair, 0, 0))),
        deps,
        grid=(pairs,),
        cost_estimate=cost(32 * rows * rows * width, 12 * rows * width, 4 * pairs * rows * rows),
        name="attend",
    )


def up_kernel(layer, place_ref, stream_ref, mixed_ref, vectors_ref, up_bias_ref, *refs):
    shares, (attended_ref, activated_ref, slope_ref, out_w, up_w, sems) = refs[:-6], refs[-6:]
    width = stream_ref.shape[1]
    share = width // SHARDS
    out_copies = load_rows(shares, place_ref, OUT, out_w, sems.at[0], share)
    up_copies = load_rows(shares, place_ref, UP[layer], up_w, sems.at[1], share)
    start_all(out_copies)
    start_all(up_copies)
    wait_all(out_copies)
    attended_ref[...] = stream_ref[...] + dot(mixed_ref[...], out_w[0]) + vectors_ref[layer, 4:5]
    standard, _ = standardize(attended_ref[...])
    second = (standard * vectors_ref[layer, 5:6] + vectors_ref[layer, 6:7]).astype(BF16)
    wait_all(up_copies)
    for block in range(SHARDS):
        at = slice(block * width, (block + 1) * width)
        hidden = dot(second, up_w[block]) + up_bias_ref[layer : layer + 1, at]
        activated, slope = gelu_parts(hidden)
        activated_ref[:, at] = activated.astype(BF16)
        slope_ref[:, at] = slope.astype(BF16)


def feed_up(layer, place, stream, mixed, vectors, up_bias, shares, deps=()):
    rows, width = stream.shape
    wide = SHARDS * width
    return call(
        functools.partial(up_kernel, layer),
        [place, stream, mixed, vectors, up_bias, *shares],
        [smem_spec()] + [vmem_spec()] * 4 + [hbm_spec()] * len(shares),
        (shaped((rows, width), F32), shaped((rows, wide), BF16), shaped((rows, wide), BF16)),
        (vmem_spec(),) * 3,
        deps,
        scratch_shapes=[
            pltpu.VMEM((1, width, width), BF16),
            pltpu.VMEM((4, width, width), BF16),
            pltpu.SemaphoreType.DMA((2, 12)),
        ],
        cost_estimate=cost(10 * rows * width * width, 24 * rows * width + 10 * width * width, rows * wide),
        name="feed_up",
    )


def down_kernel(layer, place_ref, attended_ref, activated_ref, vectors_ref, *refs):
    shares, (next_ref, down_w, sems) = refs[:-3], refs[-3:]
    width = attended_ref.shape[1]
    copies = load_down(shares, place_ref, DOWN[layer], down_w, sems, width // SHARDS)
    start_all(copies)
    next_ref[...] = attended_ref[...] + vectors_ref[layer, 7:8]
    wait_all(copies)
    next_ref[...] += dot(activated_ref[...], down_w[...].reshape(SHARDS * width, width))


def last_down_kernel(layer, place_ref, attended_ref, activated_ref, vectors_ref, *refs):
    shares, (mine_ref, other_ref, down_w, sems) = refs[:-4], refs[-4:]
    width = attended_ref.shape[1]
    copies = load_down(shares, place_ref, DOWN[layer], down_w, sems, width // SHARDS)
    start_all(copies)
    total = attended_ref[...] + vectors_ref[layer, 7:8]
    wait_all(copies)
    total += dot(activated_ref[...], down_w[...].reshape(SHARDS * width, width))
    half = mine_ref.shape[0]
    mine_ref[...] = total[:half].astype(BF16)
    other_ref[...] = total[half:].astype(BF16)


def feed_down(layer, place, attended, activated, vectors, shares, deps=()):
    rows, width = attended.shape
    last = layer == LAYERS - 1
    return call(
        functools.partial(last_down_kernel if last else down_kernel, layer),
        [place, attended, activated, vectors, *shares],
        [smem_spec()] + [vmem_spec()] * 3 + [hbm_spec()] * len(shares),
        (shaped((rows // 2, width), BF16),) * 2 if last else shaped((rows, width), F32),
        (vmem_spec(),) * 2 if last else vmem_spec(),
        deps,
        scratch_shapes=[
            pltpu.VMEM((4 * SHARDS, width // SHARDS, width), BF16),
            pltpu.SemaphoreType.DMA((12,)),
        ],
        cost_estimate=cost(8 * rows * width * width, 16 * rows * width + 8 * width * width),
        name="feed_down",
    )


def feed_scratch(width):
    return [
        pltpu.VMEM((1, width, width), BF16),
        pltpu.VMEM((4, width, width), BF16),
        pltpu.VMEM((4 * SHARDS, width // SHARDS, width), BF16),
        pltpu.SemaphoreType.DMA((3, 12)),
    ]


def feed_back_kernel(layer, place_ref, grad_ref, slope_ref, attended_ref, vectors_ref, *refs):
    shares, refs = refs[:-9], refs[-9:]
    hidden_ref, attended_grad_ref, mixed_grad_ref, sums_ref, up_sums_ref, out_w, up_w, down_w, sems = refs
    width = grad_ref.shape[1]
    share = width // SHARDS
    down_copies = load_down(shares, place_ref, DOWN[layer], down_w, sems.at[2], share)
    up_copies = load_rows(shares, place_ref, UP[layer], up_w, sems.at[1], share)
    out_copies = load_rows(shares, place_ref, OUT, out_w, sems.at[0], share)
    start_all(down_copies)
    start_all(up_copies)
    start_all(out_copies)
    branch = grad_ref[...].astype(BF16)
    sums_ref[...] = jnp.zeros_like(sums_ref)
    sums_ref[7:8] = column_sum(branch)
    wait_all(down_copies)
    wait_all(up_copies)
    second_grad = None
    for block in range(SHARDS):
        at = slice(block * width, (block + 1) * width)
        down = down_w[block * SHARDS : (block + 1) * SHARDS].reshape(width, width)
        hidden_grad = (dot(branch, down, NT) * slope_ref[:, at].astype(F32)).astype(BF16)
        hidden_ref[:, at] = hidden_grad
        up_sums_ref[:, at] = column_sum(hidden_grad)
        part = dot(hidden_grad, up_w[block], NT)
        second_grad = part if second_grad is None else second_grad + part
    standard, inverse = standardize(attended_ref[...])
    sums_ref[5:6] = column_sum(second_grad * standard)
    sums_ref[6:7] = column_sum(second_grad)
    attended_grad = grad_ref[...] + norm_input_grad(second_grad, standard, inverse, vectors_ref[layer, 5:6])
    attended_grad_ref[...] = attended_grad
    out_grad = attended_grad.astype(BF16)
    sums_ref[4:5] = column_sum(out_grad)
    wait_all(out_copies)
    mixed_grad_ref[...] = dot(out_grad, out_w[0], NT).astype(BF16)


def feed_back(layer, place, grad, slope, attended, vectors, shares, deps=()):
    rows, width = grad.shape
    wide = SHARDS * width
    return call(
        functools.partial(feed_back_kernel, layer),
        [place, grad, slope, attended, vectors, *shares],
        [smem_spec()] + [vmem_spec()] * 4 + [hbm_spec()] * len(shares),
        (
            shaped((rows, wide), BF16),
            shaped((rows, width), F32),
            shaped((rows, width), BF16),
            shaped((8, width), F32),
            shaped((1, wide), F32),
        ),
        (vmem_spec(),) * 5,
        deps,
        scratch_shapes=feed_scratch(width),
        cost_estimate=cost(18 * rows * width * width, 30 * rows * width + 18 * width * width),
        name="feed_back",
    )


def owners(place_ref, keep_ref, send_refs):
    s = place_ref[0]
    return (
        (s ^ 3, send_refs[2:]),
        (s ^ 1, send_refs[:2]),
        (s ^ 2, (keep_ref.at[1, 0], keep_ref.at[1, 1])),
        (s, (keep_ref.at[0, 0], keep_ref.at[0, 1])),
    )


def quarters(place_ref, split, rows):
    size = rows // 4
    near, inner = (place_ref[1], place_ref[3]) if split else (0, 0)
    for y in range(2):
        for z in range(2):
            start = (near ^ y) * (2 * size) + (inner ^ z) * size
            yield y, z, pl.ds(pl.multiple_of(start, size), size)


def run_steps(steps, work, sems):
    pending = [None, None]
    for index, (make, targets) in enumerate(steps):
        slot = index % 2
        if pending[slot] is not None:
            wait_all(pending[slot])
        work[slot] = make().astype(BF16).reshape(work.shape[1:])
        copies = [
            pltpu.make_async_copy(source, target, sems.at[slot, number])
            for number, (source, target) in enumerate(targets(work.at[slot]))
        ]
        start_all(copies)
        pending[slot] = copies
    for copies in pending:
        if copies is not None:
            wait_all(copies)


def by_rows(place_ref, split, keep_ref, send_refs, block):
    def targets(work):
        return [
            (work.at[shard, rows], target[y].at[z, block])
            for shard, target in owners(place_ref, keep_ref, send_refs)
            for y, z, rows in quarters(place_ref, split, work.shape[1])
        ]

    return targets


def whole_share(place_ref, split, target):
    def targets(work):
        return [
            (work.at[:, rows], target[y].at[z]) for y, z, rows in quarters(place_ref, split, work.shape[1])
        ]

    return targets


def down_grad_kernel(split, place_ref, activated_ref, grad_ref, keep_ref, *refs):
    send_refs, (work, sems) = refs[:4], refs[4:]
    width = grad_ref.shape[1]
    branch = grad_ref[...].astype(BF16)
    steps = []
    for shard, target in owners(place_ref, keep_ref, send_refs):
        at = pl.ds(pl.multiple_of(shard * width, width), width)
        steps.append(
            (lambda at=at: dot(activated_ref[:, at], branch, TN), whole_share(place_ref, split, target))
        )
    run_steps(steps, work, sems)


def grad_shapes(count, width):
    part = (2, count, width // SHARDS // 4, width)
    return (shaped((2, 2) + part, BF16),) + (shaped(part, BF16),) * 4


def grad_scratch(width):
    return [pltpu.VMEM((2, SHARDS, width // SHARDS, width), BF16), pltpu.SemaphoreType.DMA((2, 16))]


def down_weight_grad(place, split, activated, grad, deps=()):
    rows, width = grad.shape
    return call(
        functools.partial(down_grad_kernel, split),
        [place, activated, grad],
        [smem_spec()] + [vmem_spec()] * 2,
        grad_shapes(SHARDS, width),
        (hbm_spec(),) * 5,
        deps,
        scratch_shapes=grad_scratch(width),
        cost_estimate=cost(8 * rows * width * width, 12 * rows * width + 8 * width * width),
        name="down_weight_grad",
    )


def feed_grad_kernel(
    layer,
    split,
    place_ref,
    hidden_ref,
    attended_ref,
    attended_grad_ref,
    mixed_ref,
    vectors_ref,
    keep_ref,
    *refs,
):
    send_refs, (work, sems) = refs[:4], refs[4:]
    width = attended_ref.shape[1]
    standard, _ = standardize(attended_ref[...])
    second_t = (standard * vectors_ref[layer, 5:6] + vectors_ref[layer, 6:7]).astype(BF16).T
    steps = [
        (
            lambda: dot(mixed_ref[...], attended_grad_ref[...].astype(BF16), TN),
            by_rows(place_ref, split, keep_ref, send_refs, 0),
        )
    ]
    for block in range(SHARDS):
        at = slice(block * width, (block + 1) * width)
        steps.append(
            (lambda at=at: dot(second_t, hidden_ref[:, at]), by_rows(place_ref, split, keep_ref, send_refs, 1 + block))
        )
    run_steps(steps, work, sems)


def feed_weight_grads(layer, split, place, hidden_grad, attended, attended_grad, mixed, vectors, deps=()):
    rows, width = attended.shape
    return call(
        functools.partial(feed_grad_kernel, layer, split),
        [place, hidden_grad, attended, attended_grad, mixed, vectors],
        [smem_spec()] + [vmem_spec()] * 5,
        grad_shapes(1 + SHARDS, width),
        (hbm_spec(),) * 5,
        deps,
        scratch_shapes=grad_scratch(width),
        cost_estimate=cost(10 * rows * width * width, 20 * rows * width + 10 * width * width),
        name="feed_weight_grads",
    )


def qkv_grad_kernel(
    layer,
    split,
    place_ref,
    stream_ref,
    vectors_ref,
    dq_ref,
    dk_ref,
    dv_ref,
    dk_back_ref,
    dv_back_ref,
    sums_ref,
    total_ref,
    keep_ref,
    *refs,
):
    send_refs, (work, sems) = refs[:4], refs[4:]
    standard, _ = standardize(stream_ref[...])
    normed_t = (standard * vectors_ref[layer, 0:1] + vectors_ref[layer, 1:2]).astype(BF16).T
    total_ref[0] = (dk_ref[...].astype(F32) + dk_back_ref[...].astype(F32)).astype(BF16)
    total_ref[1] = (dv_ref[...].astype(F32) + dv_back_ref[...].astype(F32)).astype(BF16)
    sums_ref[...] = jnp.zeros_like(sums_ref)
    sums_ref[2:3] = column_sum(dq_ref[...])
    sums_ref[3:4] = column_sum(total_ref[1])
    makers = (
        lambda: dot(normed_t, dq_ref[...]),
        lambda: dot(normed_t, total_ref[0]),
        lambda: dot(normed_t, total_ref[1]),
    )
    run_steps(
        [(make, by_rows(place_ref, split, keep_ref, send_refs, block)) for block, make in enumerate(makers)],
        work,
        sems,
    )


def qkv_weight_grads(layer, split, place, stream, vectors, dq, dk, dv, dk_back, dv_back, deps=()):
    rows, width = stream.shape
    return call(
        functools.partial(qkv_grad_kernel, layer, split),
        [place, stream, vectors, dq, dk, dv, dk_back, dv_back],
        [smem_spec()] + [vmem_spec()] * 7,
        (shaped((8, width), F32), shaped((2, rows, width), BF16)) + grad_shapes(3, width),
        (vmem_spec(),) * 2 + (hbm_spec(),) * 5,
        deps,
        scratch_shapes=grad_scratch(width),
        cost_estimate=cost(6 * rows * width * width, 10 * rows * width + 6 * width * width),
        name="qkv_weight_grads",
    )


def attention_back_kernel(
    q_ref,
    ko_ref,
    kt_ref,
    vo_ref,
    vt_ref,
    lse_ref,
    out_grad_ref,
    dq_ref,
    dk_ref,
    dv_ref,
    dk_twin_ref,
    dv_twin_ref,
):
    queries = q_ref[...]
    out_grad = out_grad_ref[...]
    queries_t, out_grad_t = queries.T, out_grad.T
    row = lax.broadcasted_iota(jnp.int32, queries_t.shape, 0)
    lane = lax.broadcasted_iota(jnp.int32, queries.shape, 1)
    keys, values = (ko_ref, kt_ref), (vo_ref, vt_ref)
    keys_t = tuple(part[...].T for part in keys)
    key_grads, value_grads, query_grads = [None, None], [None, None], []
    for head in range(2):
        low, high = head * HEAD, (head + 1) * HEAD
        mine_t = (row >= low) & (row < high)
        mine = (lane >= low) & (lane < high)
        q_t = jnp.where(mine_t, queries_t, jnp.zeros_like(queries_t))
        o_t = jnp.where(mine_t, out_grad_t, jnp.zeros_like(queries_t))
        q_h = jnp.where(mine, queries, jnp.zeros_like(queries))
        o_h = jnp.where(mine, out_grad, jnp.zeros_like(queries))
        lse = lse_ref[0, head : head + 1, :]
        probability = [jnp.exp(dot(part[...], q_t) - lse) for part in keys]
        probability_grad = [dot(part[...], o_t) for part in values]
        inner = sum(
            jnp.sum(left * right, axis=0, keepdims=True)
            for left, right in zip(probability, probability_grad)
        )
        query_grad = None
        for index in range(2):
            score_grad = (probability[index] * (probability_grad[index] - inner)).astype(BF16)
            value_part = dot(probability[index].astype(BF16), o_h)
            key_part = dot(score_grad, q_h)
            query_part = dot(keys_t[index][low:high], score_grad)
            if head == 0:
                key_grads[index], value_grads[index] = key_part, value_part
            else:
                key_grads[index] += key_part
                value_grads[index] += value_part
            query_grad = query_part if index == 0 else query_grad + query_part
        query_grads.append(query_grad)
    dq_ref[...] = (jnp.concatenate(query_grads, axis=0).T * HEAD ** (-0.5)).astype(BF16)
    for ref, value in zip((dk_ref, dk_twin_ref, dv_ref, dv_twin_ref), key_grads + value_grads):
        ref[...] = value.astype(BF16)


def attend_back(queries, keys, keys_twin, values, values_twin, lse, out_grad, deps=()):
    rows, width = queries.shape
    pairs = width // (2 * HEAD)
    block = pl.BlockSpec((rows, 2 * HEAD), lambda pair: (0, pair))
    return call(
        attention_back_kernel,
        [queries, keys, keys_twin, values, values_twin, lse, out_grad],
        [block] * 5 + [pl.BlockSpec((1, 8, rows), lambda pair: (pair, 0, 0)), block],
        (shaped((rows, width), BF16),) * 5,
        (block,) * 5,
        deps,
        grid=(pairs,),
        cost_estimate=cost(80 * rows * rows * width, 24 * rows * width),
        name="attend_back",
    )


def norm_back_kernel(layer, place_ref, stream_ref, vectors_ref, attended_grad_ref, dq_ref, dkv_ref, *refs):
    shares, (grad_ref, sums_ref, weights, sems) = refs[:-4], refs[-4:]
    copies = load_rows(shares, place_ref, QKV, weights, sems, weights.shape[1] // SHARDS)
    start_all(copies)
    standard, inverse = standardize(stream_ref[...])
    wait_all(copies)
    normed_grad = (
        dot(dq_ref[...], weights[0], NT) + dot(dkv_ref[0], weights[1], NT) + dot(dkv_ref[1], weights[2], NT)
    )
    sums_ref[...] = jnp.zeros_like(sums_ref)
    sums_ref[0:1] = column_sum(normed_grad * standard)
    sums_ref[1:2] = column_sum(normed_grad)
    grad_ref[...] = attended_grad_ref[...] + norm_input_grad(
        normed_grad, standard, inverse, vectors_ref[layer, 0:1]
    )


def norm_back(layer, place, stream, vectors, attended_grad, dq, dkv, shares, deps=()):
    rows, width = stream.shape
    return call(
        functools.partial(norm_back_kernel, layer),
        [place, stream, vectors, attended_grad, dq, dkv, *shares],
        [smem_spec()] + [vmem_spec()] * 5 + [hbm_spec()] * len(shares),
        (shaped((rows, width), F32), shaped((8, width), F32)),
        (vmem_spec(),) * 2,
        deps,
        scratch_shapes=[pltpu.VMEM((3, width, width), BF16), pltpu.SemaphoreType.DMA((8,))],
        cost_estimate=cost(6 * rows * width * width, 18 * rows * width + 6 * width * width),
        name="norm_back",
    )


def finish_kernel(layer, split, pieces, places, place_ref, *refs):
    sources, refs = refs[: len(pieces)], refs[len(pieces) :]
    outs, (arrived, work, sems) = refs[:-3], refs[-3:]
    count = len(places)
    near, inner = (place_ref[1], place_ref[3]) if split else (0, 0)
    size, width = work.shape[1:]
    loads = []
    for index, (source, (start, _, _)) in enumerate(zip(sources, pieces)):
        at = pl.ds(index * count, count)
        loads.append(pltpu.make_async_copy(source.at[pl.ds(start, count)], arrived.at[at], sems.at[0, index]))
    start_all(loads)
    stores = []
    for number, (load, (_, y, z)) in enumerate(zip(loads, pieces)):
        load.wait()
        for block, (out, row, column) in enumerate(places):
            index = number * count + block
            work[index] = arrived[index].astype(F32)
            start = row + (near ^ y) * (2 * size) + (inner ^ z) * size
            target = outs[out].at[layer, aligned(start, size), pl.ds(column, width)]
            stores.append(pltpu.make_async_copy(work.at[index], target, sems.at[1, index]))
            stores[-1].start()
    wait_all(stores)


def finish(layer, split, sources, places, out_shapes, place, buffers=None, deps=()):
    size, width = sources[0][0].shape[-2:]
    count = 4 * len(places)
    operands = [place, *(source[0] for source in sources)]
    aliases = {}
    if buffers is not None:
        aliases = {len(operands) + index: index for index in range(len(buffers))}
        operands += list(buffers)
    first = 1 + len(sources)
    pieces = [source[1:] for source in sources]

    def kernel(*refs):
        finish_kernel(layer, split, pieces, places, *refs[:first], *refs[len(operands) :])

    return call(
        kernel,
        operands,
        [smem_spec()] + [hbm_spec()] * (len(operands) - 1),
        tuple(shaped(shape, F32) for shape in out_shapes),
        (hbm_spec(),) * len(out_shapes),
        deps,
        input_output_aliases=aliases,
        scratch_shapes=[
            pltpu.VMEM((count, size, width), BF16),
            pltpu.VMEM((count, size, width), F32),
            pltpu.SemaphoreType.DMA((2, count)),
        ],
        cost_estimate=cost(0, 6 * count * size * width),
        name="finish",
    )


def combine_kernel(plan, *refs):
    arrays = 1 + max(operand for segments in plan for _, terms in segments for operand, _ in terms)
    operands, outs, (work, sems, out_sems) = refs[:arrays], refs[arrays:-3], refs[-3:]
    jobs, copies, at = [], [], 0
    for out, segments in zip(outs, plan):
        place = 0
        for count, terms in segments:
            places = []
            for operand, start in terms:
                source = operands[operand].at[pl.ds(start, count)]
                copies.append(
                    pltpu.make_async_copy(source, work.at[pl.ds(at, count)], sems.at[len(copies)])
                )
                places.append((copies[-1], at))
                at += count
            jobs.append((out, place, count, places))
            place += count
    start_all(copies)
    stores = []
    for out, place, count, places in jobs:
        for copy, _ in places:
            copy.wait()
        first = places[0][1]
        if len(places) == 2:
            for index in range(count):
                work[first + index] += work[places[1][1] + index]
        elif len(places) > 2:
            for index in range(count):
                total = work[first + index].astype(F32)
                for _, start in places[1:]:
                    total += work[start + index].astype(F32)
                work[first + index] = total.astype(BF16)
        stores.append(
            pltpu.make_async_copy(
                work.at[pl.ds(first, count)], out.at[pl.ds(place, count)], out_sems.at[len(stores)]
            )
        )
        stores[-1].start()
    wait_all(stores)


def combine(outputs, deps=()):
    arrays, plan = [], []
    for segments in outputs:
        plan.append([])
        for count, terms in segments:
            named = []
            for array, start in terms:
                index = next((i for i, known in enumerate(arrays) if known is array), len(arrays))
                if index == len(arrays):
                    arrays.append(array)
                named.append((index, start))
            plan[-1].append((count, named))
    size, width = arrays[0].shape[1:]
    moves = [len(terms) for segments in plan for _, terms in segments]
    rows = sum(count * len(terms) for segments in plan for count, terms in segments)
    return call(
        functools.partial(combine_kernel, plan),
        arrays,
        [hbm_spec()] * len(arrays),
        tuple(shaped((sum(count for count, _ in segments), size, width), BF16) for segments in plan),
        (hbm_spec(),) * len(plan),
        deps,
        scratch_shapes=[
            pltpu.VMEM((rows, size, width), BF16),
            pltpu.SemaphoreType.DMA((sum(moves),)),
            pltpu.SemaphoreType.DMA((len(moves),)),
        ],
        cost_estimate=cost(0, 0),
        name="combine",
    )


PAIRS, MIRROR = [(0, 1), (1, 0), (2, 3), (3, 2)], [(0, 3), (3, 0), (1, 2), (2, 1)]


class Flow:
    def __init__(self, split, parts, *pins, last="spread"):
        keep, *send = parts
        self.split, self.count, self.last = split, keep.shape[3], last
        self.keep = keep.reshape((-1,) + keep.shape[-2:])
        send = after(tuple(send), *pins)
        self.back = [swap(part.reshape((-1,) + part.shape[-2:]), "core") for part in send]

    def sums(self, x, y, z, *arrivals):
        n = self.count
        terms = [(self.keep, (4 * x + 2 * y + z) * n), (self.back[2 * x + y], z * n)]
        return (n, terms + [(array, start + offset * n) for (array, start), offset in arrivals])

    def segments(self, stage):
        n = self.count
        if stage == "x":
            return {"x": [self.sums(1, y, z) for y in range(2) for z in range(2)]}
        if stage == "y":
            return {"y": [self.sums(0, 1, z, (self.x, 2 + z)) for z in range(2)]}
        if stage == "pair":
            if not self.split:
                return {"sum": [self.sums(0, 0, z, (self.x, z), (self.y, z)) for z in range(2)]}
            return {"pair": [self.sums(0, 0, 1, (self.x, 1), (self.y, 1))]}
        if stage == "mirror":
            if not self.split:
                return {}
            return {"mirror": [self.sums(0, 0, 0, (self.x, 0), (self.y, 0), (self.pair, 0))]}
        if stage == "after":
            if not self.split:
                return {"near": [(2 * n, [self.sum])]}
            whole = (n, [self.mirror_sent, self.mirror])
            return {channel: [whole] for channel in ("near", "spread", "diagonal")[: 3 if self.last is None else 2]}
        if not self.split or self.last is None:
            return {}
        return {self.last: [(n, [self.rest if self.last == "spread" else self.part_z])]}

    def record(self, stage, channel, sent, arrived):
        if stage == "after":
            if channel == "near":
                self.part, self.rest = sent, arrived
            elif channel == "spread":
                self.part_z = arrived
            else:
                self.rest_z = arrived
        elif stage == "last":
            self.rest_z = arrived
        else:
            setattr(self, channel, arrived)
            setattr(self, channel + "_sent", sent)

    def finish(self, layer, places, out_shapes, place, buffers=None, deps=()):
        n = self.count
        if self.split:
            sources = [(*self.part, 0, 0), (*self.part_z, 0, 1), (*self.rest, 1, 0), (*self.rest_z, 1, 1)]
        else:
            sources = [
                (array, start + z * n, y, z)
                for y, (array, start) in enumerate((self.part, self.rest))
                for z in range(2)
            ]
        return finish(layer, self.split, sources, places, out_shapes, place, buffers, deps)


class Totals:
    def __init__(self, split, values):
        self.split = split
        self.terms = [(values, 0), (swap(values, "core"), 0)]

    def segments(self, stage):
        if stage in ("pair", "mirror") and not self.split:
            return {"sum": [(1, self.terms)]} if stage == "pair" else {}
        return {stage: [(1, self.terms)]}

    def record(self, stage, channel, sent, arrived):
        self.terms = [arrived] if channel == "sum" else [sent, arrived]

    def done(self):
        return sum(array[start].astype(F32) for array, start in self.terms)


def exchange(steps, *pins):
    outputs, owners_of = {}, {}
    for flow, stage in steps:
        for channel, segments in flow.segments(stage).items():
            placed = outputs.setdefault(channel, [])
            start = sum(count for count, _ in placed)
            owners_of.setdefault(channel, []).append((flow, stage, start))
            placed += segments
    if not outputs:
        return pins[0], ()
    names, landed = list(outputs), []
    results = combine([outputs[name] for name in names], pins)
    for name, sent in zip(names, results):
        if name == "sum":
            arrived = lax.psum(sent, "z")
        elif name == "diagonal":
            both = [(2 * left + y, 2 * right + 1 - y) for left, right in PAIRS for y in range(2)]
            arrived = lax.ppermute(sent, ("z", "y"), both)
        elif name in ("pair", "spread", "mirror"):
            arrived = lax.ppermute(sent, "z", MIRROR if name == "mirror" else PAIRS)
        else:
            arrived = swap(sent, "y" if name == "near" else name)
        landed.append(arrived)
        for flow, stage, start in owners_of[name]:
            flow.record(stage, name, (sent, start), (arrived, start))
    return results[0], tuple(landed)


def body(
    frames,
    cotangent,
    first_gain,
    first_shift,
    query_weight,
    query_bias,
    key_weight,
    value_weight,
    value_bias,
    out_weight,
    out_bias,
    second_gain,
    second_shift,
    up_weight,
    up_bias,
    down_weight,
    down_bias,
):
    x, y, z, core = (lax.axis_index(axis) for axis in ("x", "y", "z", "core"))
    shard = 2 * x + core
    inner = jnp.where((z == 0) | (z == 3), 0, 1)
    place = jnp.stack([shard, y, x, inner]).astype(jnp.int32)
    quarter, width = frames.shape[1:]
    share = width // SHARDS
    split = lax.axis_size("z") == 4

    def blocks_of(layer):
        attention = [(source, layer, (0, 0)) for source in (0, 1, 2)]
        up = [(3, layer, (0, 0))] + [(4, layer, (0, block * width)) for block in range(SHARDS)]
        down = [(5, layer, (block * share, 0)) for block in range(SHARDS)]
        return attention, up, down

    sources = (query_weight, key_weight, value_weight, out_weight, up_weight, down_weight)
    (attention0, up0, down0), (attention1, up1, down1) = blocks_of(0), blocks_of(1)
    own0, half0, other_frames = pack_shares(
        place, sources[:3], [(True, attention0)], share, width, clips=(frames,)
    )
    near = {0: swap(half0, "x")}
    arrived_frames = swap(other_frames, "x")
    twin = {0: swap(own0, "core")}
    *packed, other_cotangent = pack_shares(
        place,
        sources,
        [
            (True, blocks)
            for blocks in (up0 + down0[:1], down0[1:], attention1, up1[:3], up1[3:], down1)
        ],
        share,
        width,
        clips=(cotangent,),
        deps=(half0,),
    )
    own, half = dict(enumerate([own0, *packed[0::2]])), dict(enumerate([half0, *packed[1::2]]))
    near[0] = after(near[0], half[1])
    far, near_twin, far_twin = {0: swap(near[0], "y")}, {0: swap(near[0], "core")}, {}

    small = jnp.stack(
        [first_gain, first_shift, query_bias, value_bias, out_bias, second_gain, second_shift, down_bias], axis=1
    )
    small = jnp.concatenate([small, up_bias.reshape(LAYERS, SHARDS, share)], axis=1)
    small = after(small, half0)
    pair = jnp.stack([small, swap(small, "core")])
    pieces = jnp.concatenate([pair, swap(pair, "x")], axis=0)
    small = jnp.stack(
        [lax.dynamic_index_in_dim(pieces, shard ^ index, 0, keepdims=False) for index in range(SHARDS)]
    ).astype(F32)
    vectors = jnp.transpose(small[:, :, :8], (1, 2, 0, 3)).reshape(LAYERS, 8, width)
    up_biases = jnp.transpose(small[:, :, 8:], (1, 0, 2, 3)).reshape(LAYERS, SHARDS * width)

    def fetch(chunk, *pins):
        near[chunk] = swap(after(half[chunk], *pins), "x")

    def spread(chunk, *pins):
        far[chunk] = swap(after(near[chunk], *pins), "y")

    def trade(chunk, *pins):
        twin[chunk] = swap(after(own[chunk], *pins), "core")

    def trade_near(chunk, *pins):
        near_twin[chunk] = swap(after(near[chunk], *pins), "core")

    def trade_far(chunk, *pins):
        far_twin[chunk] = swap(after(far[chunk], *pins), "core")

    def shares(chunk):
        return own[chunk], twin[chunk], near[chunk], far[chunk], near_twin[chunk], far_twin[chunk]

    trade_far(0)
    fetch(1, arrived_frames)
    for chunk in range(1, 7):
        trade(chunk, arrived_frames)
    stream0, queries0, keys0, values0 = first_qkv(
        place, frames, arrived_frames, vectors, shares(0), deps=tuple(twin[chunk] for chunk in range(1, 7))
    )
    qkv0 = shares(0)
    keys0, values0 = after((keys0, values0), near[1])
    keys_twin0, values_twin0 = swap(keys0, "core"), swap(values0, "core")
    fetch(2, keys0)
    spread(1, keys0)
    trade_near(1, keys0)
    mixed0, lse0 = attend(queries0, keys0, keys_twin0, values0, values_twin0, deps=(near_twin[1],))
    trade_far(1, mixed0)
    fetch(3, near[2], mixed0)
    spread(2, mixed0)
    trade_near(2, mixed0)
    attended0, activated0, slope0 = feed_up(
        0, place, stream0, mixed0, vectors, up_biases, shares(1), deps=(near_twin[2],)
    )
    trade_far(2, activated0)
    fetch(4, near[3], activated0)
    spread(3, activated0)
    trade_near(3, activated0)
    second0 = shares(1) + shares(2)
    stream1 = feed_down(0, place, attended0, activated0, vectors, second0, deps=(near_twin[3],))
    trade_far(3, stream1)
    fetch(5, near[4], stream1)
    spread(4, stream1)
    trade_near(4, stream1)
    qkv1 = shares(3)
    queries1, keys1, values1 = next_qkv(1, place, stream1, vectors, qkv1, deps=(near_twin[4],))
    keys1, values1 = after((keys1, values1), near[5], far[4])
    keys_twin1, values_twin1 = swap(keys1, "core"), swap(values1, "core")
    fetch(6, near[5], keys1)
    spread(5, keys1)
    trade_near(5, keys1)
    trade_far(4, keys1)
    mixed1, lse1 = attend(
        queries1, keys1, keys_twin1, values1, values_twin1, deps=(near_twin[5], far_twin[4])
    )
    trade_far(5, mixed1)
    spread(6, mixed1)
    trade_near(6, mixed1)
    arrived_cotangent = swap(after(other_cotangent, near[6]), "x")
    late = shares(4) + shares(5)
    attended1, activated1, slope1 = feed_up(
        1, place, stream1, mixed1, vectors, up_biases, late, deps=(near_twin[6],)
    )
    mine_cotangent = lax.dynamic_index_in_dim(cotangent, x, 0, keepdims=False)
    pieces = after((mine_cotangent, arrived_cotangent), attended1)
    gradient = jnp.concatenate(pieces, axis=0).astype(F32)
    down1 = Flow(split, down_weight_grad(place, split, activated1, gradient), far[6])
    trade_far(6, down1.keep)
    output_mine, output_other = feed_down(1, place, attended1, activated1, vectors, shares(6))
    late += shares(6)

    def by_clip(mine, other):
        return jnp.where(x == 0, jnp.stack([mine, other]), jnp.stack([other, mine]))

    def square(row_blocks, column_blocks):
        return (LAYERS, row_blocks * share, column_blocks * width)

    down_places, down_shapes = [(0, block * share, 0) for block in range(SHARDS)], [square(SHARDS, 1)]
    feed_places = [(0, 0, 0)] + [(1, 0, block * width) for block in range(SHARDS)]
    feed_shapes = [square(1, 1), square(1, SHARDS)]
    qkv_places, qkv_shapes = [(block, 0, 0) for block in range(3)], [square(1, 1)] * 3

    pin, landed = exchange([(down1, "x")], output_mine, *down1.back)
    hidden_grad, attended_grad, mixed_grad, feed_sums1, up_sums1 = feed_back(
        1, place, gradient, slope1, attended1, vectors, late, deps=(pin,)
    )
    parts = feed_weight_grads(1, split, place, hidden_grad, attended1, attended_grad, mixed1, vectors)
    feed1 = Flow(split, parts)
    pin, (near, far) = exchange([(down1, "y"), (feed1, "x")], *feed1.back)
    dq, dk, dv, dk_twin, dv_twin = attend_back(
        queries1, keys1, keys_twin1, values1, values_twin1, lse1, mixed_grad, deps=(pin,)
    )
    dk_twin, dv_twin = after((dk_twin, dv_twin), near)
    dk_back, dv_back = swap(dk_twin, "core"), swap(dv_twin, "core")
    pin, landed = exchange([(down1, "pair")], dq)
    qkv_sums1, dkv, *parts = qkv_weight_grads(
        1, split, place, stream1, vectors, dq, dk, dv, dk_back, dv_back, deps=(pin,)
    )
    gradient, norm_sums1 = norm_back(
        1, place, stream1, vectors, attended_grad, dq, dkv, qkv1, deps=(parts[0],)
    )
    qkv_1 = Flow(split, parts, far, *landed, last="near")
    pin, landed = exchange([(qkv_1, "x"), (feed1, "y"), (down1, "mirror")], gradient, *qkv_1.back)

    parts = down_weight_grad(place, split, activated0, gradient, deps=(pin,))
    hidden_grad, attended_grad, mixed_grad, feed_sums0, up_sums0 = feed_back(
        0, place, gradient, slope0, attended0, vectors, second0, deps=(parts[0],)
    )
    down0 = Flow(split, parts, mixed_grad, *landed, last="near")
    steps = [(down0, "x"), (qkv_1, "y"), (down1, "after"), (feed1, "pair")]
    pin, landed = exchange(steps, mixed_grad, *down0.back)
    parts = feed_weight_grads(
        0, split, place, hidden_grad, attended0, attended_grad, mixed0, vectors, deps=(pin,)
    )
    dq, dk, dv, dk_twin, dv_twin = attend_back(
        queries0, keys0, keys_twin0, values0, values_twin0, lse0, mixed_grad, deps=(parts[0],)
    )
    dk_twin, dv_twin = after((dk_twin, dv_twin), *landed)
    dk_back, dv_back = swap(dk_twin, "core"), swap(dv_twin, "core")
    feed0 = Flow(split, parts, dq, *landed, last=None)
    steps = [(feed0, "x"), (down0, "y"), (down1, "last"), (qkv_1, "pair"), (feed1, "mirror")]
    pin, (far, *landed) = exchange(steps, dq, *feed0.back)
    qkv_sums0, dkv, *parts = qkv_weight_grads(
        0, split, place, stream0, vectors, dq, dk, dv, dk_back, dv_back, deps=(pin,)
    )
    gradient, norm_sums0 = norm_back(
        0, place, stream0, vectors, attended_grad, dq, dkv, qkv0, deps=(parts[0],)
    )
    qkv_0 = Flow(split, parts, gradient, *landed, last=None)
    sums = jnp.concatenate(
        [
            part
            for feed, qkv, norm, up in (
                (feed_sums0, qkv_sums0, norm_sums0, up_sums0),
                (feed_sums1, qkv_sums1, norm_sums1, up_sums1),
            )
            for part in (feed + qkv + norm, up.reshape(SHARDS, width))
        ]
    ).astype(BF16)
    sums = jnp.pad(sums, ((0, share // 4 - sums.shape[0]), (0, 0)))
    totals = Totals(split, sums[None])
    steps = [(qkv_0, "x"), (totals, "x"), (down0, "pair"), (feed1, "after")]
    pin, landed = exchange(steps, gradient, *qkv_0.back)
    down_out = down1.finish(1, down_places, down_shapes, place, deps=(pin,))
    pin, landed = exchange([(feed0, "y"), (down0, "mirror"), (qkv_1, "mirror"), (feed1, "last")], down_out[0])
    input_other = swap(after(gradient[quarter:].astype(BF16), pin), "x")
    steps = [(qkv_0, "y"), (totals, "y"), (feed0, "pair"), (down0, "after"), (qkv_1, "after")]
    pin, landed = exchange(steps, pin)
    output_other = swap(after(output_other, pin), "x")
    feed_out = feed1.finish(1, feed_places, feed_shapes, place, deps=(pin, input_other))
    input_grad = by_clip(gradient[:quarter], input_other.astype(F32))
    steps = [(qkv_0, "pair"), (totals, "pair"), (feed0, "mirror"), (down0, "last"), (qkv_1, "last")]
    pin, landed = exchange(steps, feed_out[0], output_other)
    output = by_clip(output_mine, output_other)
    steps = [(qkv_0, "mirror"), (totals, "mirror"), (feed0, "after")]
    pin, landed = exchange(steps, pin)
    (down_out,) = down0.finish(0, down_places, down_shapes, place, down_out, deps=(pin,))
    qkv_out = qkv_1.finish(1, qkv_places, qkv_shapes, place, deps=(down_out,))
    pin, landed = exchange([(qkv_0, "after")], qkv_out[0])
    totals = totals.done()[: LAYERS * (8 + SHARDS)].reshape(LAYERS, 8 + SHARDS, width)
    out_out, up_out = feed0.finish(0, feed_places, feed_shapes, place, feed_out, deps=(pin,))
    query_out, key_out, value_out = qkv_0.finish(
        0, qkv_places, qkv_shapes, place, qkv_out, deps=(out_out,)
    )

    own_vectors = lax.dynamic_slice_in_dim(totals[:, :8], shard * share, share, axis=2)
    own_up = lax.dynamic_slice_in_dim(
        totals[:, 8:].reshape(LAYERS, SHARDS * width), shard * width, width, axis=1
    )
    vector = [own_vectors[:, index] for index in range(8)]
    return (
        output,
        input_grad,
        vector[0],
        vector[1],
        query_out,
        vector[2],
        key_out,
        value_out,
        vector[3],
        out_out,
        vector[4],
        vector[5],
        vector[6],
        up_out,
        own_up,
        down_out,
        vector[7],
    )


def solution(mesh):
    groups = mesh.shape["rep"]
    finer = Mesh(mesh.devices.reshape(groups // 2, 2, 2, 2), ("z", "y", "x", "core"))
    rep, shard = ("z", "y"), ("x", "core")
    rows = P(rep, shard, None)
    vector, matrix = P(None, shard), P(None, shard, None)
    parameters = (
        vector,
        vector,
        matrix,
        vector,
        matrix,
        matrix,
        vector,
        matrix,
        vector,
        vector,
        vector,
        matrix,
        vector,
        matrix,
        vector,
    )
    return jax.shard_map(
        body,
        mesh=finer,
        in_specs=(rows, rows) + parameters,
        out_specs=(rows, rows) + parameters,
        check_vma=False,
    )
```

```python
import functools

import jax
import jax.numpy as jnp
from jax import lax
from jax.experimental import pallas as pl
from jax.experimental.pallas import tpu as pltpu
from jax.sharding import Mesh
from jax.sharding import PartitionSpec as P

HEAD = 64
LAYERS = 2
SHARDS = 4
EPSILON = 1e-05
SWAP = [(0, 1), (1, 0)]
F32 = jnp.float32
BF16 = jnp.bfloat16
NN = (((1,), (0,)), ((), ()))
NT = (((1,), (1,)), ((), ()))
TN = (((0,), (0,)), ((), ()))
VMEM_LIMIT = 40 * 1024 * 1024
SCALE = 0.0

QKV = ((0, slice(0, 3), 0),)
OUT = ((0, slice(0, 1), 0),)
UP = (((0, slice(1, 5), 0),), ((0, slice(1, 3), 0), (6, slice(0, 2), 2)))
DOWN = (((0, slice(5, 6), 0), (6, slice(0, 3), 1)), ((-6, slice(0, 4), 0),))


def dot(left, right, dims=NN):
    return lax.dot_general(left, right, dims, preferred_element_type=F32)


def swap(values, axis):
    return lax.ppermute(values, axis, SWAP)


def vmem_spec():
    return pl.BlockSpec(memory_space=pltpu.VMEM)


def any_spec():
    return pl.BlockSpec(memory_space=pl.ANY)


def hbm_spec():
    return pl.BlockSpec(memory_space=pltpu.HBM)


def smem_spec():
    return pl.BlockSpec(memory_space=pltpu.SMEM)


def cost(flops, bytes_accessed, transcendentals=0):
    return pl.CostEstimate(
        flops=int(SCALE * flops), bytes_accessed=int(SCALE * bytes_accessed), transcendentals=0
    )


def shaped(shape, dtype):
    return jax.ShapeDtypeStruct(shape, dtype)


def call(kernel, operands, in_specs, out_shape, out_specs, deps=(), **options):
    def placed(array, spec):
        if spec.memory_space == pltpu.HBM:
            return pltpu.with_memory_space_constraint(array, pltpu.HBM)
        return array

    def result(shape, spec):
        return pltpu.HBM(shape.shape, shape.dtype) if spec.memory_space == pltpu.HBM else shape

    if isinstance(out_shape, tuple):
        out_shape = tuple(map(result, out_shape, out_specs))
    if deps:
        operands = [after(operands[0], *deps), *operands[1:]]
    return pl.pallas_call(
        kernel,
        in_specs=list(in_specs),
        out_shape=out_shape,
        out_specs=out_specs,
        compiler_params=pltpu.CompilerParams(vmem_limit_bytes=VMEM_LIMIT),
        **options,
    )(*map(placed, operands, in_specs))


def after(values, *deps):
    if isinstance(values, tuple):
        return lax.optimization_barrier(values + deps)[: len(values)]
    return lax.optimization_barrier((values,) + deps)[0]


def standardize(values):
    average = jnp.mean(values, axis=-1, keepdims=True)
    centered = values - average
    variance = jnp.mean(centered * centered, axis=-1, keepdims=True)
    inverse_scale = lax.rsqrt(variance + EPSILON)
    return centered * inverse_scale, inverse_scale


def norm_input_grad(grad_out, standard, inverse_scale, gain):
    grad_standard = grad_out * gain
    return inverse_scale * (
        grad_standard
        - jnp.mean(grad_standard, axis=-1, keepdims=True)
        - standard * jnp.mean(grad_standard * standard, axis=-1, keepdims=True)
    )


def column_sum(values):
    return jnp.sum(values.astype(F32), axis=0, keepdims=True)


def gelu_parts(hidden):
    density = jnp.exp(-0.5 * hidden * hidden)
    t = 1.0 / (1.0 + (0.3275911 * 0.7071067811865476) * jnp.abs(hidden))
    series = t * (
        0.127414796
        + t * (-0.142248368 + t * (0.7107068705 + t * (-0.7265760135 + t * 0.5307027145)))
    )
    tail = series * density
    phi = jnp.where(hidden >= 0.0, 1.0 - tail, tail)
    return hidden * phi, phi + (hidden * 0.3989422804014327) * density


def pieces_of(place_ref, refs):
    s, y = place_ref[0], place_ref[1]
    places = ((s, None), (s ^ 1, None), (s ^ 2, y), (s ^ 2, 1 - y), (s ^ 3, y), (s ^ 3, 1 - y))
    return [(ref, *place) for ref, place in zip(refs, places)]


def aligned(start, size):
    return pl.ds(start if isinstance(start, int) else pl.multiple_of(start, size), size)


def load_rows(refs, place_ref, groups, target, sems, rows):
    copies = []
    for first, blocks, block in groups:
        for piece, shard, half in pieces_of(place_ref, refs[first:]):
            start, size = shard * rows, rows
            if half is not None:
                size = rows // 2
                start = start + half * size
            place = target.at[pl.ds(block, blocks.stop - blocks.start), aligned(start, size), :]
            copies.append(pltpu.make_async_copy(piece.at[blocks], place, sems.at[len(copies)]))
    return copies


def load_down(refs, place_ref, groups, target, sems, rows):
    copies = []
    for first, blocks, block in groups:
        for piece, shard, half in pieces_of(place_ref, refs[first:]):
            at = pl.ds(shard * SHARDS + block, blocks.stop - blocks.start)
            place = target.at[at]
            if half is not None:
                size = rows // 2
                place = target.at[at, aligned(half * size, size)]
            copies.append(pltpu.make_async_copy(piece.at[blocks], place, sems.at[len(copies)]))
    return copies


def start_all(copies):
    for copy in copies:
        copy.start()


def wait_all(copies):
    for copy in copies:
        copy.wait()


def pack_kernel(jobs, outs_of, slices, place_ref, *refs):
    count = 1 + max(source for _, _, source, _, _ in jobs)
    sources, inputs, refs = refs[:count], refs[count : count + slices], refs[count + slices :]
    outs, picked, work, frames, sems = refs[: -3 - slices], refs[-3 - slices : -3], *refs[-3:]
    loads, stores = [], []
    for index, (chunk, block, source, layer, (rows, columns)) in enumerate(jobs):
        own, half = outs_of[chunk]
        size, width = outs[half].shape[1:]
        whole = sources[source].at[layer, pl.ds(rows, 2 * size), pl.ds(columns, width)]
        part = work.at[index, pl.ds(pl.multiple_of(place_ref[1] * size, size), size)]
        loads.append([pltpu.make_async_copy(whole, work.at[index], sems.at[0, index])])
        stores.append([pltpu.make_async_copy(part, outs[half].at[block], sems.at[1, index])])
        if own is not None:
            stores[-1].append(pltpu.make_async_copy(work.at[index], outs[own].at[block], sems.at[2, index]))
    for index, (source, target) in enumerate(zip(inputs, picked)):
        at = len(jobs) + index
        loads.append([pltpu.make_async_copy(source.at[1 - place_ref[2]], frames.at[index], sems.at[0, at])])
        stores.append([pltpu.make_async_copy(frames.at[index], target, sems.at[1, at])])
    for copies in loads:
        start_all(copies)
    for load, store in zip(loads, stores):
        wait_all(load)
        start_all(store)
    for copies in stores:
        wait_all(copies)


def pack_shares(place, sources, chunks, share, width, clips=(), deps=()):
    jobs = [
        (chunk, block) + place_of
        for chunk, (_, blocks) in enumerate(chunks)
        for block, place_of in enumerate(blocks)
    ]
    out_shape, outs_of = [], []
    for whole, blocks in chunks:
        outs_of.append((len(out_shape) if whole else None, len(out_shape) + whole))
        if whole:
            out_shape.append(shaped((len(blocks), share, width), BF16))
        out_shape.append(shaped((len(blocks), share // 2, width), BF16))
    out_shape += [shaped(clip.shape[1:], BF16) for clip in clips]
    count = len(jobs) + len(clips)
    return call(
        functools.partial(pack_kernel, jobs, outs_of, len(clips)),
        [place, *sources, *clips],
        [smem_spec()] + [hbm_spec()] * (len(sources) + len(clips)),
        tuple(out_shape),
        (hbm_spec(),) * len(out_shape),
        deps,
        scratch_shapes=[
            pltpu.VMEM((len(jobs), share, width), BF16),
            pltpu.VMEM((len(clips), clips[0].shape[1], width), BF16),
            pltpu.SemaphoreType.DMA((3, count)),
        ],
        cost_estimate=cost(0, 0),
        name="pack_shares",
    )


def project(layer, standard, vectors_ref, weights, queries_ref, keys_ref, values_ref, ready):
    normed = (standard * vectors_ref[layer, 0:1] + vectors_ref[layer, 1:2]).astype(BF16)
    ready()
    queries = (dot(normed, weights[0]) + vectors_ref[layer, 2:3]).astype(BF16)
    queries_ref[...] = queries * jnp.asarray(HEAD ** (-0.5), BF16)
    keys_ref[...] = dot(normed, weights[1]).astype(BF16)
    values_ref[...] = (dot(normed, weights[2]) + vectors_ref[layer, 3:4]).astype(BF16)


def first_qkv_kernel(place_ref, frames_ref, arrived_ref, vectors_ref, *refs):
    shares, (stream_ref, *outs, weights, sems) = refs[:-6], refs[-6:]
    copies = load_rows(shares, place_ref, QKV, weights, sems, weights.shape[1] // SHARDS)
    start_all(copies)
    quarter = arrived_ref.shape[0]
    stream_ref[:quarter] = frames_ref[place_ref[2]].astype(F32)
    stream_ref[quarter:] = arrived_ref[...].astype(F32)
    standard, _ = standardize(stream_ref[...])
    project(0, standard, vectors_ref, weights, *outs, lambda: wait_all(copies))


def qkv_kernel(layer, place_ref, stream_ref, vectors_ref, *refs):
    shares, (*outs, weights, sems) = refs[:-5], refs[-5:]
    copies = load_rows(shares, place_ref, QKV, weights, sems, weights.shape[1] // SHARDS)
    start_all(copies)
    standard, _ = standardize(stream_ref[...])
    project(layer, standard, vectors_ref, weights, *outs, lambda: wait_all(copies))


def qkv_options(rows, width, name):
    return dict(
        scratch_shapes=[pltpu.VMEM((3, width, width), BF16), pltpu.SemaphoreType.DMA((8,))],
        cost_estimate=cost(6 * rows * width * width, 10 * rows * width + 6 * width * width),
        name=name,
    )


def first_qkv(place, frames, arrived, vectors, shares, deps=()):
    rows, width = 2 * arrived.shape[0], arrived.shape[1]
    return call(
        first_qkv_kernel,
        [place, frames, arrived, vectors, *shares],
        [smem_spec()] + [vmem_spec()] * 3 + [hbm_spec()] * len(shares),
        (shaped((rows, width), F32),) + (shaped((rows, width), BF16),) * 3,
        (vmem_spec(),) * 4,
        deps,
        **qkv_options(rows, width, "first_qkv"),
    )


def next_qkv(layer, place, stream, vectors, shares, deps=()):
    rows, width = stream.shape
    return call(
        functools.partial(qkv_kernel, layer),
        [place, stream, vectors, *shares],
        [smem_spec()] + [vmem_spec()] * 2 + [hbm_spec()] * len(shares),
        (shaped((rows, width), BF16),) * 3,
        (vmem_spec(),) * 3,
        deps,
        **qkv_options(rows, width, "next_qkv"),
    )


def attention_kernel(q_ref, ko_ref, kt_ref, vo_ref, vt_ref, mixed_ref, lse_ref):
    queries_t = q_ref[...].T
    row = lax.broadcasted_iota(jnp.int32, queries_t.shape, 0)
    values_t = (vo_ref[...].T, vt_ref[...].T)
    outs = []
    for head in range(2):
        mine = (row >= head * HEAD) & (row < (head + 1) * HEAD)
        q_t = jnp.where(mine, queries_t, jnp.zeros_like(queries_t))
        scores = (dot(ko_ref[...], q_t), dot(kt_ref[...], q_t))
        peak = jnp.maximum(
            jnp.max(scores[0], axis=0, keepdims=True), jnp.max(scores[1], axis=0, keepdims=True)
        )
        weights = tuple(jnp.exp(part - peak) for part in scores)
        total = jnp.sum(weights[0], axis=0, keepdims=True) + jnp.sum(weights[1], axis=0, keepdims=True)
        lse_ref[0, head : head + 1, :] = peak + jnp.log(total)
        at = slice(head * HEAD, (head + 1) * HEAD)
        out = dot(values_t[0][at], weights[0].astype(BF16)) + dot(values_t[1][at], weights[1].astype(BF16))
        outs.append(out / total)
    mixed_ref[...] = jnp.concatenate(outs, axis=0).T.astype(BF16)


def attend(queries, keys, keys_twin, values, values_twin, deps=()):
    rows, width = queries.shape
    pairs = width // (2 * HEAD)
    block = pl.BlockSpec((rows, 2 * HEAD), lambda pair: (0, pair))
    return call(
        attention_kernel,
        [queries, keys, keys_twin, values, values_twin],
        [block] * 5,
        (shaped((rows, width), BF16), shaped((pairs, 8, rows), F32)),
        (block, pl.BlockSpec((1, 8, rows), lambda pair: (pair, 0, 0))),
        deps,
        grid=(pairs,),
        cost_estimate=cost(32 * rows * rows * width, 12 * rows * width, 4 * pairs * rows * rows),
        name="attend",
    )


def up_kernel(layer, place_ref, stream_ref, mixed_ref, vectors_ref, up_bias_ref, *refs):
    shares, (attended_ref, activated_ref, slope_ref, out_w, up_w, sems) = refs[:-6], refs[-6:]
    width = stream_ref.shape[1]
    share = width // SHARDS
    out_copies = load_rows(shares, place_ref, OUT, out_w, sems.at[0], share)
    up_copies = load_rows(shares, place_ref, UP[layer], up_w, sems.at[1], share)
    start_all(out_copies)
    start_all(up_copies)
    wait_all(out_copies)
    attended_ref[...] = stream_ref[...] + dot(mixed_ref[...], out_w[0]) + vectors_ref[layer, 4:5]
    standard, _ = standardize(attended_ref[...])
    second = (standard * vectors_ref[layer, 5:6] + vectors_ref[layer, 6:7]).astype(BF16)
    wait_all(up_copies)
    for block in range(SHARDS):
        at = slice(block * width, (block + 1) * width)
        hidden = dot(second, up_w[block]) + up_bias_ref[layer : layer + 1, at]
        activated, slope = gelu_parts(hidden)
        activated_ref[:, at] = activated.astype(BF16)
        slope_ref[:, at] = slope.astype(BF16)


def feed_up(layer, place, stream, mixed, vectors, up_bias, shares, deps=()):
    rows, width = stream.shape
    wide = SHARDS * width
    return call(
        functools.partial(up_kernel, layer),
        [place, stream, mixed, vectors, up_bias, *shares],
        [smem_spec()] + [vmem_spec()] * 4 + [hbm_spec()] * len(shares),
        (shaped((rows, width), F32), shaped((rows, wide), BF16), shaped((rows, wide), BF16)),
        (vmem_spec(),) * 3,
        deps,
        scratch_shapes=[
            pltpu.VMEM((1, width, width), BF16),
            pltpu.VMEM((4, width, width), BF16),
            pltpu.SemaphoreType.DMA((2, 12)),
        ],
        cost_estimate=cost(10 * rows * width * width, 24 * rows * width + 10 * width * width, rows * wide),
        name="feed_up",
    )


def down_kernel(layer, place_ref, attended_ref, activated_ref, vectors_ref, *refs):
    shares, (next_ref, down_w, sems) = refs[:-3], refs[-3:]
    width = attended_ref.shape[1]
    copies = load_down(shares, place_ref, DOWN[layer], down_w, sems, width // SHARDS)
    start_all(copies)
    next_ref[...] = attended_ref[...] + vectors_ref[layer, 7:8]
    wait_all(copies)
    next_ref[...] += dot(activated_ref[...], down_w[...].reshape(SHARDS * width, width))


def last_down_kernel(layer, place_ref, attended_ref, activated_ref, vectors_ref, *refs):
    shares, (mine_ref, other_ref, down_w, sems) = refs[:-4], refs[-4:]
    width = attended_ref.shape[1]
    copies = load_down(shares, place_ref, DOWN[layer], down_w, sems, width // SHARDS)
    start_all(copies)
    total = attended_ref[...] + vectors_ref[layer, 7:8]
    wait_all(copies)
    total += dot(activated_ref[...], down_w[...].reshape(SHARDS * width, width))
    half = mine_ref.shape[0]
    mine_ref[...] = total[:half].astype(BF16)
    other_ref[...] = total[half:].astype(BF16)


def feed_down(layer, place, attended, activated, vectors, shares, deps=()):
    rows, width = attended.shape
    last = layer == LAYERS - 1
    return call(
        functools.partial(last_down_kernel if last else down_kernel, layer),
        [place, attended, activated, vectors, *shares],
        [smem_spec()] + [vmem_spec()] * 3 + [hbm_spec()] * len(shares),
        (shaped((rows // 2, width), BF16),) * 2 if last else shaped((rows, width), F32),
        (vmem_spec(),) * 2 if last else vmem_spec(),
        deps,
        scratch_shapes=[
            pltpu.VMEM((4 * SHARDS, width // SHARDS, width), BF16),
            pltpu.SemaphoreType.DMA((12,)),
        ],
        cost_estimate=cost(8 * rows * width * width, 16 * rows * width + 8 * width * width),
        name="feed_down",
    )


def feed_scratch(width):
    return [
        pltpu.VMEM((1, width, width), BF16),
        pltpu.VMEM((4, width, width), BF16),
        pltpu.VMEM((4 * SHARDS, width // SHARDS, width), BF16),
        pltpu.SemaphoreType.DMA((3, 12)),
    ]


def feed_back_kernel(layer, place_ref, grad_ref, slope_ref, attended_ref, vectors_ref, *refs):
    shares, refs = refs[:-9], refs[-9:]
    hidden_ref, attended_grad_ref, mixed_grad_ref, sums_ref, up_sums_ref, out_w, up_w, down_w, sems = refs
    width = grad_ref.shape[1]
    share = width // SHARDS
    down_copies = load_down(shares, place_ref, DOWN[layer], down_w, sems.at[2], share)
    up_copies = load_rows(shares, place_ref, UP[layer], up_w, sems.at[1], share)
    out_copies = load_rows(shares, place_ref, OUT, out_w, sems.at[0], share)
    start_all(down_copies)
    start_all(up_copies)
    start_all(out_copies)
    branch = grad_ref[...].astype(BF16)
    sums_ref[...] = jnp.zeros_like(sums_ref)
    sums_ref[7:8] = column_sum(branch)
    standard, inverse = standardize(attended_ref[...])
    wait_all(down_copies)
    second_grad = None
    for block in range(SHARDS):
        at = slice(block * width, (block + 1) * width)
        down = down_w[block * SHARDS : (block + 1) * SHARDS].reshape(width, width)
        hidden_grad = (dot(branch, down, NT) * slope_ref[:, at].astype(F32)).astype(BF16)
        hidden_ref[:, at] = hidden_grad
        up_sums_ref[:, at] = column_sum(hidden_grad)
        if block == 0:
            wait_all(up_copies)
        part = dot(hidden_grad, up_w[block], NT)
        second_grad = part if second_grad is None else second_grad + part
    sums_ref[5:6] = column_sum(second_grad * standard)
    sums_ref[6:7] = column_sum(second_grad)
    attended_grad = grad_ref[...] + norm_input_grad(second_grad, standard, inverse, vectors_ref[layer, 5:6])
    attended_grad_ref[...] = attended_grad
    out_grad = attended_grad.astype(BF16)
    sums_ref[4:5] = column_sum(out_grad)
    wait_all(out_copies)
    mixed_grad_ref[...] = dot(out_grad, out_w[0], NT).astype(BF16)


def feed_back(layer, place, grad, slope, attended, vectors, shares, deps=()):
    rows, width = grad.shape
    wide = SHARDS * width
    return call(
        functools.partial(feed_back_kernel, layer),
        [place, grad, slope, attended, vectors, *shares],
        [smem_spec()] + [vmem_spec()] * 4 + [hbm_spec()] * len(shares),
        (
            shaped((rows, wide), BF16),
            shaped((rows, width), F32),
            shaped((rows, width), BF16),
            shaped((8, width), F32),
            shaped((1, wide), F32),
        ),
        (vmem_spec(),) * 5,
        deps,
        scratch_shapes=feed_scratch(width),
        cost_estimate=cost(18 * rows * width * width, 30 * rows * width + 18 * width * width),
        name="feed_back",
    )


def owners(place_ref, keep_ref, send_refs):
    s = place_ref[0]
    return (
        (s ^ 3, send_refs[2:]),
        (s ^ 1, send_refs[:2]),
        (s ^ 2, (keep_ref.at[1, 0], keep_ref.at[1, 1])),
        (s, (keep_ref.at[0, 0], keep_ref.at[0, 1])),
    )


def quarters(place_ref, split, rows):
    size = rows // 4
    near, inner = (place_ref[1], place_ref[3]) if split else (0, 0)
    for y in range(2):
        for z in range(2):
            start = (near ^ y) * (2 * size) + (inner ^ z) * size
            yield y, z, pl.ds(pl.multiple_of(start, size), size)


def run_steps(steps, work, sems):
    pending = [None, None]
    for index, (make, targets) in enumerate(steps):
        slot = index % 2
        if pending[slot] is not None:
            wait_all(pending[slot])
        work[slot] = make().astype(BF16).reshape(work.shape[1:])
        copies = [
            pltpu.make_async_copy(source, target, sems.at[slot, number])
            for number, (source, target) in enumerate(targets(work.at[slot]))
        ]
        start_all(copies)
        pending[slot] = copies
    for copies in pending:
        if copies is not None:
            wait_all(copies)


def by_rows(place_ref, split, keep_ref, send_refs, block):
    def targets(work):
        return [
            (work.at[shard, rows], target[y].at[z, block])
            for shard, target in owners(place_ref, keep_ref, send_refs)
            for y, z, rows in quarters(place_ref, split, work.shape[1])
        ]

    return targets


def whole_share(place_ref, split, target):
    def targets(work):
        return [
            (work.at[:, rows], target[y].at[z]) for y, z, rows in quarters(place_ref, split, work.shape[1])
        ]

    return targets


def down_grad_kernel(split, place_ref, activated_ref, grad_ref, keep_ref, *refs):
    send_refs, (work, sems) = refs[:4], refs[4:]
    width = grad_ref.shape[1]
    branch = grad_ref[...].astype(BF16)
    steps = []
    for shard, target in owners(place_ref, keep_ref, send_refs):
        at = pl.ds(pl.multiple_of(shard * width, width), width)
        steps.append(
            (lambda at=at: dot(activated_ref[:, at], branch, TN), whole_share(place_ref, split, target))
        )
    run_steps(steps, work, sems)


def grad_shapes(count, width):
    part = (2, count, width // SHARDS // 4, width)
    return (shaped((2, 2) + part, BF16),) + (shaped(part, BF16),) * 4


def grad_scratch(width):
    return [pltpu.VMEM((2, SHARDS, width // SHARDS, width), BF16), pltpu.SemaphoreType.DMA((2, 16))]


def down_weight_grad(place, split, activated, grad, deps=()):
    rows, width = grad.shape
    return call(
        functools.partial(down_grad_kernel, split),
        [place, activated, grad],
        [smem_spec()] + [vmem_spec()] * 2,
        grad_shapes(SHARDS, width),
        (hbm_spec(),) * 5,
        deps,
        scratch_shapes=grad_scratch(width),
        cost_estimate=cost(8 * rows * width * width, 12 * rows * width + 8 * width * width),
        name="down_weight_grad",
    )


def feed_grad_kernel(
    layer,
    split,
    place_ref,
    hidden_ref,
    attended_ref,
    attended_grad_ref,
    mixed_ref,
    vectors_ref,
    keep_ref,
    *refs,
):
    send_refs, (work, sems) = refs[:4], refs[4:]
    width = attended_ref.shape[1]
    standard, _ = standardize(attended_ref[...])
    second_t = (standard * vectors_ref[layer, 5:6] + vectors_ref[layer, 6:7]).astype(BF16).T
    steps = [
        (
            lambda: dot(mixed_ref[...], attended_grad_ref[...].astype(BF16), TN),
            by_rows(place_ref, split, keep_ref, send_refs, 0),
        )
    ]
    for block in range(SHARDS):
        at = slice(block * width, (block + 1) * width)
        steps.append(
            (lambda at=at: dot(second_t, hidden_ref[:, at]), by_rows(place_ref, split, keep_ref, send_refs, 1 + block))
        )
    run_steps(steps, work, sems)


def feed_weight_grads(layer, split, place, hidden_grad, attended, attended_grad, mixed, vectors, deps=()):
    rows, width = attended.shape
    return call(
        functools.partial(feed_grad_kernel, layer, split),
        [place, hidden_grad, attended, attended_grad, mixed, vectors],
        [smem_spec()] + [vmem_spec()] * 5,
        grad_shapes(1 + SHARDS, width),
        (hbm_spec(),) * 5,
        deps,
        scratch_shapes=grad_scratch(width),
        cost_estimate=cost(10 * rows * width * width, 20 * rows * width + 10 * width * width),
        name="feed_weight_grads",
    )


def qkv_grad_kernel(
    layer,
    split,
    place_ref,
    stream_ref,
    vectors_ref,
    dq_ref,
    dk_ref,
    dv_ref,
    dk_back_ref,
    dv_back_ref,
    sums_ref,
    total_ref,
    keep_ref,
    *refs,
):
    send_refs, (work, sems) = refs[:4], refs[4:]
    standard, _ = standardize(stream_ref[...])
    normed_t = (standard * vectors_ref[layer, 0:1] + vectors_ref[layer, 1:2]).astype(BF16).T
    total_ref[0] = (dk_ref[...].astype(F32) + dk_back_ref[...].astype(F32)).astype(BF16)
    total_ref[1] = (dv_ref[...].astype(F32) + dv_back_ref[...].astype(F32)).astype(BF16)
    sums_ref[...] = jnp.zeros_like(sums_ref)
    sums_ref[2:3] = column_sum(dq_ref[...])
    sums_ref[3:4] = column_sum(total_ref[1])
    makers = (
        lambda: dot(normed_t, dq_ref[...]),
        lambda: dot(normed_t, total_ref[0]),
        lambda: dot(normed_t, total_ref[1]),
    )
    run_steps(
        [(make, by_rows(place_ref, split, keep_ref, send_refs, block)) for block, make in enumerate(makers)],
        work,
        sems,
    )


def qkv_weight_grads(layer, split, place, stream, vectors, dq, dk, dv, dk_back, dv_back, deps=()):
    rows, width = stream.shape
    return call(
        functools.partial(qkv_grad_kernel, layer, split),
        [place, stream, vectors, dq, dk, dv, dk_back, dv_back],
        [smem_spec()] + [vmem_spec()] * 7,
        (shaped((8, width), F32), shaped((2, rows, width), BF16)) + grad_shapes(3, width),
        (vmem_spec(),) * 2 + (hbm_spec(),) * 5,
        deps,
        scratch_shapes=grad_scratch(width),
        cost_estimate=cost(6 * rows * width * width, 10 * rows * width + 6 * width * width),
        name="qkv_weight_grads",
    )


def attention_back_kernel(
    q_ref,
    ko_ref,
    kt_ref,
    vo_ref,
    vt_ref,
    lse_ref,
    out_grad_ref,
    dq_ref,
    dk_ref,
    dv_ref,
    dk_twin_ref,
    dv_twin_ref,
):
    queries = q_ref[...]
    out_grad = out_grad_ref[...]
    queries_t, out_grad_t = queries.T, out_grad.T
    row = lax.broadcasted_iota(jnp.int32, queries_t.shape, 0)
    lane = lax.broadcasted_iota(jnp.int32, queries.shape, 1)
    keys, values = (ko_ref, kt_ref), (vo_ref, vt_ref)
    keys_t = tuple(part[...].T for part in keys)
    key_grads, value_grads, query_grads = [None, None], [None, None], []
    for head in range(2):
        low, high = head * HEAD, (head + 1) * HEAD
        mine_t = (row >= low) & (row < high)
        mine = (lane >= low) & (lane < high)
        q_t = jnp.where(mine_t, queries_t, jnp.zeros_like(queries_t))
        o_t = jnp.where(mine_t, out_grad_t, jnp.zeros_like(queries_t))
        q_h = jnp.where(mine, queries, jnp.zeros_like(queries))
        o_h = jnp.where(mine, out_grad, jnp.zeros_like(queries))
        lse = lse_ref[0, head : head + 1, :]
        probability = [jnp.exp(dot(part[...], q_t) - lse) for part in keys]
        probability_grad = [dot(part[...], o_t) for part in values]
        inner = sum(
            jnp.sum(left * right, axis=0, keepdims=True)
            for left, right in zip(probability, probability_grad)
        )
        query_grad = None
        for index in range(2):
            score_grad = (probability[index] * (probability_grad[index] - inner)).astype(BF16)
            value_part = dot(probability[index].astype(BF16), o_h)
            key_part = dot(score_grad, q_h)
            query_part = dot(keys_t[index][low:high], score_grad)
            if head == 0:
                key_grads[index], value_grads[index] = key_part, value_part
            else:
                key_grads[index] += key_part
                value_grads[index] += value_part
            query_grad = query_part if index == 0 else query_grad + query_part
        query_grads.append(query_grad)
    dq_ref[...] = (jnp.concatenate(query_grads, axis=0).T * HEAD ** (-0.5)).astype(BF16)
    for ref, value in zip((dk_ref, dk_twin_ref, dv_ref, dv_twin_ref), key_grads + value_grads):
        ref[...] = value.astype(BF16)


def attend_back(queries, keys, keys_twin, values, values_twin, lse, out_grad, deps=()):
    rows, width = queries.shape
    pairs = width // (2 * HEAD)
    block = pl.BlockSpec((rows, 2 * HEAD), lambda pair: (0, pair))
    return call(
        attention_back_kernel,
        [queries, keys, keys_twin, values, values_twin, lse, out_grad],
        [block] * 5 + [pl.BlockSpec((1, 8, rows), lambda pair: (pair, 0, 0)), block],
        (shaped((rows, width), BF16),) * 5,
        (block,) * 5,
        deps,
        grid=(pairs,),
        cost_estimate=cost(80 * rows * rows * width, 24 * rows * width),
        name="attend_back",
    )


def norm_back_kernel(layer, place_ref, stream_ref, vectors_ref, attended_grad_ref, dq_ref, dkv_ref, *refs):
    shares, (grad_ref, sums_ref, weights, sems) = refs[:-4], refs[-4:]
    copies = load_rows(shares, place_ref, QKV, weights, sems, weights.shape[1] // SHARDS)
    start_all(copies)
    standard, inverse = standardize(stream_ref[...])
    wait_all(copies)
    normed_grad = (
        dot(dq_ref[...], weights[0], NT) + dot(dkv_ref[0], weights[1], NT) + dot(dkv_ref[1], weights[2], NT)
    )
    sums_ref[...] = jnp.zeros_like(sums_ref)
    sums_ref[0:1] = column_sum(normed_grad * standard)
    sums_ref[1:2] = column_sum(normed_grad)
    grad_ref[...] = attended_grad_ref[...] + norm_input_grad(
        normed_grad, standard, inverse, vectors_ref[layer, 0:1]
    )


def norm_back(layer, place, stream, vectors, attended_grad, dq, dkv, shares, deps=()):
    rows, width = stream.shape
    return call(
        functools.partial(norm_back_kernel, layer),
        [place, stream, vectors, attended_grad, dq, dkv, *shares],
        [smem_spec()] + [vmem_spec()] * 5 + [hbm_spec()] * len(shares),
        (shaped((rows, width), F32), shaped((8, width), F32)),
        (vmem_spec(),) * 2,
        deps,
        scratch_shapes=[pltpu.VMEM((3, width, width), BF16), pltpu.SemaphoreType.DMA((8,))],
        cost_estimate=cost(6 * rows * width * width, 18 * rows * width + 6 * width * width),
        name="norm_back",
    )


def finish_kernel(layer, split, pieces, places, place_ref, *refs):
    sources, refs = refs[: len(pieces)], refs[len(pieces) :]
    outs, (arrived, work, sems) = refs[:-3], refs[-3:]
    count = len(places)
    near, inner = (place_ref[1], place_ref[3]) if split else (0, 0)
    size, width = work.shape[1:]
    loads = []
    for index, (source, (start, _, _)) in enumerate(zip(sources, pieces)):
        at = pl.ds(index * count, count)
        loads.append(pltpu.make_async_copy(source.at[pl.ds(start, count)], arrived.at[at], sems.at[0, index]))
    start_all(loads)
    stores = []
    for number, (load, (_, y, z)) in enumerate(zip(loads, pieces)):
        load.wait()
        for block, (out, row, column) in enumerate(places):
            index = number * count + block
            work[index] = arrived[index].astype(F32)
            start = row + (near ^ y) * (2 * size) + (inner ^ z) * size
            target = outs[out].at[layer, aligned(start, size), pl.ds(column, width)]
            stores.append(pltpu.make_async_copy(work.at[index], target, sems.at[1, index]))
            stores[-1].start()
    wait_all(stores)


def finish(layer, split, sources, places, out_shapes, place, buffers=None, deps=()):
    size, width = sources[0][0].shape[-2:]
    count = 4 * len(places)
    operands = [place, *(source[0] for source in sources)]
    aliases = {}
    if buffers is not None:
        aliases = {len(operands) + index: index for index in range(len(buffers))}
        operands += list(buffers)
    first = 1 + len(sources)
    pieces = [source[1:] for source in sources]

    def kernel(*refs):
        finish_kernel(layer, split, pieces, places, *refs[:first], *refs[len(operands) :])

    return call(
        kernel,
        operands,
        [smem_spec()] + [hbm_spec()] * (len(operands) - 1),
        tuple(shaped(shape, F32) for shape in out_shapes),
        (hbm_spec(),) * len(out_shapes),
        deps,
        input_output_aliases=aliases,
        scratch_shapes=[
            pltpu.VMEM((count, size, width), BF16),
            pltpu.VMEM((count, size, width), F32),
            pltpu.SemaphoreType.DMA((2, count)),
        ],
        cost_estimate=cost(0, 6 * count * size * width),
        name="finish",
    )


def combine_kernel(plan, *refs):
    arrays = 1 + max(operand for segments in plan for _, terms in segments for operand, _ in terms)
    operands, outs, (work, sems, out_sems) = refs[:arrays], refs[arrays:-3], refs[-3:]
    jobs, copies, at = [], [], 0
    for out, segments in zip(outs, plan):
        place = 0
        for count, terms in segments:
            places = []
            for operand, start in terms:
                source = operands[operand].at[pl.ds(start, count)]
                copies.append(
                    pltpu.make_async_copy(source, work.at[pl.ds(at, count)], sems.at[len(copies)])
                )
                places.append((copies[-1], at))
                at += count
            jobs.append((out, place, count, places))
            place += count
    start_all(copies)
    stores = []
    for out, place, count, places in jobs:
        for copy, _ in places:
            copy.wait()
        first = places[0][1]
        if len(places) == 2:
            for index in range(count):
                work[first + index] += work[places[1][1] + index]
        elif len(places) > 2:
            for index in range(count):
                total = work[first + index].astype(F32)
                for _, start in places[1:]:
                    total += work[start + index].astype(F32)
                work[first + index] = total.astype(BF16)
        stores.append(
            pltpu.make_async_copy(
                work.at[pl.ds(first, count)], out.at[pl.ds(place, count)], out_sems.at[len(stores)]
            )
        )
        stores[-1].start()
    wait_all(stores)


def combine(outputs, deps=()):
    arrays, plan = [], []
    for segments in outputs:
        plan.append([])
        for count, terms in segments:
            named = []
            for array, start in terms:
                index = next((i for i, known in enumerate(arrays) if known is array), len(arrays))
                if index == len(arrays):
                    arrays.append(array)
                named.append((index, start))
            plan[-1].append((count, named))
    size, width = arrays[0].shape[1:]
    moves = [len(terms) for segments in plan for _, terms in segments]
    rows = sum(count * len(terms) for segments in plan for count, terms in segments)
    return call(
        functools.partial(combine_kernel, plan),
        arrays,
        [hbm_spec()] * len(arrays),
        tuple(shaped((sum(count for count, _ in segments), size, width), BF16) for segments in plan),
        (hbm_spec(),) * len(plan),
        deps,
        scratch_shapes=[
            pltpu.VMEM((rows, size, width), BF16),
            pltpu.SemaphoreType.DMA((sum(moves),)),
            pltpu.SemaphoreType.DMA((len(moves),)),
        ],
        cost_estimate=cost(0, 0),
        name="combine",
    )


PAIRS, MIRROR = [(0, 1), (1, 0), (2, 3), (3, 2)], [(0, 3), (3, 0), (1, 2), (2, 1)]


class Flow:
    def __init__(self, split, parts, *pins, last="spread"):
        keep, *send = parts
        self.split, self.count, self.last = split, keep.shape[3], last
        self.keep = keep.reshape((-1,) + keep.shape[-2:])
        send = after(tuple(send), *pins)
        self.back = [swap(part.reshape((-1,) + part.shape[-2:]), "core") for part in send]

    def sums(self, x, y, z, *arrivals):
        n = self.count
        terms = [(self.keep, (4 * x + 2 * y + z) * n), (self.back[2 * x + y], z * n)]
        return (n, terms + [(array, start + offset * n) for (array, start), offset in arrivals])

    def segments(self, stage):
        n = self.count
        if stage == "x":
            return {"x": [self.sums(1, y, z) for y in range(2) for z in range(2)]}
        if stage == "y":
            return {"y": [self.sums(0, 1, z, (self.x, 2 + z)) for z in range(2)]}
        if stage == "pair":
            if not self.split:
                return {"sum": [self.sums(0, 0, z, (self.x, z), (self.y, z)) for z in range(2)]}
            return {"pair": [self.sums(0, 0, 1, (self.x, 1), (self.y, 1))]}
        if stage == "mirror":
            if not self.split:
                return {}
            return {"mirror": [self.sums(0, 0, 0, (self.x, 0), (self.y, 0), (self.pair, 0))]}
        if stage == "after":
            if not self.split:
                return {"near": [(2 * n, [self.sum])]}
            whole = (n, [self.mirror_sent, self.mirror])
            return {channel: [whole] for channel in ("near", "spread", "diagonal")[: 3 if self.last is None else 2]}
        if not self.split or self.last is None:
            return {}
        return {self.last: [(n, [self.rest if self.last == "spread" else self.part_z])]}

    def record(self, stage, channel, sent, arrived):
        if stage == "after":
            if channel == "near":
                self.part, self.rest = sent, arrived
            elif channel == "spread":
                self.part_z = arrived
            else:
                self.rest_z = arrived
        elif stage == "last":
            self.rest_z = arrived
        else:
            setattr(self, channel, arrived)
            setattr(self, channel + "_sent", sent)

    def finish(self, layer, places, out_shapes, place, buffers=None, deps=()):
        n = self.count
        if self.split:
            sources = [(*self.part, 0, 0), (*self.part_z, 0, 1), (*self.rest, 1, 0), (*self.rest_z, 1, 1)]
        else:
            sources = [
                (array, start + z * n, y, z)
                for y, (array, start) in enumerate((self.part, self.rest))
                for z in range(2)
            ]
        return finish(layer, self.split, sources, places, out_shapes, place, buffers, deps)


class Totals:
    def __init__(self, split, values):
        self.split = split
        self.terms = [(values, 0), (swap(values, "core"), 0)]

    def segments(self, stage):
        if stage in ("pair", "mirror") and not self.split:
            return {"sum": [(1, self.terms)]} if stage == "pair" else {}
        return {stage: [(1, self.terms)]}

    def record(self, stage, channel, sent, arrived):
        self.terms = [arrived] if channel == "sum" else [sent, arrived]

    def done(self):
        return sum(array[start].astype(F32) for array, start in self.terms)


def exchange(steps, *pins):
    outputs, owners_of = {}, {}
    for flow, stage in steps:
        for channel, segments in flow.segments(stage).items():
            placed = outputs.setdefault(channel, [])
            start = sum(count for count, _ in placed)
            owners_of.setdefault(channel, []).append((flow, stage, start))
            placed += segments
    if not outputs:
        return pins[0], ()
    names, landed = list(outputs), []
    results = combine([outputs[name] for name in names], pins)
    for name, sent in zip(names, results):
        if name == "sum":
            arrived = lax.psum(sent, "z")
        elif name == "diagonal":
            both = [(2 * left + y, 2 * right + 1 - y) for left, right in PAIRS for y in range(2)]
            arrived = lax.ppermute(sent, ("z", "y"), both)
        elif name in ("pair", "spread", "mirror"):
            arrived = lax.ppermute(sent, "z", MIRROR if name == "mirror" else PAIRS)
        else:
            arrived = swap(sent, "y" if name == "near" else name)
        landed.append(arrived)
        for flow, stage, start in owners_of[name]:
            flow.record(stage, name, (sent, start), (arrived, start))
    return results[0], tuple(landed)


def body(
    frames,
    cotangent,
    first_gain,
    first_shift,
    query_weight,
    query_bias,
    key_weight,
    value_weight,
    value_bias,
    out_weight,
    out_bias,
    second_gain,
    second_shift,
    up_weight,
    up_bias,
    down_weight,
    down_bias,
):
    x, y, z, core = (lax.axis_index(axis) for axis in ("x", "y", "z", "core"))
    shard = 2 * x + core
    inner = jnp.where((z == 0) | (z == 3), 0, 1)
    place = jnp.stack([shard, y, x, inner]).astype(jnp.int32)
    quarter, width = frames.shape[1:]
    share = width // SHARDS
    split = lax.axis_size("z") == 4

    def blocks_of(layer):
        attention = [(source, layer, (0, 0)) for source in (0, 1, 2)]
        up = [(3, layer, (0, 0))] + [(4, layer, (0, block * width)) for block in range(SHARDS)]
        down = [(5, layer, (block * share, 0)) for block in range(SHARDS)]
        return attention, up, down

    sources = (query_weight, key_weight, value_weight, out_weight, up_weight, down_weight)
    (attention0, up0, down0), (attention1, up1, down1) = blocks_of(0), blocks_of(1)
    own0, half0, other_frames = pack_shares(
        place, sources[:3], [(True, attention0)], share, width, clips=(frames,)
    )
    near = {0: swap(half0, "x")}
    arrived_frames = swap(other_frames, "x")
    twin = {0: swap(own0, "core")}
    *packed, other_cotangent = pack_shares(
        place,
        sources,
        [
            (True, blocks)
            for blocks in (up0 + down0[:1], down0[1:], attention1, up1[:3], up1[3:], down1)
        ],
        share,
        width,
        clips=(cotangent,),
        deps=(half0,),
    )
    own, half = dict(enumerate([own0, *packed[0::2]])), dict(enumerate([half0, *packed[1::2]]))
    near[0] = after(near[0], half[1])
    far, near_twin, far_twin = {0: swap(near[0], "y")}, {0: swap(near[0], "core")}, {}

    small = jnp.stack(
        [first_gain, first_shift, query_bias, value_bias, out_bias, second_gain, second_shift, down_bias], axis=1
    )
    small = jnp.concatenate([small, up_bias.reshape(LAYERS, SHARDS, share)], axis=1)
    small = after(small, half0)
    pair = jnp.stack([small, swap(small, "core")])
    pieces = jnp.concatenate([pair, swap(pair, "x")], axis=0)
    small = jnp.stack(
        [lax.dynamic_index_in_dim(pieces, shard ^ index, 0, keepdims=False) for index in range(SHARDS)]
    ).astype(F32)
    vectors = jnp.transpose(small[:, :, :8], (1, 2, 0, 3)).reshape(LAYERS, 8, width)
    up_biases = jnp.transpose(small[:, :, 8:], (1, 0, 2, 3)).reshape(LAYERS, SHARDS * width)

    def fetch(chunk, *pins):
        near[chunk] = swap(after(half[chunk], *pins), "x")

    def spread(chunk, *pins):
        far[chunk] = swap(after(near[chunk], *pins), "y")

    def trade(chunk, *pins):
        twin[chunk] = swap(after(own[chunk], *pins), "core")

    def trade_near(chunk, *pins):
        near_twin[chunk] = swap(after(near[chunk], *pins), "core")

    def trade_far(chunk, *pins):
        far_twin[chunk] = swap(after(far[chunk], *pins), "core")

    def shares(chunk):
        return own[chunk], twin[chunk], near[chunk], far[chunk], near_twin[chunk], far_twin[chunk]

    trade_far(0)
    fetch(1, arrived_frames)
    for chunk in range(1, 7):
        trade(chunk, arrived_frames)
    stream0, queries0, keys0, values0 = first_qkv(
        place, frames, arrived_frames, vectors, shares(0), deps=tuple(twin[chunk] for chunk in range(1, 7))
    )
    qkv0 = shares(0)
    keys0, values0 = after((keys0, values0), near[1])
    keys_twin0, values_twin0 = swap(keys0, "core"), swap(values0, "core")
    fetch(2, keys0)
    spread(1, keys0)
    trade_near(1, keys0)
    mixed0, lse0 = attend(queries0, keys0, keys_twin0, values0, values_twin0, deps=(near_twin[1],))
    trade_far(1, mixed0)
    fetch(3, near[2], mixed0)
    spread(2, mixed0)
    trade_near(2, mixed0)
    attended0, activated0, slope0 = feed_up(
        0, place, stream0, mixed0, vectors, up_biases, shares(1), deps=(near_twin[2],)
    )
    trade_far(2, activated0)
    fetch(4, near[3], activated0)
    spread(3, activated0)
    trade_near(3, activated0)
    second0 = shares(1) + shares(2)
    stream1 = feed_down(0, place, attended0, activated0, vectors, second0, deps=(near_twin[3],))
    trade_far(3, stream1)
    fetch(5, near[4], stream1)
    spread(4, stream1)
    trade_near(4, stream1)
    qkv1 = shares(3)
    queries1, keys1, values1 = next_qkv(1, place, stream1, vectors, qkv1, deps=(near_twin[4],))
    keys1, values1 = after((keys1, values1), near[5], far[4])
    keys_twin1, values_twin1 = swap(keys1, "core"), swap(values1, "core")
    fetch(6, near[5], keys1)
    spread(5, keys1)
    trade_near(5, keys1)
    trade_far(4, keys1)
    mixed1, lse1 = attend(
        queries1, keys1, keys_twin1, values1, values_twin1, deps=(near_twin[5], far_twin[4])
    )
    trade_far(5, mixed1)
    spread(6, mixed1)
    trade_near(6, mixed1)
    arrived_cotangent = swap(after(other_cotangent, near[6]), "x")
    late = shares(4) + shares(5)
    attended1, activated1, slope1 = feed_up(
        1, place, stream1, mixed1, vectors, up_biases, late, deps=(near_twin[6],)
    )
    mine_cotangent = lax.dynamic_index_in_dim(cotangent, x, 0, keepdims=False)
    pieces = after((mine_cotangent, arrived_cotangent), attended1)
    gradient = jnp.concatenate(pieces, axis=0).astype(F32)
    down1 = Flow(split, down_weight_grad(place, split, activated1, gradient), far[6])
    trade_far(6, down1.keep)
    output_mine, output_other = feed_down(1, place, attended1, activated1, vectors, shares(6))
    late += shares(6)

    def by_clip(mine, other):
        return jnp.where(x == 0, jnp.stack([mine, other]), jnp.stack([other, mine]))

    def square(row_blocks, column_blocks):
        return (LAYERS, row_blocks * share, column_blocks * width)

    down_places, down_shapes = [(0, block * share, 0) for block in range(SHARDS)], [square(SHARDS, 1)]
    feed_places = [(0, 0, 0)] + [(1, 0, block * width) for block in range(SHARDS)]
    feed_shapes = [square(1, 1), square(1, SHARDS)]
    qkv_places, qkv_shapes = [(block, 0, 0) for block in range(3)], [square(1, 1)] * 3

    pin, landed = exchange([(down1, "x")], output_mine, *down1.back)
    hidden_grad, attended_grad, mixed_grad, feed_sums1, up_sums1 = feed_back(
        1, place, gradient, slope1, attended1, vectors, late, deps=(pin,)
    )
    parts = feed_weight_grads(1, split, place, hidden_grad, attended1, attended_grad, mixed1, vectors)
    feed1 = Flow(split, parts)
    pin, (near, far) = exchange([(down1, "y"), (feed1, "x")], *feed1.back)
    dq, dk, dv, dk_twin, dv_twin = attend_back(
        queries1, keys1, keys_twin1, values1, values_twin1, lse1, mixed_grad, deps=(pin,)
    )
    dk_twin, dv_twin = after((dk_twin, dv_twin), near)
    dk_back, dv_back = swap(dk_twin, "core"), swap(dv_twin, "core")
    pin, landed = exchange([(down1, "pair")], dq)
    qkv_sums1, dkv, *parts = qkv_weight_grads(
        1, split, place, stream1, vectors, dq, dk, dv, dk_back, dv_back, deps=(pin,)
    )
    gradient, norm_sums1 = norm_back(
        1, place, stream1, vectors, attended_grad, dq, dkv, qkv1, deps=(parts[0],)
    )
    qkv_1 = Flow(split, parts, far, *landed, last="near")
    pin, landed = exchange([(qkv_1, "x"), (feed1, "y"), (down1, "mirror")], gradient, *qkv_1.back)

    parts = down_weight_grad(place, split, activated0, gradient, deps=(pin,))
    hidden_grad, attended_grad, mixed_grad, feed_sums0, up_sums0 = feed_back(
        0, place, gradient, slope0, attended0, vectors, second0, deps=(parts[0],)
    )
    down0 = Flow(split, parts, mixed_grad, *landed, last="near")
    steps = [(down0, "x"), (qkv_1, "y"), (down1, "after"), (feed1, "pair")]
    pin, landed = exchange(steps, mixed_grad, *down0.back)
    parts = feed_weight_grads(
        0, split, place, hidden_grad, attended0, attended_grad, mixed0, vectors, deps=(pin,)
    )
    dq, dk, dv, dk_twin, dv_twin = attend_back(
        queries0, keys0, keys_twin0, values0, values_twin0, lse0, mixed_grad, deps=(parts[0],)
    )
    dk_twin, dv_twin = after((dk_twin, dv_twin), *landed)
    dk_back, dv_back = swap(dk_twin, "core"), swap(dv_twin, "core")
    feed0 = Flow(split, parts, dq, *landed, last=None)
    steps = [(feed0, "x"), (down0, "y"), (down1, "last"), (qkv_1, "pair"), (feed1, "mirror")]
    pin, (far, *landed) = exchange(steps, dq, *feed0.back)
    qkv_sums0, dkv, *parts = qkv_weight_grads(
        0, split, place, stream0, vectors, dq, dk, dv, dk_back, dv_back, deps=(pin,)
    )
    gradient, norm_sums0 = norm_back(
        0, place, stream0, vectors, attended_grad, dq, dkv, qkv0, deps=(parts[0],)
    )
    qkv_0 = Flow(split, parts, gradient, *landed, last=None)
    sums = jnp.concatenate(
        [
            part
            for feed, qkv, norm, up in (
                (feed_sums0, qkv_sums0, norm_sums0, up_sums0),
                (feed_sums1, qkv_sums1, norm_sums1, up_sums1),
            )
            for part in (feed + qkv + norm, up.reshape(SHARDS, width))
        ]
    ).astype(BF16)
    sums = jnp.pad(sums, ((0, share // 4 - sums.shape[0]), (0, 0)))
    totals = Totals(split, sums[None])
    steps = [(qkv_0, "x"), (totals, "x"), (down0, "pair"), (feed1, "after")]
    pin, landed = exchange(steps, gradient, *qkv_0.back)
    down_out = down1.finish(1, down_places, down_shapes, place, deps=(pin,))
    pin, landed = exchange([(feed0, "y"), (down0, "mirror"), (qkv_1, "mirror"), (feed1, "last")], down_out[0])
    input_other = swap(after(gradient[quarter:].astype(BF16), pin), "x")
    steps = [(qkv_0, "y"), (totals, "y"), (feed0, "pair"), (down0, "after"), (qkv_1, "after")]
    pin, landed = exchange(steps, pin)
    output_other = swap(after(output_other, pin), "x")
    feed_out = feed1.finish(1, feed_places, feed_shapes, place, deps=(pin, input_other))
    input_grad = by_clip(gradient[:quarter], input_other.astype(F32))
    steps = [(qkv_0, "pair"), (totals, "pair"), (feed0, "mirror"), (down0, "last"), (qkv_1, "last")]
    pin, landed = exchange(steps, feed_out[0], output_other)
    output = by_clip(output_mine, output_other)
    steps = [(qkv_0, "mirror"), (totals, "mirror"), (feed0, "after")]
    pin, landed = exchange(steps, pin)
    (down_out,) = down0.finish(0, down_places, down_shapes, place, down_out, deps=(pin,))
    qkv_out = qkv_1.finish(1, qkv_places, qkv_shapes, place, deps=(down_out,))
    pin, landed = exchange([(qkv_0, "after")], qkv_out[0])
    totals = totals.done()[: LAYERS * (8 + SHARDS)].reshape(LAYERS, 8 + SHARDS, width)
    out_out, up_out = feed0.finish(0, feed_places, feed_shapes, place, feed_out, deps=(pin,))
    query_out, key_out, value_out = qkv_0.finish(
        0, qkv_places, qkv_shapes, place, qkv_out, deps=(out_out,)
    )

    own_vectors = lax.dynamic_slice_in_dim(totals[:, :8], shard * share, share, axis=2)
    own_up = lax.dynamic_slice_in_dim(
        totals[:, 8:].reshape(LAYERS, SHARDS * width), shard * width, width, axis=1
    )
    vector = [own_vectors[:, index] for index in range(8)]
    return (
        output,
        input_grad,
        vector[0],
        vector[1],
        query_out,
        vector[2],
        key_out,
        value_out,
        vector[3],
        out_out,
        vector[4],
        vector[5],
        vector[6],
        up_out,
        own_up,
        down_out,
        vector[7],
    )


def solution(mesh):
    groups = mesh.shape["rep"]
    finer = Mesh(mesh.devices.reshape(groups // 2, 2, 2, 2), ("z", "y", "x", "core"))
    rep, shard = ("z", "y"), ("x", "core")
    rows = P(rep, shard, None)
    vector, matrix = P(None, shard), P(None, shard, None)
    parameters = (
        vector,
        vector,
        matrix,
        vector,
        matrix,
        matrix,
        vector,
        matrix,
        vector,
        vector,
        vector,
        matrix,
        vector,
        matrix,
        vector,
    )
    return jax.shard_map(
        body,
        mesh=finer,
        in_specs=(rows, rows) + parameters,
        out_specs=(rows, rows) + parameters,
        check_vma=False,
    )
```
